32 devices in a mesh: gx: 16 (over z, y, core), gy: 2 (over x).
Axes of the slice: x: 2, y: 2, z: 4, core: 2. Of those that a mesh axis runs over, the one named last changes fastest.
Arguments:
- control: bfloat16 [2048, 8, 2048], P('gx', None, 'gy'), may hold values from -6 to 6
- innovation: float32 [2048, 8, 2048], P('gx', None, 'gy'), may hold values from -6 to 6
- obs_weight: float32 [2048, 8, 2048], P('gx', None, 'gy'), may hold values from 0.5 to 4
- courant_x: float32 [2048, 8, 2048], P('gx', None, 'gy'), may hold values from -0.9 to 0.9
- courant_y: float32 [2048, 8, 2048], P('gx', None, 'gy'), may hold values from -0.9 to 0.9
- filter_x: bfloat16 [2048, 2048], P('gx'), may hold values from -3 to 3
- filter_y: bfloat16 [2048, 2048], P('gy'), may hold values from -3 to 3
Outputs:
- end_state: float32 [2048, 8, 2048], P('gx', None, 'gy')
- gradient: float32 [2048, 8, 2048], P('gx', None, 'gy')
The draws below stay inside these ranges and needn't reach their ends.
All inputs are finite; a program needn't handle non-finite values.
Results may differ from the reference program's by a relative error of at most 0.0029.
Values may be sent and summed in bfloat16 or wider, within the bound.
No kernel may reach another device: no remote copies, remote signals or barrier semaphores. Data moves between devices by JAX's collectives and lax.ppermute only.
A program may use at most 192 MiB of HBM per device.

```python
import math
import jax
import jax.numpy as jnp

NX = 2048
NY = 2048
LEV = 8


def filter_matrix(key, order):
    key_len = jax.random.fold_in(key, 11)
    key_gain = jax.random.fold_in(key, 12)
    key_far = jax.random.fold_in(key, 13)
    places = jnp.arange(order, dtype=jnp.float32)
    distance = jnp.abs(places[:, None] - places[None, :])
    lengths = jnp.exp(jax.random.uniform(key_len, (order, 1), jnp.float32, math.log(order / 64.0), math.log(order / 4.0)))
    gains = jax.random.uniform(key_gain, (order, order), jnp.float32, 0.5, 1.5)
    local_part = jnp.exp(-distance / lengths) * gains / jnp.sqrt(2.0 * lengths)
    far_part = jnp.clip(jax.random.normal(key_far, (order, order), jnp.float32), -5.0, 5.0) * (0.5 / math.sqrt(order))
    return local_part + far_part + jnp.eye(order, dtype=jnp.float32)


def draw_filter_x(key, part):
    return filter_matrix(key, NX).astype(jnp.bfloat16)


def draw_filter_y(key, part):
    return filter_matrix(jax.random.fold_in(key, 77), NY).astype(jnp.bfloat16)


def block_scale(own_key, dims, shards, least, top_value):
    def one(position, parts):
        steps = jax.random.uniform(jax.random.fold_in(jax.random.fold_in(own_key, 6), position), (parts,), jnp.float32, least / len(shards), top_value / len(shards))
        return jnp.repeat(jnp.exp(steps), dims[position] // parts).reshape((-1,) + (1,) * (len(dims) - position - 1))

    gain = one(*shards[0])
    for cut in shards[1:]:
        gain = gain * one(*cut)
    return gain


def gaussian(rng, dims, deviation, limit, pieces=(), held_as=jnp.bfloat16):
    values = deviation * jax.random.normal(rng, dims, jnp.float32)
    if pieces:
        values = values * block_scale(rng, dims, pieces, -0.22, 0.18)
    return jnp.clip(values, -limit, limit).astype(held_as)


def setup_inputs(seed: int = 0) -> dict:
    streams_of = jax.random.split(jax.random.key(seed), 8)
    return {
        "control": gaussian(streams_of[0], (NX, LEV, NY), 1.0, 6.0, ((0, 16), (2, 2))),
        "innovation": gaussian(streams_of[1], (NX, LEV, NY), 1.0, 6.0, ((0, 16), (2, 2)), jnp.float32),
        "obs_weight": jnp.clip(jnp.exp(math.log(4.0) - 2.0794415 * jax.random.uniform(streams_of[2], (NX, LEV, NY), jnp.float32) ** block_scale(streams_of[2], (NX, LEV, NY), ((0, 16), (2, 2)), -0.2, 0.2)), 0.5, 4.0),
        "courant_x": jnp.clip(jax.random.uniform(streams_of[3], (NX, LEV, NY), jnp.float32, -0.9, 0.9) * block_scale(streams_of[3], (NX, LEV, NY), ((0, 16), (2, 2)), -0.4, 0.0), -0.9, 0.9),
        "courant_y": jnp.clip(jax.random.uniform(streams_of[4], (NX, LEV, NY), jnp.float32, -0.9, 0.9) * block_scale(streams_of[4], (NX, LEV, NY), ((0, 16), (2, 2)), -0.4, 0.0), -0.9, 0.9),
        "filter_x": draw_filter_x(jax.random.fold_in(streams_of[7], 71), 0),
        "filter_y": draw_filter_y(jax.random.fold_in(streams_of[7], 71), 0),
    }


def reference(control, innovation, obs_weight, courant_x, courant_y, filter_x, filter_y):
    matrix_x = filter_x.astype(jnp.float32)
    matrix_y = filter_y.astype(jnp.float32)
    control_f = control.astype(jnp.float32)
    smoothed = jnp.einsum("ij,jlc->ilc", matrix_x, control_f).astype(jnp.bfloat16)
    start_state = jnp.einsum("kc,xlc->xlk", matrix_y, smoothed.astype(jnp.float32))
    padded = jnp.pad(start_state, ((1, 1), (0, 0), (1, 1)))
    end_state = (start_state
                 - courant_x * (padded[2:, :, 1:-1] - padded[:-2, :, 1:-1]) * 0.5
                 - courant_y * (padded[1:-1, :, 2:] - padded[1:-1, :, :-2]) * 0.5)
    misfit = obs_weight * (end_state - innovation)
    flux_x = jnp.pad(courant_x * misfit, ((1, 1), (0, 0), (1, 1)))
    flux_y = jnp.pad(courant_y * misfit, ((1, 1), (0, 0), (1, 1)))
    adjoint = (misfit
               + 0.5 * (flux_x[2:, :, 1:-1] - flux_x[:-2, :, 1:-1])
               + 0.5 * (flux_y[1:-1, :, 2:] - flux_y[1:-1, :, :-2])).astype(jnp.bfloat16)
    pulled = jnp.einsum("kc,xlk->xlc", matrix_y, adjoint.astype(jnp.float32)).astype(jnp.bfloat16)
    gradient = control_f + jnp.einsum("ij,ilc->jlc", matrix_x, pulled.astype(jnp.float32))
    return end_state, gradient
```

```python
import jax
import jax.numpy as jnp
from jax import lax
from jax.sharding import PartitionSpec as P

BF16 = jnp.bfloat16
F32 = jnp.float32


def extended(array, sides, width):
    for axis, dim in sides:
        size, length = (lax.axis_size(axis), array.shape[dim])
        up = [(i, (i + 1) % size) for i in range(size - 1)]
        down = [(j, i) for i, j in up]
        last = lax.slice_in_dim(array, length - width, length, axis=dim)
        initial = lax.slice_in_dim(array, 0, width, axis=dim)
        before = lax.ppermute(last, axis, up)
        after = lax.ppermute(initial, axis, down)
        array = jnp.concatenate([before, array, after], axis=dim)
    return array


def to_lines(block, parts):
    rows, levels, width = block.shape
    part = width // parts
    sent = block.reshape(rows, levels, parts, part).transpose(1, 2, 0, 3)
    sent = sent.reshape(levels * parts * rows, part)
    return lax.all_to_all(sent, "gx", 0, 0, tiled=True)


def to_blocks(lines, levels, parts):
    part = lines.shape[1]
    got = lax.all_to_all(lines, "gx", 0, 0, tiled=True)
    got = got.reshape(levels, parts, -1, part).transpose(2, 0, 1, 3)
    return got.reshape(got.shape[0], levels, parts * part)


def level_plane(lines, parts):
    plane = lax.all_gather(lines, "gy", axis=0, tiled=False)
    if parts == 1:
        return plane[None]
    size = lax.axis_size("gx")
    groups = [list(range(i, i + parts)) for i in range(0, size, parts)]
    return lax.all_gather(plane, "gx", axis=0, tiled=False, axis_index_groups=groups)


def per_device(control, innovation, obs_weight, courant_x, courant_y, filter_x, filter_y):
    rows, levels, width = control.shape
    n_x, n_y = lax.axis_size("gx"), lax.axis_size("gy")
    parts = n_x // levels
    part = width // parts
    sub = lax.rem(lax.axis_index("gx"), parts)

    matrix_x = lax.all_gather(filter_x, "gx", axis=0, tiled=True)
    rows_y = lax.dynamic_slice_in_dim(filter_y, sub * part, part, axis=0)
    split_y = filter_y.reshape(width, n_y, parts, part)
    columns_y = lax.dynamic_index_in_dim(split_y, sub, axis=2, keepdims=False)
    columns_y = lax.all_to_all(columns_y, "gy", 1, 0, tiled=True)
    columns_y = columns_y.reshape(n_y, parts, part, part)
    rows_y = rows_y.reshape(part, n_y, parts, part)

    lines = to_lines(control, parts)
    smoothed = jnp.dot(matrix_x, lines, preferred_element_type=F32).astype(BF16)
    plane = level_plane(smoothed, parts)
    start = sum(
        jnp.einsum("xc,kc->xk", plane[s, g], rows_y[:, g, s], preferred_element_type=F32)
        for s in range(parts)
        for g in range(n_y)
    ).astype(BF16)
    start_state = to_blocks(start, levels, parts)

    padded = extended(start_state, (("gx", 0), ("gy", 2)), 1).astype(F32)
    start_state = start_state.astype(F32)
    end_state = (
        start_state
        - courant_x * (padded[2:, :, 1:-1] - padded[:-2, :, 1:-1]) * 0.5
        - courant_y * (padded[1:-1, :, 2:] - padded[1:-1, :, :-2]) * 0.5
    )
    misfit = obs_weight * (end_state - innovation)
    q = extended(courant_x * misfit, (("gx", 0),), 1)
    p = extended(courant_y * misfit, (("gy", 2),), 1)
    adjoint = (
        misfit + 0.5 * (q[2:] - q[:-2]) + 0.5 * (p[:, :, 2:] - p[:, :, :-2])
    ).astype(BF16)

    plane = level_plane(to_lines(adjoint, parts), parts)
    pulled = sum(
        jnp.einsum("xk,kc->xc", plane[s, g], columns_y[g, s], preferred_element_type=F32)
        for s in range(parts)
        for g in range(n_y)
    ).astype(BF16)
    carried = jnp.einsum("ij,ic->jc", matrix_x, pulled, preferred_element_type=F32)
    carried = to_blocks(carried.astype(BF16), levels, parts)
    gradient = control.astype(F32) + carried.astype(F32)
    return (end_state, gradient)


def solution(mesh):
    placed = (
        P("gx", None, "gy"),
        P("gx", None, "gy"),
        P("gx", None, "gy"),
        P("gx", None, "gy"),
        P("gx", None, "gy"),
        P("gx", None),
        P("gy", None),
    )
    return jax.shard_map(
        per_device,
        mesh=mesh,
        in_specs=placed,
        out_specs=(P("gx", None, "gy"), P("gx", None, "gy")),
        check_vma=False,
    )
```

```python
import functools

import jax
import jax.numpy as jnp
from jax import lax
from jax.experimental import pallas as pl
from jax.experimental.pallas import tpu as pltpu
from jax.sharding import PartitionSpec as P

BF16 = jnp.bfloat16
F32 = jnp.float32
STEP = 16
CHUNKS = 2
PARAMS = pltpu.CompilerParams(vmem_limit_bytes=56 * 1024 * 1024)


def cost(flops, *arrays):
    return pl.CostEstimate(
        flops=flops,
        bytes_accessed=sum(a.size * a.dtype.itemsize for a in arrays),
        transcendentals=0,
    )


def lines_body(parts, block, out, turned):
    levels, width = block.shape[1:]
    part = width // parts
    turned[...] = block[...].astype(F32)
    for l in range(levels):
        for s in range(parts):
            out[l * parts + s] = turned[:, l, s * part : (s + 1) * part].astype(BF16)


def as_lines(block, parts):
    rows, levels, width = block.shape
    shape = (levels * parts, rows, width // parts)
    return pl.pallas_call(
        functools.partial(lines_body, parts),
        grid=(rows // STEP,),
        in_specs=[pl.BlockSpec((STEP, levels, width), lambda i: (i, 0, 0))],
        out_specs=pl.BlockSpec((shape[0], STEP, shape[2]), lambda i: (0, i, 0)),
        out_shape=jax.ShapeDtypeStruct(shape, BF16),
        scratch_shapes=[pltpu.VMEM((STEP, levels, width), F32)],
        compiler_params=PARAMS,
        cost_estimate=cost(0, block, block),
        name="as_lines",
    )(block)


def gradient_body(parts, lines, control, out, turned):
    levels, width = control.shape[1:]
    part = width // parts
    for l in range(levels):
        for s in range(parts):
            turned[:, l, s * part : (s + 1) * part] = lines[l * parts + s].astype(F32)
    out[...] = control[...].astype(F32) + turned[...]


def add_lines(control, lines, parts):
    rows, levels, width = control.shape
    whole = (STEP, levels, width)
    return pl.pallas_call(
        functools.partial(gradient_body, parts),
        grid=(rows // STEP,),
        in_specs=[
            pl.BlockSpec((levels * parts, STEP, width // parts), lambda i: (0, i, 0)),
            pl.BlockSpec(whole, lambda i: (i, 0, 0)),
        ],
        out_specs=pl.BlockSpec(whole, lambda i: (i, 0, 0)),
        out_shape=jax.ShapeDtypeStruct(control.shape, F32),
        scratch_shapes=[pltpu.VMEM(whole, F32)],
        compiler_params=PARAMS,
        cost_estimate=cost(control.size, control, control, control, control),
        name="add_lines",
    )(lines, control)


def forward_body(parts, *refs):
    lines = refs[:CHUNKS]
    rows_in, sides, innovation, weight, wind_x, wind_y = refs[CHUNKS : CHUNKS + 6]
    end, flat, row_flux, side_flux, state, flux = refs[CHUNKS + 6 :]
    step = pl.program_id(0)
    rows, levels, width = flat.shape
    part = width // parts
    cut = rows // CHUNKS

    @pl.when(step == 0)
    def _():
        state[pl.ds(0, 1)] = rows_in[pl.ds(0, 1)]
        state[pl.ds(rows + 1, 1)] = rows_in[pl.ds(1, 1)]
        for h in range(CHUNKS):
            for l in range(levels):
                for s in range(parts):
                    got = lines[h][l * parts + s].astype(F32)
                    state[pl.ds(1 + h * cut, cut), l, s * part : (s + 1) * part] = got
        flux[pl.ds(0, 2)] = jnp.zeros((2, levels, width), F32)
        flux[pl.ds(rows + 2, 1)] = jnp.zeros((1, levels, width), F32)

    first = step * STEP
    place = lax.broadcasted_iota(jnp.int32, (STEP, levels, width), 2)
    left_edge, right_edge = place == 0, place == width - 1
    here = state[pl.ds(first + 1, STEP)]
    cx, cy = wind_x[...], wind_y[...]
    left = jnp.where(left_edge, sides[:, :, 0:1], pltpu.roll(here, 1, 2))
    right = jnp.where(right_edge, sides[:, :, 1:2], pltpu.roll(here, width - 1, 2))
    after = (
        here
        - cx * (state[pl.ds(first + 2, STEP)] - state[pl.ds(first, STEP)]) * 0.5
        - cy * (right - left) * 0.5
    )
    end[...] = after
    misfit = weight[...] * (after - innovation[...])
    p = cy * misfit
    side_flux[:, :, 0:1] = p[:, :, 0:1]
    side_flux[:, :, 1:2] = p[:, :, width - 1 : width]
    left = jnp.where(left_edge, 0.0, pltpu.roll(p, 1, 2))
    right = jnp.where(right_edge, 0.0, pltpu.roll(p, width - 1, 2))
    flat[pl.ds(first, STEP)] = misfit + 0.5 * (right - left)
    flux[pl.ds(first + 2, STEP)] = cx * misfit

    @pl.when(step == 0)
    def _():
        flat[pl.ds(0, STEP - 1)] += 0.5 * (
            flux[pl.ds(3, STEP - 1)] - flux[pl.ds(1, STEP - 1)]
        )

    @pl.when(step > 0)
    def _():
        flat[pl.ds(first - 1, STEP)] += 0.5 * (
            flux[pl.ds(first + 2, STEP)] - flux[pl.ds(first, STEP)]
        )

    @pl.when(step == rows // STEP - 1)
    def _():
        flat[pl.ds(rows - 1, 1)] += -0.5 * flux[pl.ds(rows, 1)]
        row_flux[pl.ds(0, 1)] = flux[pl.ds(2, 1)]
        row_flux[pl.ds(1, 1)] = flux[pl.ds(rows + 1, 1)]


def forward(lines, rows_in, sides, innovation, weight, wind_x, wind_y, parts):
    rows, levels, width = innovation.shape
    blocked = pl.BlockSpec((STEP, levels, width), lambda i: (i, 0, 0))
    side = pl.BlockSpec((STEP, levels, 2), lambda i: (i, 0, 0))
    pair = pl.BlockSpec((2, levels, width), lambda i: (0, 0, 0))
    line = pl.BlockSpec(lines[0].shape, lambda i: (0, 0, 0))
    whole = pl.BlockSpec((rows, levels, width), lambda i: (0, 0, 0))
    return pl.pallas_call(
        functools.partial(forward_body, parts),
        grid=(rows // STEP,),
        in_specs=[line] * CHUNKS + [pair, side, blocked, blocked, blocked, blocked],
        out_specs=[blocked, whole, pair, side],
        out_shape=[
            jax.ShapeDtypeStruct((rows, levels, width), F32),
            jax.ShapeDtypeStruct((rows, levels, width), F32),
            jax.ShapeDtypeStruct((2, levels, width), F32),
            jax.ShapeDtypeStruct((rows, levels, 2), F32),
        ],
        scratch_shapes=[
            pltpu.VMEM((rows + 2, levels, width), F32),
            pltpu.VMEM((rows + 3, levels, width), F32),
        ],
        compiler_params=PARAMS,
        cost_estimate=cost(30 * innovation.size, *[innovation] * 7),
        name="forward",
    )(*lines, rows_in, sides, innovation, weight, wind_x, wind_y)


def rim_body(parts, offset, last, flat, rows_in, sides, out, turned):
    step = pl.program_id(0) + offset
    levels, width = flat.shape[1:]
    part = width // parts
    place = lax.broadcasted_iota(jnp.int32, flat.shape, 2)
    value = flat[...]
    value = value - jnp.where(place == 0, 0.5 * sides[:, :, 0:1], 0.0)
    value = value + jnp.where(place == width - 1, 0.5 * sides[:, :, 1:2], 0.0)
    turned[...] = value

    @pl.when(step == 0)
    def _():
        turned[pl.ds(0, 1)] += -0.5 * rows_in[pl.ds(0, 1)]

    @pl.when(step == last)
    def _():
        turned[pl.ds(STEP - 1, 1)] += 0.5 * rows_in[pl.ds(1, 1)]

    for l in range(levels):
        for s in range(parts):
            out[l * parts + s] = turned[:, l, s * part : (s + 1) * part].astype(BF16)


def rim_lines(flat, rows_in, sides, parts, chunk):
    rows, levels, width = flat.shape
    cut = rows // CHUNKS
    offset = chunk * cut // STEP
    shape = (levels * parts, cut, width // parts)
    return pl.pallas_call(
        functools.partial(rim_body, parts, offset, rows // STEP - 1),
        grid=(cut // STEP,),
        in_specs=[
            pl.BlockSpec((STEP, levels, width), lambda i: (i + offset, 0, 0)),
            pl.BlockSpec((2, levels, width), lambda i: (0, 0, 0)),
            pl.BlockSpec((STEP, levels, 2), lambda i: (i + offset, 0, 0)),
        ],
        out_specs=pl.BlockSpec((shape[0], STEP, shape[2]), lambda i: (0, i, 0)),
        out_shape=jax.ShapeDtypeStruct(shape, BF16),
        scratch_shapes=[pltpu.VMEM((STEP, levels, width), F32)],
        compiler_params=PARAMS,
        cost_estimate=cost(4 * flat.size, flat, flat),
        name="rim_lines",
    )(flat, rows_in, sides)


def swap_all(lines):
    return lax.all_to_all(lines, "gx", 0, 0, tiled=True)


def plane_pieces(lines, parts):
    n_x, n_y = lax.axis_size("gx"), lax.axis_size("gy")
    groups = [list(range(i, i + parts)) for i in range(0, n_x, parts)]
    if n_y == 2 and parts == 2:
        pairs = [(a, b) for g in groups for a, b in (g, g[::-1])]
        far = lax.ppermute(lines, "gy", [(0, 1), (1, 0)])
        near = lax.ppermute(lines, "gx", pairs)
        cross = lax.ppermute(far, "gx", pairs)
        return [lines, near, far, cross]
    plane = lax.all_gather(lines, "gy", axis=0, tiled=False)
    plane = lax.all_gather(plane, "gx", axis=0, tiled=False, axis_index_groups=groups)
    return [plane[s, g] for s in range(parts) for g in range(n_y)]


def piece_order(parts):
    n_y = lax.axis_size("gy")
    sub, me = lax.rem(lax.axis_index("gx"), parts), lax.axis_index("gy")
    if n_y == 2 and parts == 2:
        return [(sub, me), (1 - sub, me), (sub, 1 - me), (1 - sub, 1 - me)]
    return [(s, g) for s in range(parts) for g in range(n_y)]


def filter_pieces(filter_y, parts):
    width, n_y = filter_y.shape[0], lax.axis_size("gy")
    part = width // parts
    sub, me = lax.rem(lax.axis_index("gx"), parts), lax.axis_index("gy")
    order = piece_order(parts)
    rows = [
        lax.dynamic_slice(filter_y, (sub * part, g * width + s * part), (part, part))
        for s, g in order
    ]
    if n_y == 2 and parts == 2:
        mine = lax.dynamic_slice(filter_y, (0, me * width + sub * part), (width, part))
        sent = lax.dynamic_slice(
            filter_y, (0, (1 - me) * width + sub * part), (width, part)
        )
        got = lax.ppermute(sent, "gy", [(0, 1), (1, 0)])
        columns = [
            lax.dynamic_slice_in_dim(source, s * part, part, axis=0)
            for source, (s, _) in zip((mine, mine, got, got), order)
        ]
    else:
        split = filter_y.reshape(width, n_y, parts, part)
        split = lax.dynamic_index_in_dim(split, sub, axis=2, keepdims=False)
        split = lax.all_to_all(split, "gy", 1, 0, tiled=True)
        split = split.reshape(n_y, parts, part, part)
        columns = [split[g, s] for s, g in order]
    return rows, columns


def row_halo(first, last):
    n_x = lax.axis_size("gx")
    up = [(i, i + 1) for i in range(n_x - 1)]
    down = [(i + 1, i) for i in range(n_x - 1)]
    return jnp.stack([lax.ppermute(last, "gx", up), lax.ppermute(first, "gx", down)])


def side_halo(first, last):
    n_y, me = lax.axis_size("gy"), lax.axis_index("gy")
    if n_y == 2:
        got = lax.ppermute(jnp.where(me == 0, last, first), "gy", [(0, 1), (1, 0)])
        none = jnp.zeros_like(got)
        return jnp.where(me == 0, none, got), jnp.where(me == 0, got, none)
    up = [(i, i + 1) for i in range(n_y - 1)]
    down = [(i + 1, i) for i in range(n_y - 1)]
    return lax.ppermute(last, "gy", up), lax.ppermute(first, "gy", down)


def per_device(control, innovation, obs_weight, courant_x, courant_y, filter_x, filter_y):
    rows, levels, width = control.shape
    n_x = lax.axis_size("gx")
    parts = n_x // levels
    part = width // parts
    cut = rows // CHUNKS

    lines = swap_all(as_lines(control, parts)).reshape(n_x * rows, part)
    matrix_x = lax.all_gather(filter_x, "gx", axis=0, tiled=True)
    rows_y, columns_y = filter_pieces(filter_y, parts)
    split_x = matrix_x.reshape(n_x, CHUNKS, cut, n_x * rows)

    came = []
    for h in range(CHUNKS):
        smoothed = jnp.einsum(
            "brj,jc->brc", split_x[:, h], lines, preferred_element_type=F32
        ).astype(BF16)
        start = sum(
            jnp.einsum("brc,kc->brk", piece, matrix, preferred_element_type=F32)
            for piece, matrix in zip(plane_pieces(smoothed, parts), rows_y)
        )
        came.append(swap_all(start.astype(BF16)))

    def as_row(edge):
        edge = edge.reshape(levels, parts * part)
        return edge

    rows_in = row_halo(as_row(came[0][:, 0]), as_row(came[-1][:, -1])).astype(F32)
    by_level = [c.reshape(levels, parts, cut, part) for c in came]
    first = jnp.concatenate([c[:, 0, :, 0] for c in by_level], axis=1)
    last = jnp.concatenate([c[:, -1, :, -1] for c in by_level], axis=1)
    before, after = side_halo(first, last)
    sides = jnp.stack([before.T, after.T], axis=2).astype(F32)

    end_state, flat, row_flux, side_flux = forward(
        came, rows_in, sides, innovation, obs_weight, courant_x, courant_y, parts
    )
    rows_in = row_halo(row_flux[0], row_flux[1])
    before, after = side_halo(side_flux[:, :, 0].T, side_flux[:, :, 1].T)
    sides = jnp.stack([before.T, after.T], axis=2)

    carried = 0.0
    for h in range(CHUNKS):
        adjoint = swap_all(rim_lines(flat, rows_in, sides, parts, h))
        pulled = sum(
            jnp.einsum("brk,kc->brc", piece, matrix, preferred_element_type=F32)
            for piece, matrix in zip(plane_pieces(adjoint, parts), columns_y)
        ).astype(BF16)
        carried = carried + jnp.einsum(
            "brj,brc->jc", split_x[:, h], pulled, preferred_element_type=F32
        )
    carried = swap_all(carried.astype(BF16).reshape(n_x, rows, part))
    return (end_state, add_lines(control, carried, parts))


def solution(mesh):
    placed = (
        P("gx", None, "gy"),
        P("gx", None, "gy"),
        P("gx", None, "gy"),
        P("gx", None, "gy"),
        P("gx", None, "gy"),
        P("gx", None),
        P("gy", None),
    )
    return jax.shard_map(
        per_device,
        mesh=mesh,
        in_specs=placed,
        out_specs=(P("gx", None, "gy"), P("gx", None, "gy")),
        check_vma=False,
    )
```

```python
import functools

import jax
import jax.numpy as jnp
from jax import lax
from jax.experimental import pallas as pl
from jax.experimental.pallas import tpu as pltpu
from jax.sharding import PartitionSpec as P

BF16 = jnp.bfloat16
F32 = jnp.float32
STEP = 16
CHUNKS = 2
PARAMS = pltpu.CompilerParams(vmem_limit_bytes=56 * 1024 * 1024)


def cost(flops, *arrays):
    return pl.CostEstimate(
        flops=flops,
        bytes_accessed=sum(a.size * a.dtype.itemsize for a in arrays),
        transcendentals=0,
    )


def lines_body(parts, block, out, turned):
    levels, width = block.shape[1:]
    part = width // parts
    turned[...] = block[...].astype(F32)
    for l in range(levels):
        for s in range(parts):
            out[l * parts + s] = turned[:, l, s * part : (s + 1) * part].astype(BF16)


def as_lines(block, parts):
    rows, levels, width = block.shape
    shape = (levels * parts, rows, width // parts)
    return pl.pallas_call(
        functools.partial(lines_body, parts),
        grid=(rows // STEP,),
        in_specs=[pl.BlockSpec((STEP, levels, width), lambda i: (i, 0, 0))],
        out_specs=pl.BlockSpec((shape[0], STEP, shape[2]), lambda i: (0, i, 0)),
        out_shape=jax.ShapeDtypeStruct(shape, BF16),
        scratch_shapes=[pltpu.VMEM((STEP, levels, width), F32)],
        compiler_params=PARAMS,
        cost_estimate=cost(0, block, block),
        name="as_lines",
    )(block)


def gradient_body(parts, *refs):
    lines, (control, out, turned) = refs[:CHUNKS], refs[CHUNKS:]
    levels, width = control.shape[1:]
    piece = width // parts // CHUNKS
    for l in range(levels):
        for s in range(parts):
            for w in range(CHUNKS):
                at = (s * CHUNKS + w) * piece
                got = lines[w][l * parts + s].astype(F32)
                turned[:, l, at : at + piece] = got
    out[...] = control[...].astype(F32) + turned[...]


def add_lines(control, lines, parts):
    rows, levels, width = control.shape
    whole = (STEP, levels, width)
    return pl.pallas_call(
        functools.partial(gradient_body, parts),
        grid=(rows // STEP,),
        in_specs=[
            pl.BlockSpec((l.shape[0], STEP, l.shape[2]), lambda i: (0, i, 0)) for l in lines
        ]
        + [pl.BlockSpec(whole, lambda i: (i, 0, 0))],
        out_specs=pl.BlockSpec(whole, lambda i: (i, 0, 0)),
        out_shape=jax.ShapeDtypeStruct(control.shape, F32),
        scratch_shapes=[pltpu.VMEM(whole, F32)],
        compiler_params=PARAMS,
        cost_estimate=cost(control.size, control, control, control, control),
        name="add_lines",
    )(*lines, control)


def forward_body(parts, *refs):
    lines = refs[:CHUNKS]
    rows_in, sides, innovation, weight, wind_x, wind_y = refs[CHUNKS : CHUNKS + 6]
    end, flat, row_flux, side_flux, state, flux = refs[CHUNKS + 6 :]
    step = pl.program_id(0)
    rows, levels, width = flat.shape
    part = width // parts
    cut = rows // CHUNKS

    @pl.when(step == 0)
    def _():
        state[pl.ds(0, 1)] = rows_in[pl.ds(0, 1)]
        state[pl.ds(rows + 1, 1)] = rows_in[pl.ds(1, 1)]
        for h in range(CHUNKS):
            for l in range(levels):
                for s in range(parts):
                    got = lines[h][l * parts + s].astype(F32)
                    state[pl.ds(1 + h * cut, cut), l, s * part : (s + 1) * part] = got
        flux[pl.ds(0, 2)] = jnp.zeros((2, levels, width), F32)
        flux[pl.ds(rows + 2, 1)] = jnp.zeros((1, levels, width), F32)

    first = step * STEP
    place = lax.broadcasted_iota(jnp.int32, (levels, width), 1)
    left_edge, right_edge = place == 0, place == width - 1
    for j in range(STEP):
        r = first + j
        here = state[r + 1]
        cx, cy = wind_x[j], wind_y[j]
        left = jnp.where(left_edge, sides[j, :, 0:1], pltpu.roll(here, 1, 1))
        right = jnp.where(right_edge, sides[j, :, 1:2], pltpu.roll(here, width - 1, 1))
        after = here - cx * (state[r + 2] - state[r]) * 0.5 - cy * (right - left) * 0.5
        end[j] = after
        misfit = weight[j] * (after - innovation[j])
        p, q = cy * misfit, cx * misfit
        side_flux[j, :, 0:1] = p[:, 0:1]
        side_flux[j, :, 1:2] = p[:, width - 1 : width]
        left = jnp.where(left_edge, 0.0, pltpu.roll(p, 1, 1))
        right = jnp.where(right_edge, 0.0, pltpu.roll(p, width - 1, 1))
        flat[r] = misfit + 0.5 * (right - left)
        flux[r + 2] = q
        if j > 0:
            flat[r - 1] += 0.5 * (q - flux[r])
        else:

            @pl.when(step > 0)
            def _():
                flat[r - 1] += 0.5 * (flux[r + 2] - flux[r])

    @pl.when(step == rows // STEP - 1)
    def _():
        flat[pl.ds(rows - 1, 1)] += -0.5 * flux[pl.ds(rows, 1)]
        row_flux[pl.ds(0, 1)] = flux[pl.ds(2, 1)]
        row_flux[pl.ds(1, 1)] = flux[pl.ds(rows + 1, 1)]


def forward(lines, rows_in, sides, innovation, weight, wind_x, wind_y, parts):
    rows, levels, width = innovation.shape
    blocked = pl.BlockSpec((STEP, levels, width), lambda i: (i, 0, 0))
    side = pl.BlockSpec((STEP, levels, 2), lambda i: (i, 0, 0))
    pair = pl.BlockSpec((2, levels, width), lambda i: (0, 0, 0))
    line = pl.BlockSpec(lines[0].shape, lambda i: (0, 0, 0))
    whole = pl.BlockSpec((rows, levels, width), lambda i: (0, 0, 0))
    return pl.pallas_call(
        functools.partial(forward_body, parts),
        grid=(rows // STEP,),
        in_specs=[line] * CHUNKS + [pair, side, blocked, blocked, blocked, blocked],
        out_specs=[blocked, whole, pair, side],
        out_shape=[
            jax.ShapeDtypeStruct((rows, levels, width), F32),
            jax.ShapeDtypeStruct((rows, levels, width), F32),
            jax.ShapeDtypeStruct((2, levels, width), F32),
            jax.ShapeDtypeStruct((rows, levels, 2), F32),
        ],
        scratch_shapes=[
            pltpu.VMEM((rows + 2, levels, width), F32),
            pltpu.VMEM((rows + 3, levels, width), F32),
        ],
        compiler_params=PARAMS,
        cost_estimate=cost(30 * innovation.size, *[innovation] * 7),
        name="forward",
    )(*lines, rows_in, sides, innovation, weight, wind_x, wind_y)


def rim_body(parts, offset, last, flat, rows_in, sides, out, turned):
    step = pl.program_id(0) + offset
    levels, width = flat.shape[1:]
    part = width // parts
    place = lax.broadcasted_iota(jnp.int32, flat.shape, 2)
    value = flat[...]
    value = value - jnp.where(place == 0, 0.5 * sides[:, :, 0:1], 0.0)
    value = value + jnp.where(place == width - 1, 0.5 * sides[:, :, 1:2], 0.0)
    turned[...] = value

    @pl.when(step == 0)
    def _():
        turned[pl.ds(0, 1)] += -0.5 * rows_in[pl.ds(0, 1)]

    @pl.when(step == last)
    def _():
        turned[pl.ds(STEP - 1, 1)] += 0.5 * rows_in[pl.ds(1, 1)]

    for l in range(levels):
        for s in range(parts):
            out[l * parts + s] = turned[:, l, s * part : (s + 1) * part].astype(BF16)


def rim_lines(flat, rows_in, sides, parts, chunk):
    rows, levels, width = flat.shape
    cut = rows // CHUNKS
    offset = chunk * cut // STEP
    shape = (levels * parts, cut, width // parts)
    return pl.pallas_call(
        functools.partial(rim_body, parts, offset, rows // STEP - 1),
        grid=(cut // STEP,),
        in_specs=[
            pl.BlockSpec((STEP, levels, width), lambda i: (i + offset, 0, 0)),
            pl.BlockSpec((2, levels, width), lambda i: (0, 0, 0)),
            pl.BlockSpec((STEP, levels, 2), lambda i: (i + offset, 0, 0)),
        ],
        out_specs=pl.BlockSpec((shape[0], STEP, shape[2]), lambda i: (0, i, 0)),
        out_shape=jax.ShapeDtypeStruct(shape, BF16),
        scratch_shapes=[pltpu.VMEM((STEP, levels, width), F32)],
        compiler_params=PARAMS,
        cost_estimate=cost(4 * flat.size, flat, flat),
        name="rim_lines",
    )(flat, rows_in, sides)


def swap_all(lines):
    return lax.all_to_all(lines, "gx", 0, 0, tiled=True)


def plane_pieces(lines, parts):
    n_x, n_y = lax.axis_size("gx"), lax.axis_size("gy")
    groups = [list(range(i, i + parts)) for i in range(0, n_x, parts)]
    if n_y == 2 and parts == 2:
        pairs = [(a, b) for g in groups for a, b in (g, g[::-1])]
        far = lax.ppermute(lines, "gy", [(0, 1), (1, 0)])
        near = lax.ppermute(lines, "gx", pairs)
        cross = lax.ppermute(far, "gx", pairs)
        return [lines, near, far, cross]
    plane = lax.all_gather(lines, "gy", axis=0, tiled=False)
    plane = lax.all_gather(plane, "gx", axis=0, tiled=False, axis_index_groups=groups)
    return [plane[s, g] for s in range(parts) for g in range(n_y)]


def piece_order(parts):
    n_y = lax.axis_size("gy")
    sub, me = lax.rem(lax.axis_index("gx"), parts), lax.axis_index("gy")
    if n_y == 2 and parts == 2:
        return [(sub, me), (1 - sub, me), (sub, 1 - me), (1 - sub, 1 - me)]
    return [(s, g) for s in range(parts) for g in range(n_y)]


def filter_pieces(filter_y, parts):
    width, n_y = filter_y.shape[0], lax.axis_size("gy")
    part = width // parts
    sub, me = lax.rem(lax.axis_index("gx"), parts), lax.axis_index("gy")
    order = piece_order(parts)
    rows = [
        lax.dynamic_slice(filter_y, (sub * part, g * width + s * part), (part, part))
        for s, g in order
    ]
    if n_y == 2 and parts == 2:
        mine = lax.dynamic_slice(filter_y, (0, me * width + sub * part), (width, part))
        sent = lax.dynamic_slice(
            filter_y, (0, (1 - me) * width + sub * part), (width, part)
        )
        got = lax.ppermute(sent, "gy", [(0, 1), (1, 0)])
        columns = [
            lax.dynamic_slice_in_dim(source, s * part, part, axis=0)
            for source, (s, _) in zip((mine, mine, got, got), order)
        ]
    else:
        split = filter_y.reshape(width, n_y, parts, part)
        split = lax.dynamic_index_in_dim(split, sub, axis=2, keepdims=False)
        split = lax.all_to_all(split, "gy", 1, 0, tiled=True)
        split = split.reshape(n_y, parts, part, part)
        columns = [split[g, s] for s, g in order]
    return rows, columns


def row_halo(first, last):
    n_x = lax.axis_size("gx")
    up = [(i, i + 1) for i in range(n_x - 1)]
    down = [(i + 1, i) for i in range(n_x - 1)]
    return jnp.stack([lax.ppermute(last, "gx", up), lax.ppermute(first, "gx", down)])


def side_halo(first, last):
    n_y, me = lax.axis_size("gy"), lax.axis_index("gy")
    if n_y == 2:
        got = lax.ppermute(jnp.where(me == 0, last, first), "gy", [(0, 1), (1, 0)])
        none = jnp.zeros_like(got)
        return jnp.where(me == 0, none, got), jnp.where(me == 0, got, none)
    up = [(i, i + 1) for i in range(n_y - 1)]
    down = [(i + 1, i) for i in range(n_y - 1)]
    return lax.ppermute(last, "gy", up), lax.ppermute(first, "gy", down)


def per_device(control, innovation, obs_weight, courant_x, courant_y, filter_x, filter_y):
    rows, levels, width = control.shape
    n_x = lax.axis_size("gx")
    parts = n_x // levels
    part = width // parts
    cut = rows // CHUNKS

    turned = as_lines(control, parts)
    rows_y, columns_y = filter_pieces(filter_y, parts)
    matrix_x = [lax.all_gather(filter_x[:cut], "gx", axis=0, tiled=True)]
    lines = swap_all(turned).reshape(n_x * rows, part)
    lines, filter_x = lax.optimization_barrier((lines, filter_x))
    for h in range(1, CHUNKS):
        share = filter_x[h * cut : (h + 1) * cut]
        matrix_x.append(lax.all_gather(share, "gx", axis=0, tiled=True))
    lines, columns_y = lax.optimization_barrier((lines, columns_y))

    came = []
    for h in range(CHUNKS):
        smoothed = jnp.dot(matrix_x[h], lines, preferred_element_type=F32)
        smoothed = smoothed.astype(BF16).reshape(n_x, cut, part)
        start = sum(
            jnp.einsum("brc,kc->brk", piece, matrix, preferred_element_type=F32)
            for piece, matrix in zip(plane_pieces(smoothed, parts), rows_y)
        )
        came.append(swap_all(start.astype(BF16)))

    def as_row(edge):
        edge = edge.reshape(levels, parts * part)
        return edge

    rows_in = row_halo(as_row(came[0][:, 0]), as_row(came[-1][:, -1])).astype(F32)
    by_level = [c.reshape(levels, parts, cut, part) for c in came]
    first = jnp.concatenate([c[:, 0, :, 0] for c in by_level], axis=1)
    last = jnp.concatenate([c[:, -1, :, -1] for c in by_level], axis=1)
    before, after = side_halo(first, last)
    sides = jnp.stack([before.T, after.T], axis=2).astype(F32)

    end_state, flat, row_flux, side_flux = forward(
        came, rows_in, sides, innovation, obs_weight, courant_x, courant_y, parts
    )
    rows_in = row_halo(row_flux[0], row_flux[1])
    before, after = side_halo(side_flux[:, :, 0].T, side_flux[:, :, 1].T)
    sides = jnp.stack([before.T, after.T], axis=2)

    planes = [
        plane_pieces(swap_all(rim_lines(flat, rows_in, sides, parts, h)), parts)
        for h in range(CHUNKS)
    ]
    piece = part // CHUNKS
    carried = []
    for w in range(CHUNKS):
        total = 0.0
        for h in range(CHUNKS):
            pulled = sum(
                jnp.einsum(
                    "brk,kc->brc",
                    plane,
                    matrix[:, w * piece : (w + 1) * piece],
                    preferred_element_type=F32,
                )
                for plane, matrix in zip(planes[h], columns_y)
            ).astype(BF16)
            total = total + jnp.einsum(
                "ij,ic->jc",
                matrix_x[h],
                pulled.reshape(n_x * cut, piece),
                preferred_element_type=F32,
            )
        carried.append(swap_all(total.astype(BF16).reshape(n_x, rows, piece)))
    return (end_state, add_lines(control, carried, parts))


def solution(mesh):
    placed = (
        P("gx", None, "gy"),
        P("gx", None, "gy"),
        P("gx", None, "gy"),
        P("gx", None, "gy"),
        P("gx", None, "gy"),
        P("gx", None),
        P("gy", None),
    )
    return jax.shard_map(
        per_device,
        mesh=mesh,
        in_specs=placed,
        out_specs=(P("gx", None, "gy"), P("gx", None, "gy")),
        check_vma=False,
    )
```

```python
import functools

import jax
import jax.numpy as jnp
from jax import lax
from jax.experimental import pallas as pl
from jax.experimental.pallas import tpu as pltpu
from jax.sharding import PartitionSpec as P

BF16 = jnp.bfloat16
F32 = jnp.float32
STEP = 16
CHUNKS = 2
PARAMS = pltpu.CompilerParams(vmem_limit_bytes=56 * 1024 * 1024)


def cost(flops, *arrays):
    return pl.CostEstimate(
        flops=flops,
        bytes_accessed=sum(a.size * a.dtype.itemsize for a in arrays),
        transcendentals=0,
    )


def store_lines(turned, out, parts, chunk):
    levels, width = turned.shape[1:]
    part, piece = width // parts, out.shape[2]
    for l in range(levels):
        for s in range(parts):
            at = s * part + chunk * piece
            out[l * parts + s] = turned[:, l, at : at + piece].astype(BF16)


def lines_body(parts, chunk, block, out, turned):
    turned[...] = block[...].astype(F32)
    store_lines(turned, out, parts, chunk)


def as_lines(block, parts, chunk):
    rows, levels, width = block.shape
    shape = (levels * parts, rows, width // parts // CHUNKS)
    return pl.pallas_call(
        functools.partial(lines_body, parts, chunk),
        grid=(rows // STEP,),
        in_specs=[pl.BlockSpec((STEP, levels, width), lambda i: (i, 0, 0))],
        out_specs=pl.BlockSpec((shape[0], STEP, shape[2]), lambda i: (0, i, 0)),
        out_shape=jax.ShapeDtypeStruct(shape, BF16),
        scratch_shapes=[pltpu.VMEM((STEP, levels, width), F32)],
        compiler_params=PARAMS,
        cost_estimate=cost(0, block, block),
        name="as_lines",
    )(block)


def gradient_body(parts, lines, control, *rest):
    out, turned = rest[-2:]
    levels, width = control.shape[1:]
    part = width // parts
    for l in range(levels):
        for s in range(parts):
            turned[:, l, s * part : (s + 1) * part] = lines[l * parts + s].astype(F32)
    out[...] = control[...].astype(F32) + turned[...]


def add_lines(control, lines, parts, chunk, target):
    rows, levels, width = control.shape
    whole = (STEP, levels, width)
    cut = rows // CHUNKS
    offset = chunk * cut // STEP
    operands = [lines, control] + ([] if target is None else [target])
    return pl.pallas_call(
        functools.partial(gradient_body, parts),
        grid=(cut // STEP,),
        in_specs=[
            pl.BlockSpec((lines.shape[0], STEP, lines.shape[2]), lambda i: (0, i, 0)),
            pl.BlockSpec(whole, lambda i: (i + offset, 0, 0)),
        ]
        + [pl.BlockSpec(memory_space=pl.ANY)] * (len(operands) - 2),
        out_specs=pl.BlockSpec(whole, lambda i: (i + offset, 0, 0)),
        out_shape=jax.ShapeDtypeStruct(control.shape, F32),
        input_output_aliases={} if target is None else {2: 0},
        scratch_shapes=[pltpu.VMEM(whole, F32)],
        compiler_params=PARAMS,
        cost_estimate=cost(control.size // 2, control, control),
        name="add_lines",
    )(*operands)


def forward_body(*refs):
    starts = refs[:CHUNKS]
    rows_in, sides, innovation, weight, wind_x, wind_y = refs[CHUNKS : CHUNKS + 6]
    end, flat, row_flux, side_flux, state, carry = refs[CHUNKS + 6 :]
    step = pl.program_id(0)
    rows, levels, width = flat.shape
    cut = rows // CHUNKS

    @pl.when(step == 0)
    def _():
        state[pl.ds(0, 1)] = rows_in[pl.ds(0, 1)]
        state[pl.ds(rows + 1, 1)] = rows_in[pl.ds(1, 1)]
        for h in range(CHUNKS):
            state[pl.ds(1 + h * cut, cut)] = starts[h][...].astype(F32)
        carry[...] = jnp.zeros(carry.shape, F32)

    first = step * STEP
    place = lax.broadcasted_iota(jnp.int32, (levels, width), 1)
    left_edge, right_edge = place == 0, place == width - 1
    q_old, q_last, pending = carry[0], carry[1], carry[2]
    up, here = state[first], state[first + 1]
    for j in range(STEP):
        down = state[first + j + 2]
        cx, cy = wind_x[j], wind_y[j]
        left = jnp.where(left_edge, sides[j, :, 0:1], pltpu.roll(here, 1, 1))
        right = jnp.where(right_edge, sides[j, :, 1:2], pltpu.roll(here, width - 1, 1))
        after = here - cx * (down - up) * 0.5 - cy * (right - left) * 0.5
        end[j] = after
        misfit = weight[j] * (after - innovation[j])
        p, q = cy * misfit, cx * misfit
        side_flux[j, :, 0:1] = p[:, 0:1]
        side_flux[j, :, 1:2] = p[:, width - 1 : width]
        at = first + j - 1 if j > 0 else jnp.maximum(first - 1, 0)
        flat[at] = pending + 0.5 * (q - q_old)
        left = jnp.where(left_edge, 0.0, pltpu.roll(p, 1, 1))
        right = jnp.where(right_edge, 0.0, pltpu.roll(p, width - 1, 1))
        pending = misfit + 0.5 * (right - left)
        q_old, q_last = q_last, q
        up, here = here, down
        if j == 0:

            @pl.when(step == 0)
            def _(q=q):
                row_flux[0] = q

    carry[0], carry[1], carry[2] = q_old, q_last, pending

    @pl.when(step == rows // STEP - 1)
    def _():
        flat[rows - 1] = pending - 0.5 * q_old
        row_flux[1] = q_last


def forward(starts, rows_in, sides, innovation, weight, wind_x, wind_y):
    rows, levels, width = innovation.shape
    blocked = pl.BlockSpec((STEP, levels, width), lambda i: (i, 0, 0))
    side = pl.BlockSpec((STEP, levels, 2), lambda i: (i, 0, 0))
    pair = pl.BlockSpec((2, levels, width), lambda i: (0, 0, 0))
    start = pl.BlockSpec(starts[0].shape, lambda i: (0, 0, 0))
    whole = pl.BlockSpec((rows, levels, width), lambda i: (0, 0, 0))
    return pl.pallas_call(
        forward_body,
        grid=(rows // STEP,),
        in_specs=[start] * CHUNKS + [pair, side, blocked, blocked, blocked, blocked],
        out_specs=[blocked, whole, pair, side],
        out_shape=[
            jax.ShapeDtypeStruct((rows, levels, width), F32),
            jax.ShapeDtypeStruct((rows, levels, width), F32),
            jax.ShapeDtypeStruct((2, levels, width), F32),
            jax.ShapeDtypeStruct((rows, levels, 2), F32),
        ],
        scratch_shapes=[
            pltpu.VMEM((rows + 2, levels, width), F32),
            pltpu.VMEM((3, levels, width), F32),
        ],
        compiler_params=PARAMS,
        cost_estimate=cost(30 * innovation.size, *[innovation] * 7),
        name="forward",
    )(*starts, rows_in, sides, innovation, weight, wind_x, wind_y)


def rim_body(parts, chunk, last, flat, rows_in, sides, out, turned):
    step = pl.program_id(0)
    width = flat.shape[2]
    place = lax.broadcasted_iota(jnp.int32, flat.shape, 2)
    value = flat[...]
    value = value - jnp.where(place == 0, 0.5 * sides[:, :, 0:1], 0.0)
    value = value + jnp.where(place == width - 1, 0.5 * sides[:, :, 1:2], 0.0)
    turned[...] = value

    @pl.when(step == 0)
    def _():
        turned[pl.ds(0, 1)] += -0.5 * rows_in[pl.ds(0, 1)]

    @pl.when(step == last)
    def _():
        turned[pl.ds(STEP - 1, 1)] += 0.5 * rows_in[pl.ds(1, 1)]

    store_lines(turned, out, parts, chunk)


def rim_lines(flat, rows_in, sides, parts, chunk):
    rows, levels, width = flat.shape
    shape = (levels * parts, rows, width // parts // CHUNKS)
    return pl.pallas_call(
        functools.partial(rim_body, parts, chunk, rows // STEP - 1),
        grid=(rows // STEP,),
        in_specs=[
            pl.BlockSpec((STEP, levels, width), lambda i: (i, 0, 0)),
            pl.BlockSpec((2, levels, width), lambda i: (0, 0, 0)),
            pl.BlockSpec((STEP, levels, 2), lambda i: (i, 0, 0)),
        ],
        out_specs=pl.BlockSpec((shape[0], STEP, shape[2]), lambda i: (0, i, 0)),
        out_shape=jax.ShapeDtypeStruct(shape, BF16),
        scratch_shapes=[pltpu.VMEM((STEP, levels, width), F32)],
        compiler_params=PARAMS,
        cost_estimate=cost(4 * flat.size, flat, flat),
        name="rim_lines",
    )(flat, rows_in, sides)


def swap_all(lines):
    return lax.all_to_all(lines, "gx", 0, 0, tiled=True)


def plane_pieces(lines, parts):
    n_x, n_y = lax.axis_size("gx"), lax.axis_size("gy")
    groups = [list(range(i, i + parts)) for i in range(0, n_x, parts)]
    if n_y == 2 and parts == 2:
        pairs = [(a, b) for g in groups for a, b in (g, g[::-1])]
        far = lax.ppermute(lines, "gy", [(0, 1), (1, 0)])
        near = lax.ppermute(lines, "gx", pairs)
        cross = lax.ppermute(far, "gx", pairs)
        return [lines, near, far, cross]
    plane = lax.all_gather(lines, "gy", axis=0, tiled=False)
    plane = lax.all_gather(plane, "gx", axis=0, tiled=False, axis_index_groups=groups)
    return [plane[s, g] for s in range(parts) for g in range(n_y)]


def piece_order(parts):
    n_y = lax.axis_size("gy")
    sub, me = lax.rem(lax.axis_index("gx"), parts), lax.axis_index("gy")
    if n_y == 2 and parts == 2:
        return [(sub, me), (1 - sub, me), (sub, 1 - me), (1 - sub, 1 - me)]
    return [(s, g) for s in range(parts) for g in range(n_y)]


def filter_rows(filter_y, parts):
    width = filter_y.shape[0]
    part = width // parts
    sub = lax.rem(lax.axis_index("gx"), parts)
    return [
        lax.dynamic_slice(filter_y, (sub * part, g * width + s * part), (part, part))
        for s, g in piece_order(parts)
    ]


def filter_columns(filter_y, parts):
    width, n_y = filter_y.shape[0], lax.axis_size("gy")
    part = width // parts
    sub, me = lax.rem(lax.axis_index("gx"), parts), lax.axis_index("gy")
    order = piece_order(parts)
    if n_y == 2 and parts == 2:
        mine = lax.dynamic_slice(filter_y, (0, me * width + sub * part), (width, part))
        sent = lax.dynamic_slice(
            filter_y, (0, (1 - me) * width + sub * part), (width, part)
        )
        got = lax.ppermute(sent, "gy", [(0, 1), (1, 0)])
        return [
            lax.dynamic_slice_in_dim(source, s * part, part, axis=0)
            for source, (s, _) in zip((mine, mine, got, got), order)
        ]
    split = filter_y.reshape(width, n_y, parts, part)
    split = lax.dynamic_index_in_dim(split, sub, axis=2, keepdims=False)
    split = lax.all_to_all(split, "gy", 1, 0, tiled=True)
    split = split.reshape(n_y, parts, part, part)
    return [split[g, s] for s, g in order]


def row_halo(first, last):
    n_x = lax.axis_size("gx")
    up = [(i, i + 1) for i in range(n_x - 1)]
    down = [(i + 1, i) for i in range(n_x - 1)]
    return jnp.stack([lax.ppermute(last, "gx", up), lax.ppermute(first, "gx", down)])


def side_halo(first, last):
    n_y, me = lax.axis_size("gy"), lax.axis_index("gy")
    if n_y == 2:
        got = lax.ppermute(jnp.where(me == 0, last, first), "gy", [(0, 1), (1, 0)])
        none = jnp.zeros_like(got)
        return jnp.where(me == 0, none, got), jnp.where(me == 0, got, none)
    up = [(i, i + 1) for i in range(n_y - 1)]
    down = [(i + 1, i) for i in range(n_y - 1)]
    return lax.ppermute(last, "gy", up), lax.ppermute(first, "gy", down)


def per_device(control, innovation, obs_weight, courant_x, courant_y, filter_x, filter_y):
    rows, levels, width = control.shape
    n_x = lax.axis_size("gx")
    parts = n_x // levels
    part = width // parts
    cut, piece = rows // CHUNKS, part // CHUNKS
    spans = [slice(w * piece, (w + 1) * piece) for w in range(CHUNKS)]

    rows_y = filter_rows(filter_y, parts)
    matrix_x = [lax.all_gather(filter_x[:cut], "gx", axis=0, tiled=True)]
    lines = [swap_all(as_lines(control, parts, w)) for w in range(CHUNKS)]
    lines = [l.reshape(n_x * rows, piece) for l in lines]
    lines[-1], filter_x = lax.optimization_barrier((lines[-1], filter_x))
    for h in range(1, CHUNKS):
        share = filter_x[h * cut : (h + 1) * cut]
        matrix_x.append(lax.all_gather(share, "gx", axis=0, tiled=True))
    starts = []
    for h in range(CHUNKS):
        start = 0.0
        for w, span in enumerate(spans):
            smoothed = jnp.dot(matrix_x[h], lines[w], preferred_element_type=F32)
            smoothed = smoothed.astype(BF16).reshape(n_x, cut, piece)
            for plane, matrix in zip(plane_pieces(smoothed, parts), rows_y):
                start = start + jnp.einsum(
                    "brc,kc->brk", plane, matrix[:, span], preferred_element_type=F32
                )
        came = swap_all(start.astype(BF16)).reshape(levels, parts, cut, part)
        came = came.transpose(2, 0, 1, 3).reshape(cut, levels, width)
        if h == 0:
            came, filter_y = lax.optimization_barrier((came, filter_y))
            columns_y = filter_columns(filter_y, parts)
        starts.append(came)

    rows_in = row_halo(starts[0][0], starts[-1][-1]).astype(F32)
    before, after = side_halo(
        jnp.concatenate([s[:, :, 0] for s in starts]),
        jnp.concatenate([s[:, :, -1] for s in starts]),
    )
    sides = jnp.stack([before, after], axis=2).astype(F32)
    end_state, flat, row_flux, side_flux = forward(
        starts, rows_in, sides, innovation, obs_weight, courant_x, courant_y
    )
    rows_in = row_halo(row_flux[0], row_flux[1])
    before, after = side_halo(side_flux[:, :, 0], side_flux[:, :, 1])
    sides = jnp.stack([before, after], axis=2)
    flat, columns_y = lax.optimization_barrier((flat, columns_y))

    pulled = []
    for w in range(CHUNKS):
        adjoint = swap_all(rim_lines(flat, rows_in, sides, parts, w))
        adjoint = adjoint.reshape(n_x, CHUNKS, cut, piece)
        total = 0.0
        for h in range(CHUNKS):
            total = total + jnp.einsum(
                "ij,ic->jc",
                matrix_x[h],
                adjoint[:, h].reshape(n_x * cut, piece),
                preferred_element_type=F32,
            )
        pulled.append(total.astype(BF16).reshape(n_x, CHUNKS, cut, piece))
    gradient = None
    for h in range(CHUNKS):
        carried = 0.0
        for w, span in enumerate(spans):
            for plane, matrix in zip(plane_pieces(pulled[w][:, h], parts), columns_y):
                carried = carried + jnp.einsum(
                    "brk,kc->brc", plane, matrix[span], preferred_element_type=F32
                )
        carried = swap_all(carried.astype(BF16))
        gradient = add_lines(control, carried, parts, h, gradient)
    return (end_state, gradient)


def solution(mesh):
    placed = (
        P("gx", None, "gy"),
        P("gx", None, "gy"),
        P("gx", None, "gy"),
        P("gx", None, "gy"),
        P("gx", None, "gy"),
        P("gx", None),
        P("gy", None),
    )
    return jax.shard_map(
        per_device,
        mesh=mesh,
        in_specs=placed,
        out_specs=(P("gx", None, "gy"), P("gx", None, "gy")),
        check_vma=False,
    )
```

```python
import functools

import jax
import jax.numpy as jnp
from jax import lax
from jax.experimental import pallas as pl
from jax.experimental.pallas import tpu as pltpu
from jax.sharding import PartitionSpec as P

BF16 = jnp.bfloat16
F32 = jnp.float32
STEP = 32
GROUP = 4
CHUNKS = 2
PARAMS = pltpu.CompilerParams(vmem_limit_bytes=56 * 1024 * 1024)


def cost(flops, *arrays):
    return pl.CostEstimate(
        flops=flops,
        bytes_accessed=sum(a.size * a.dtype.itemsize for a in arrays),
        transcendentals=0,
    )


def chunk_spans(width, parts, chunk):
    part = width // parts
    piece = part // CHUNKS
    return [
        slice(s * part + chunk * piece, s * part + (chunk + 1) * piece)
        for s in range(parts)
    ]


def store_lines(turned, out, parts):
    piece = out.shape[2]
    for l in range(turned.shape[1]):
        for s in range(parts):
            got = turned[:, l, s * piece : (s + 1) * piece]
            out[l * parts + s] = got.astype(BF16)


def lines_body(parts, chunk, block, out, turned):
    piece = out.shape[2]
    for s, span in enumerate(chunk_spans(block.shape[2], parts, chunk)):
        turned[:, :, s * piece : (s + 1) * piece] = block[:, :, span].astype(F32)
    store_lines(turned, out, parts)


def as_lines(block, parts, chunk):
    rows, levels, width = block.shape
    shape = (levels * parts, rows, width // parts // CHUNKS)
    return pl.pallas_call(
        functools.partial(lines_body, parts, chunk),
        grid=(rows // STEP,),
        in_specs=[pl.BlockSpec((STEP, levels, width), lambda i: (i, 0, 0))],
        out_specs=pl.BlockSpec((shape[0], STEP, shape[2]), lambda i: (0, i, 0)),
        out_shape=jax.ShapeDtypeStruct(shape, BF16),
        scratch_shapes=[pltpu.VMEM((STEP, levels, width // CHUNKS), F32)],
        compiler_params=PARAMS,
        cost_estimate=cost(0, block, block),
        name="as_lines",
    )(block)


def gradient_body(parts, lines, control, *rest):
    out, turned = rest[-2:]
    levels, width = control.shape[1:]
    part = width // parts
    for l in range(levels):
        for s in range(parts):
            turned[:, l, s * part : (s + 1) * part] = lines[l * parts + s].astype(F32)
    out[...] = control[...].astype(F32) + turned[...]


def add_lines(control, lines, parts, chunk, target):
    rows, levels, width = control.shape
    whole = (STEP, levels, width)
    cut = rows // CHUNKS
    offset = chunk * cut // STEP
    operands = [lines, control] + ([] if target is None else [target])
    return pl.pallas_call(
        functools.partial(gradient_body, parts),
        grid=(cut // STEP,),
        in_specs=[
            pl.BlockSpec((lines.shape[0], STEP, lines.shape[2]), lambda i: (0, i, 0)),
            pl.BlockSpec(whole, lambda i: (i + offset, 0, 0)),
        ]
        + [pl.BlockSpec(memory_space=pl.ANY)] * (len(operands) - 2),
        out_specs=pl.BlockSpec(whole, lambda i: (i + offset, 0, 0)),
        out_shape=jax.ShapeDtypeStruct(control.shape, F32),
        input_output_aliases={} if target is None else {2: 0},
        scratch_shapes=[pltpu.VMEM(whole, F32)],
        compiler_params=PARAMS,
        cost_estimate=cost(control.size // 2, control, control),
        name="add_lines",
    )(*operands)


def forward_body(*refs):
    starts = refs[:CHUNKS]
    rows_in, sides, innovation, weight, wind_x, wind_y = refs[CHUNKS : CHUNKS + 6]
    end, flat, row_flux, side_flux, state, carry = refs[CHUNKS + 6 :]
    step = pl.program_id(0)
    rows, levels, width = flat.shape
    cut = rows // CHUNKS

    @pl.when(step == 0)
    def _():
        state[pl.ds(0, 1)] = rows_in[pl.ds(0, 1)]
        state[pl.ds(rows + 1, 1)] = rows_in[pl.ds(1, 1)]
        for h in range(CHUNKS):
            state[pl.ds(1 + h * cut, cut)] = starts[h][...].astype(F32)
        carry[...] = jnp.zeros(carry.shape, F32)

    first = step * STEP
    place = lax.broadcasted_iota(jnp.int32, (GROUP, levels, width), 2)
    left_edge, right_edge = place == 0, place == width - 1
    for j in range(0, STEP, GROUP):
        rows_j, at = pl.ds(j, GROUP), first + j
        here = state[pl.ds(at + 1, GROUP)]
        cx, cy = wind_x[rows_j], wind_y[rows_j]
        left = jnp.where(left_edge, sides[rows_j, :, 0:1], pltpu.roll(here, 1, 2))
        right = jnp.where(
            right_edge, sides[rows_j, :, 1:2], pltpu.roll(here, width - 1, 2)
        )
        dx = state[pl.ds(at + 2, GROUP)] - state[pl.ds(at, GROUP)]
        after = here - cx * dx * 0.5 - cy * (right - left) * 0.5
        end[rows_j] = after
        misfit = weight[rows_j] * (after - innovation[rows_j])
        p, q = cy * misfit, cx * misfit
        side_flux[rows_j, :, 0:1] = p[:, :, 0:1]
        side_flux[rows_j, :, 1:2] = p[:, :, width - 1 : width]
        left = jnp.where(left_edge, 0.0, pltpu.roll(p, 1, 2))
        right = jnp.where(right_edge, 0.0, pltpu.roll(p, width - 1, 2))
        flat_j = misfit + 0.5 * (right - left)
        flat[jnp.maximum(at - 1, 0)] = carry[2] + 0.5 * (q[0] - carry[0])
        flat[at] = flat_j[0] + 0.5 * (q[1] - carry[1])
        flat[pl.ds(at + 1, GROUP - 2)] = flat_j[1:-1] + 0.5 * (q[2:] - q[:-2])
        if j == 0:
            carry[3] = q[0]
        carry[0], carry[1], carry[2] = q[GROUP - 2], q[GROUP - 1], flat_j[GROUP - 1]

    @pl.when(step == 0)
    def _():
        row_flux[0] = carry[3]

    @pl.when(step == rows // STEP - 1)
    def _():
        flat[rows - 1] = carry[2] - 0.5 * carry[0]
        row_flux[1] = carry[1]


def forward(starts, rows_in, sides, innovation, weight, wind_x, wind_y):
    rows, levels, width = innovation.shape
    blocked = pl.BlockSpec((STEP, levels, width), lambda i: (i, 0, 0))
    side = pl.BlockSpec((STEP, levels, 2), lambda i: (i, 0, 0))
    pair = pl.BlockSpec((2, levels, width), lambda i: (0, 0, 0))
    start = pl.BlockSpec(starts[0].shape, lambda i: (0, 0, 0))
    whole = pl.BlockSpec((rows, levels, width), lambda i: (0, 0, 0))
    return pl.pallas_call(
        forward_body,
        grid=(rows // STEP,),
        in_specs=[start] * CHUNKS + [pair, side, blocked, blocked, blocked, blocked],
        out_specs=[blocked, whole, pair, side],
        out_shape=[
            jax.ShapeDtypeStruct((rows, levels, width), F32),
            jax.ShapeDtypeStruct((rows, levels, width), F32),
            jax.ShapeDtypeStruct((2, levels, width), F32),
            jax.ShapeDtypeStruct((rows, levels, 2), F32),
        ],
        scratch_shapes=[
            pltpu.VMEM((rows + 2, levels, width), F32),
            pltpu.VMEM((4, levels, width), F32),
        ],
        compiler_params=PARAMS,
        cost_estimate=cost(30 * innovation.size, *[innovation] * 7),
        name="forward",
    )(*starts, rows_in, sides, innovation, weight, wind_x, wind_y)


def rim_body(parts, chunk, last, flat, rows_in, sides, out, turned):
    step = pl.program_id(0)
    levels, width = flat.shape[1:]
    piece = out.shape[2]
    place = lax.broadcasted_iota(jnp.int32, (STEP, levels, piece), 2)
    spans = chunk_spans(width, parts, chunk)
    for s, span in enumerate(spans):
        value = flat[:, :, span]
        if span.start == 0:
            value = value - jnp.where(place == 0, 0.5 * sides[:, :, 0:1], 0.0)
        if span.stop == width:
            value = value + jnp.where(place == piece - 1, 0.5 * sides[:, :, 1:2], 0.0)
        turned[:, :, s * piece : (s + 1) * piece] = value

    @pl.when(step == 0)
    def _():
        for s, span in enumerate(spans):
            at = slice(s * piece, (s + 1) * piece)
            turned[0, :, at] += -0.5 * rows_in[0, :, span]

    @pl.when(step == last)
    def _():
        for s, span in enumerate(spans):
            at = slice(s * piece, (s + 1) * piece)
            turned[STEP - 1, :, at] += 0.5 * rows_in[1, :, span]

    store_lines(turned, out, parts)


def rim_lines(flat, rows_in, sides, parts, chunk):
    rows, levels, width = flat.shape
    shape = (levels * parts, rows, width // parts // CHUNKS)
    return pl.pallas_call(
        functools.partial(rim_body, parts, chunk, rows // STEP - 1),
        grid=(rows // STEP,),
        in_specs=[
            pl.BlockSpec((STEP, levels, width), lambda i: (i, 0, 0)),
            pl.BlockSpec((2, levels, width), lambda i: (0, 0, 0)),
            pl.BlockSpec((STEP, levels, 2), lambda i: (i, 0, 0)),
        ],
        out_specs=pl.BlockSpec((shape[0], STEP, shape[2]), lambda i: (0, i, 0)),
        out_shape=jax.ShapeDtypeStruct(shape, BF16),
        scratch_shapes=[pltpu.VMEM((STEP, levels, width // CHUNKS), F32)],
        compiler_params=PARAMS,
        cost_estimate=cost(4 * flat.size, flat, flat),
        name="rim_lines",
    )(flat, rows_in, sides)


def swap_all(lines):
    return lax.all_to_all(lines, "gx", 0, 0, tiled=True)


def plane_pieces(lines, parts):
    n_x, n_y = lax.axis_size("gx"), lax.axis_size("gy")
    groups = [list(range(i, i + parts)) for i in range(0, n_x, parts)]
    if n_y == 2 and parts == 2:
        pairs = [(a, b) for g in groups for a, b in (g, g[::-1])]
        far = lax.ppermute(lines, "gy", [(0, 1), (1, 0)])
        near = lax.ppermute(lines, "gx", pairs)
        cross = lax.ppermute(far, "gx", pairs)
        return [lines, near, far, cross]
    plane = lax.all_gather(lines, "gy", axis=0, tiled=False)
    plane = lax.all_gather(plane, "gx", axis=0, tiled=False, axis_index_groups=groups)
    return [plane[s, g] for s in range(parts) for g in range(n_y)]


def piece_order(parts):
    n_y = lax.axis_size("gy")
    sub, me = lax.rem(lax.axis_index("gx"), parts), lax.axis_index("gy")
    if n_y == 2 and parts == 2:
        return [(sub, me), (1 - sub, me), (sub, 1 - me), (1 - sub, 1 - me)]
    return [(s, g) for s in range(parts) for g in range(n_y)]


def filter_rows(filter_y, parts):
    width = filter_y.shape[0]
    part = width // parts
    sub = lax.rem(lax.axis_index("gx"), parts)
    return [
        lax.dynamic_slice(filter_y, (sub * part, g * width + s * part), (part, part))
        for s, g in piece_order(parts)
    ]


def filter_columns(filter_y, parts):
    width, n_y = filter_y.shape[0], lax.axis_size("gy")
    part = width // parts
    sub, me = lax.rem(lax.axis_index("gx"), parts), lax.axis_index("gy")
    order = piece_order(parts)
    if n_y == 2 and parts == 2:
        mine = lax.dynamic_slice(filter_y, (0, me * width + sub * part), (width, part))
        sent = lax.dynamic_slice(
            filter_y, (0, (1 - me) * width + sub * part), (width, part)
        )
        got = lax.ppermute(sent, "gy", [(0, 1), (1, 0)])
        return [
            lax.dynamic_slice_in_dim(source, s * part, part, axis=0)
            for source, (s, _) in zip((mine, mine, got, got), order)
        ]
    split = filter_y.reshape(width, n_y, parts, part)
    split = lax.dynamic_index_in_dim(split, sub, axis=2, keepdims=False)
    split = lax.all_to_all(split, "gy", 1, 0, tiled=True)
    split = split.reshape(n_y, parts, part, part)
    return [split[g, s] for s, g in order]


def row_halo(first, last):
    n_x = lax.axis_size("gx")
    up = [(i, i + 1) for i in range(n_x - 1)]
    down = [(i + 1, i) for i in range(n_x - 1)]
    return jnp.stack([lax.ppermute(last, "gx", up), lax.ppermute(first, "gx", down)])


def side_halo(first, last):
    n_y, me = lax.axis_size("gy"), lax.axis_index("gy")
    if n_y == 2:
        got = lax.ppermute(jnp.where(me == 0, last, first), "gy", [(0, 1), (1, 0)])
        none = jnp.zeros_like(got)
        return jnp.where(me == 0, none, got), jnp.where(me == 0, got, none)
    up = [(i, i + 1) for i in range(n_y - 1)]
    down = [(i + 1, i) for i in range(n_y - 1)]
    return lax.ppermute(last, "gy", up), lax.ppermute(first, "gy", down)


def per_device(control, innovation, obs_weight, courant_x, courant_y, filter_x, filter_y):
    rows, levels, width = control.shape
    n_x = lax.axis_size("gx")
    parts = n_x // levels
    part = width // parts
    cut, piece = rows // CHUNKS, part // CHUNKS
    spans = [slice(w * piece, (w + 1) * piece) for w in range(CHUNKS)]

    rows_y = filter_rows(filter_y, parts)
    matrix_x = [lax.all_gather(filter_x[:cut], "gx", axis=0, tiled=True)]
    lines = [swap_all(as_lines(control, parts, w)) for w in range(CHUNKS)]
    lines = [l.reshape(n_x * rows, piece) for l in lines]
    lines[-1], filter_x = lax.optimization_barrier((lines[-1], filter_x))
    for h in range(1, CHUNKS):
        share = filter_x[h * cut : (h + 1) * cut]
        matrix_x.append(lax.all_gather(share, "gx", axis=0, tiled=True))
    starts = []
    for h in range(CHUNKS):
        start = 0.0
        for w, span in enumerate(spans):
            smoothed = jnp.dot(matrix_x[h], lines[w], preferred_element_type=F32)
            smoothed = smoothed.astype(BF16).reshape(n_x, cut, piece)
            for plane, matrix in zip(plane_pieces(smoothed, parts), rows_y):
                start = start + jnp.einsum(
                    "brc,kc->brk", plane, matrix[:, span], preferred_element_type=F32
                )
        start = start.astype(BF16)
        if h == CHUNKS - 1:
            start, filter_y = lax.optimization_barrier((start, filter_y))
            columns_y = filter_columns(filter_y, parts)
        came = swap_all(start).reshape(levels, parts, cut, part)
        came = came.transpose(2, 0, 1, 3).reshape(cut, levels, width)
        starts.append(came)

    rows_in = row_halo(starts[0][0], starts[-1][-1]).astype(F32)
    before, after = side_halo(
        jnp.concatenate([s[:, :, 0] for s in starts]),
        jnp.concatenate([s[:, :, -1] for s in starts]),
    )
    sides = jnp.stack([before, after], axis=2).astype(F32)
    end_state, flat, row_flux, side_flux = forward(
        starts, rows_in, sides, innovation, obs_weight, courant_x, courant_y
    )
    rows_in = row_halo(row_flux[0], row_flux[1])
    before, after = side_halo(side_flux[:, :, 0], side_flux[:, :, 1])
    sides = jnp.stack([before, after], axis=2)
    flat, columns_y = lax.optimization_barrier((flat, columns_y))

    pulled = []
    for w in range(CHUNKS):
        adjoint = swap_all(rim_lines(flat, rows_in, sides, parts, w))
        adjoint = adjoint.reshape(n_x, CHUNKS, cut, piece)
        total = 0.0
        for h in range(CHUNKS):
            total = total + jnp.einsum(
                "ij,ic->jc",
                matrix_x[h],
                adjoint[:, h].reshape(n_x * cut, piece),
                preferred_element_type=F32,
            )
        pulled.append(total.astype(BF16).reshape(n_x, CHUNKS, cut, piece))
    gradient = None
    for h in range(CHUNKS):
        carried = 0.0
        for w, span in enumerate(spans):
            for plane, matrix in zip(plane_pieces(pulled[w][:, h], parts), columns_y):
                carried = carried + jnp.einsum(
                    "brk,kc->brc", plane, matrix[span], preferred_element_type=F32
                )
        carried = swap_all(carried.astype(BF16))
        gradient = add_lines(control, carried, parts, h, gradient)
    return (end_state, gradient)


def solution(mesh):
    placed = (
        P("gx", None, "gy"),
        P("gx", None, "gy"),
        P("gx", None, "gy"),
        P("gx", None, "gy"),
        P("gx", None, "gy"),
        P("gx", None),
        P("gy", None),
    )
    return jax.shard_map(
        per_device,
        mesh=mesh,
        in_specs=placed,
        out_specs=(P("gx", None, "gy"), P("gx", None, "gy")),
        check_vma=False,
    )
```

```python
import functools

import jax
import jax.numpy as jnp
from jax import lax
from jax.experimental import pallas as pl
from jax.experimental.pallas import tpu as pltpu
from jax.sharding import PartitionSpec as P

BF16 = jnp.bfloat16
F32 = jnp.float32
STEP = 32
GROUP = 4
CHUNKS = 2
PARAMS = pltpu.CompilerParams(vmem_limit_bytes=56 * 1024 * 1024)


def cost(flops, *arrays):
    return pl.CostEstimate(
        flops=flops,
        bytes_accessed=sum(a.size * a.dtype.itemsize for a in arrays),
        transcendentals=0,
    )


def chunk_spans(width, parts, chunk):
    part = width // parts
    piece = part // CHUNKS
    return [
        slice(s * part + chunk * piece, s * part + (chunk + 1) * piece)
        for s in range(parts)
    ]


def store_lines(turned, out, parts):
    piece = out.shape[2]
    for l in range(turned.shape[1]):
        for s in range(parts):
            got = turned[:, l, s * piece : (s + 1) * piece]
            out[l * parts + s] = got.astype(BF16)


def lines_body(parts, chunk, block, out, turned):
    piece = out.shape[2]
    for s, span in enumerate(chunk_spans(block.shape[2], parts, chunk)):
        turned[:, :, s * piece : (s + 1) * piece] = block[:, :, span].astype(F32)
    store_lines(turned, out, parts)


def as_lines(block, parts, chunk):
    rows, levels, width = block.shape
    shape = (levels * parts, rows, width // parts // CHUNKS)
    return pl.pallas_call(
        functools.partial(lines_body, parts, chunk),
        grid=(rows // STEP,),
        in_specs=[pl.BlockSpec((STEP, levels, width), lambda i: (i, 0, 0))],
        out_specs=pl.BlockSpec((shape[0], STEP, shape[2]), lambda i: (0, i, 0)),
        out_shape=jax.ShapeDtypeStruct(shape, BF16),
        scratch_shapes=[pltpu.VMEM((STEP, levels, width // CHUNKS), F32)],
        compiler_params=PARAMS,
        cost_estimate=cost(0, block, block),
        name="as_lines",
    )(block)


def gradient_body(parts, lines, control, *rest):
    out, turned = rest[-2:]
    levels, width = control.shape[1:]
    part = width // parts
    for l in range(levels):
        for s in range(parts):
            turned[:, l, s * part : (s + 1) * part] = lines[l * parts + s].astype(F32)
    out[...] = control[...].astype(F32) + turned[...]


def add_lines(control, lines, parts, chunk, target):
    rows, levels, width = control.shape
    whole = (STEP, levels, width)
    cut = rows // CHUNKS
    offset = chunk * cut // STEP
    operands = [lines, control] + ([] if target is None else [target])
    return pl.pallas_call(
        functools.partial(gradient_body, parts),
        grid=(cut // STEP,),
        in_specs=[
            pl.BlockSpec((lines.shape[0], STEP, lines.shape[2]), lambda i: (0, i, 0)),
            pl.BlockSpec(whole, lambda i: (i + offset, 0, 0)),
        ]
        + [pl.BlockSpec(memory_space=pl.ANY)] * (len(operands) - 2),
        out_specs=pl.BlockSpec(whole, lambda i: (i + offset, 0, 0)),
        out_shape=jax.ShapeDtypeStruct(control.shape, F32),
        input_output_aliases={} if target is None else {2: 0},
        scratch_shapes=[pltpu.VMEM(whole, F32)],
        compiler_params=PARAMS,
        cost_estimate=cost(control.size // 2, control, control),
        name="add_lines",
    )(*operands)


def forward_body(*refs):
    starts = refs[:CHUNKS]
    rows_in, sides, innovation, weight, wind_x, wind_y = refs[CHUNKS : CHUNKS + 6]
    end, flat, state, carry = refs[CHUNKS + 6 :]
    step = pl.program_id(0)
    rows, levels, width = flat.shape
    cut = rows // CHUNKS

    @pl.when(step == 0)
    def _():
        state[pl.ds(0, 1)] = rows_in[pl.ds(0, 1)]
        state[pl.ds(rows + 1, 1)] = rows_in[pl.ds(1, 1)]
        for h in range(CHUNKS):
            state[pl.ds(1 + h * cut, cut)] = starts[h][...].astype(F32)
        carry[...] = jnp.zeros(carry.shape, F32)

    first = step * STEP
    place = lax.broadcasted_iota(jnp.int32, (GROUP, levels, width), 2)
    left_edge, right_edge = place == 0, place == width - 1
    for j in range(0, STEP, GROUP):
        rows_j, at = pl.ds(j, GROUP), first + j
        here = state[pl.ds(at + 1, GROUP)]
        cx, cy = wind_x[rows_j], wind_y[rows_j]
        left = jnp.where(left_edge, sides[rows_j, :, 0:1], pltpu.roll(here, 1, 2))
        right = jnp.where(
            right_edge, sides[rows_j, :, 1:2], pltpu.roll(here, width - 1, 2)
        )
        dx = state[pl.ds(at + 2, GROUP)] - state[pl.ds(at, GROUP)]
        after = here - cx * dx * 0.5 - cy * (right - left) * 0.5
        end[rows_j] = after
        misfit = weight[rows_j] * (after - innovation[rows_j])
        p, q = cy * misfit, cx * misfit
        left = jnp.where(left_edge, 0.0, pltpu.roll(p, 1, 2))
        right = jnp.where(right_edge, 0.0, pltpu.roll(p, width - 1, 2))
        flat_j = misfit + 0.5 * (right - left)
        flat[jnp.maximum(at - 1, 0)] = carry[2] + 0.5 * (q[0] - carry[0])
        flat[at] = flat_j[0] + 0.5 * (q[1] - carry[1])
        flat[pl.ds(at + 1, GROUP - 2)] = flat_j[1:-1] + 0.5 * (q[2:] - q[:-2])
        carry[0], carry[1], carry[2] = q[GROUP - 2], q[GROUP - 1], flat_j[GROUP - 1]

    @pl.when(step == rows // STEP - 1)
    def _():
        flat[rows - 1] = carry[2] - 0.5 * carry[0]


def forward(starts, rows_in, sides, innovation, weight, wind_x, wind_y):
    rows, levels, width = innovation.shape
    blocked = pl.BlockSpec((STEP, levels, width), lambda i: (i, 0, 0))
    side = pl.BlockSpec((STEP, levels, 2), lambda i: (i, 0, 0))
    pair = pl.BlockSpec((2, levels, width), lambda i: (0, 0, 0))
    start = pl.BlockSpec(starts[0].shape, lambda i: (0, 0, 0))
    whole = pl.BlockSpec((rows, levels, width), lambda i: (0, 0, 0))
    return pl.pallas_call(
        forward_body,
        grid=(rows // STEP,),
        in_specs=[start] * CHUNKS + [pair, side, blocked, blocked, blocked, blocked],
        out_specs=[blocked, whole],
        out_shape=[
            jax.ShapeDtypeStruct((rows, levels, width), F32),
            jax.ShapeDtypeStruct((rows, levels, width), F32),
        ],
        scratch_shapes=[
            pltpu.VMEM((rows + 2, levels, width), F32),
            pltpu.VMEM((3, levels, width), F32),
        ],
        compiler_params=PARAMS,
        cost_estimate=cost(30 * innovation.size, *[innovation] * 7),
        name="forward",
    )(*starts, rows_in, sides, innovation, weight, wind_x, wind_y)


def rim_body(parts, chunk, last, flat, rows_in, sides, out, turned):
    step = pl.program_id(0)
    levels, width = flat.shape[1:]
    piece = out.shape[2]
    place = lax.broadcasted_iota(jnp.int32, (STEP, levels, piece), 2)
    spans = chunk_spans(width, parts, chunk)
    for s, span in enumerate(spans):
        value = flat[:, :, span]
        if span.start == 0:
            value = value - jnp.where(place == 0, 0.5 * sides[:, :, 0:1], 0.0)
        if span.stop == width:
            value = value + jnp.where(place == piece - 1, 0.5 * sides[:, :, 1:2], 0.0)
        turned[:, :, s * piece : (s + 1) * piece] = value

    @pl.when(step == 0)
    def _():
        for s, span in enumerate(spans):
            at = slice(s * piece, (s + 1) * piece)
            turned[0, :, at] += -0.5 * rows_in[0, :, span]

    @pl.when(step == last)
    def _():
        for s, span in enumerate(spans):
            at = slice(s * piece, (s + 1) * piece)
            turned[STEP - 1, :, at] += 0.5 * rows_in[1, :, span]

    store_lines(turned, out, parts)


def rim_lines(flat, rows_in, sides, parts, chunk):
    rows, levels, width = flat.shape
    shape = (levels * parts, rows, width // parts // CHUNKS)
    return pl.pallas_call(
        functools.partial(rim_body, parts, chunk, rows // STEP - 1),
        grid=(rows // STEP,),
        in_specs=[
            pl.BlockSpec((STEP, levels, width), lambda i: (i, 0, 0)),
            pl.BlockSpec((2, levels, width), lambda i: (0, 0, 0)),
            pl.BlockSpec((STEP, levels, 2), lambda i: (i, 0, 0)),
        ],
        out_specs=pl.BlockSpec((shape[0], STEP, shape[2]), lambda i: (0, i, 0)),
        out_shape=jax.ShapeDtypeStruct(shape, BF16),
        scratch_shapes=[pltpu.VMEM((STEP, levels, width // CHUNKS), F32)],
        compiler_params=PARAMS,
        cost_estimate=cost(4 * flat.size, flat, flat),
        name="rim_lines",
    )(flat, rows_in, sides)


def swap_all(lines):
    return lax.all_to_all(lines, "gx", 0, 0, tiled=True)


def plane_pieces(lines, parts, after=None):
    n_x, n_y = lax.axis_size("gx"), lax.axis_size("gy")
    groups = [list(range(i, i + parts)) for i in range(0, n_x, parts)]
    if n_y == 2 and parts == 2:
        pairs = [(a, b) for g in groups for a, b in (g, g[::-1])]
        sent = lines if after is None else lax.optimization_barrier((lines, after))[0]
        far = lax.ppermute(sent, "gy", [(0, 1), (1, 0)])
        near = lax.ppermute(lines, "gx", pairs)
        cross = lax.ppermute(far, "gx", pairs)
        return [lines, near, far, cross]
    plane = lax.all_gather(lines, "gy", axis=0, tiled=False)
    plane = lax.all_gather(plane, "gx", axis=0, tiled=False, axis_index_groups=groups)
    return [plane[s, g] for s in range(parts) for g in range(n_y)]


def piece_order(parts):
    n_y = lax.axis_size("gy")
    sub, me = lax.rem(lax.axis_index("gx"), parts), lax.axis_index("gy")
    if n_y == 2 and parts == 2:
        return [(sub, me), (1 - sub, me), (sub, 1 - me), (1 - sub, 1 - me)]
    return [(s, g) for s in range(parts) for g in range(n_y)]


def filter_rows(filter_y, parts):
    width = filter_y.shape[0]
    part = width // parts
    sub = lax.rem(lax.axis_index("gx"), parts)
    return [
        lax.dynamic_slice(filter_y, (sub * part, g * width + s * part), (part, part))
        for s, g in piece_order(parts)
    ]


def send_columns(filter_y, parts):
    width, n_y = filter_y.shape[0], lax.axis_size("gy")
    part = width // parts
    sub, me = lax.rem(lax.axis_index("gx"), parts), lax.axis_index("gy")
    if n_y == 2 and parts == 2:
        sent = lax.dynamic_slice(
            filter_y, (0, (1 - me) * width + sub * part), (width, part)
        )
        return lax.ppermute(sent, "gy", [(0, 1), (1, 0)])
    split = filter_y.reshape(width, n_y, parts, part)
    split = lax.dynamic_index_in_dim(split, sub, axis=2, keepdims=False)
    return lax.all_to_all(split, "gy", 1, 0, tiled=True)


def filter_columns(filter_y, got, parts):
    width, n_y = filter_y.shape[0], lax.axis_size("gy")
    part = width // parts
    sub, me = lax.rem(lax.axis_index("gx"), parts), lax.axis_index("gy")
    order = piece_order(parts)
    if n_y == 2 and parts == 2:
        mine = lax.dynamic_slice(filter_y, (0, me * width + sub * part), (width, part))
        return [
            lax.dynamic_slice_in_dim(source, s * part, part, axis=0)
            for source, (s, _) in zip((mine, mine, got, got), order)
        ]
    split = got.reshape(n_y, parts, part, part)
    return [split[g, s] for s, g in order]


def row_halo(first, last):
    n_x = lax.axis_size("gx")
    up = [(i, i + 1) for i in range(n_x - 1)]
    down = [(i + 1, i) for i in range(n_x - 1)]
    return jnp.stack([lax.ppermute(last, "gx", up), lax.ppermute(first, "gx", down)])


def side_halo(first, last):
    n_y, me = lax.axis_size("gy"), lax.axis_index("gy")
    if n_y == 2:
        got = lax.ppermute(jnp.where(me == 0, last, first), "gy", [(0, 1), (1, 0)])
        none = jnp.zeros_like(got)
        return jnp.where(me == 0, none, got), jnp.where(me == 0, got, none)
    up = [(i, i + 1) for i in range(n_y - 1)]
    down = [(i + 1, i) for i in range(n_y - 1)]
    return lax.ppermute(last, "gy", up), lax.ppermute(first, "gy", down)


def edge_flux(starts, rows_in, before, after, fields):
    def flux(up, here, down, left, right, fields, wind):
        innovation, weight, cx, cy = fields
        end = here - cx * (down - up) * 0.5 - cy * (right - left) * 0.5
        return fields[wind] * (weight * (end - innovation))

    top = starts[0][:2].astype(F32)
    bottom = starts[-1][-2:].astype(F32)
    here = jnp.stack([top[0], bottom[1]])
    ends = jnp.stack([before[0], before[-1]]), jnp.stack([after[0], after[-1]])
    row_flux = flux(
        jnp.stack([rows_in[0], bottom[0]]),
        here,
        jnp.stack([top[1], rows_in[1]]),
        jnp.concatenate([ends[0][:, :, None], here[:, :, :-1]], axis=2),
        jnp.concatenate([here[:, :, 1:], ends[1][:, :, None]], axis=2),
        [jnp.stack([f[0], f[-1]]) for f in fields],
        2,
    )
    side = [
        jnp.concatenate([s[:, :, at] for s in starts]).astype(F32)
        for at in (0, 1, -2, -1)
    ]
    here = jnp.stack([side[0], side[3]])
    halo = jnp.stack([rows_in[:, :, 0], rows_in[:, :, -1]])
    side_flux = flux(
        jnp.concatenate([halo[:, :1], here[:, :-1]], axis=1),
        here,
        jnp.concatenate([here[:, 1:], halo[:, 1:]], axis=1),
        jnp.stack([before, side[2]]),
        jnp.stack([side[1], after]),
        [jnp.stack([f[:, :, 0], f[:, :, -1]]) for f in fields],
        3,
    )
    return row_flux, side_flux


def per_device(control, innovation, obs_weight, courant_x, courant_y, filter_x, filter_y):
    rows, levels, width = control.shape
    n_x = lax.axis_size("gx")
    parts = n_x // levels
    part = width // parts
    cut, piece = rows // CHUNKS, part // CHUNKS
    spans = [slice(w * piece, (w + 1) * piece) for w in range(CHUNKS)]

    rows_y = filter_rows(filter_y, parts)
    matrix_x = [lax.all_gather(filter_x[:cut], "gx", axis=0, tiled=True)]
    lines = [swap_all(as_lines(control, parts, w)) for w in range(CHUNKS)]
    lines = [l.reshape(n_x * rows, piece) for l in lines]
    lines[-1], filter_x = lax.optimization_barrier((lines[-1], filter_x))
    for h in range(1, CHUNKS):
        share = filter_x[h * cut : (h + 1) * cut]
        matrix_x.append(lax.all_gather(share, "gx", axis=0, tiled=True))
    starts = []
    for h in range(CHUNKS):
        start = 0.0
        for w, span in enumerate(spans):
            smoothed = jnp.dot(matrix_x[h], lines[w], preferred_element_type=F32)
            smoothed = smoothed.astype(BF16).reshape(n_x, cut, piece)
            for plane, matrix in zip(plane_pieces(smoothed, parts), rows_y):
                start = start + jnp.einsum(
                    "brc,kc->brk", plane, matrix[:, span], preferred_element_type=F32
                )
        start = start.astype(BF16)
        if h == CHUNKS - 1:
            start, filter_y = lax.optimization_barrier((start, filter_y))
            columns_y = send_columns(filter_y, parts)
        came = swap_all(start).reshape(levels, parts, cut, part)
        came = came.transpose(2, 0, 1, 3).reshape(cut, levels, width)
        starts.append(came)

    rows_in = row_halo(starts[0][0], starts[-1][-1]).astype(F32)
    before, after = side_halo(
        jnp.concatenate([s[:, :, 0] for s in starts]),
        jnp.concatenate([s[:, :, -1] for s in starts]),
    )
    before, after = before.astype(F32), after.astype(F32)
    fields = (innovation, obs_weight, courant_x, courant_y)
    row_flux, side_flux = edge_flux(starts, rows_in, before, after, fields)
    end_state, flat = forward(
        starts, rows_in, jnp.stack([before, after], axis=2), *fields
    )
    rows_in = row_halo(row_flux[0], row_flux[1])
    sides = jnp.stack(side_halo(side_flux[0], side_flux[1]), axis=2)
    flat, columns_y = lax.optimization_barrier((flat, columns_y))
    columns_y = filter_columns(filter_y, columns_y, parts)

    pulled = []
    for w in range(CHUNKS):
        adjoint = swap_all(rim_lines(flat, rows_in, sides, parts, w))
        adjoint = adjoint.reshape(n_x, CHUNKS, cut, piece)
        total = 0.0
        for h in range(CHUNKS):
            total = total + jnp.einsum(
                "ij,ic->jc",
                matrix_x[h],
                adjoint[:, h].reshape(n_x * cut, piece),
                preferred_element_type=F32,
            )
        pulled.append(total.astype(BF16).reshape(n_x, CHUNKS, cut, piece))
    gradient = far = None
    for h in range(CHUNKS):
        carried = 0.0
        for w, span in enumerate(spans):
            held = far if h > 0 and w == CHUNKS - 1 else None
            planes = plane_pieces(pulled[w][:, h], parts, held)
            far = planes[-2] if w == CHUNKS - 1 else far
            for plane, matrix in zip(planes, columns_y):
                carried = carried + jnp.einsum(
                    "brk,kc->brc", plane, matrix[span], preferred_element_type=F32
                )
        carried = swap_all(carried.astype(BF16))
        gradient = add_lines(control, carried, parts, h, gradient)
    return (end_state, gradient)


def solution(mesh):
    placed = (
        P("gx", None, "gy"),
        P("gx", None, "gy"),
        P("gx", None, "gy"),
        P("gx", None, "gy"),
        P("gx", None, "gy"),
        P("gx", None),
        P("gy", None),
    )
    return jax.shard_map(
        per_device,
        mesh=mesh,
        in_specs=placed,
        out_specs=(P("gx", None, "gy"), P("gx", None, "gy")),
        check_vma=False,
    )
```

```python
import functools

import jax
import jax.numpy as jnp
from jax import lax
from jax.experimental import pallas as pl
from jax.experimental.pallas import tpu as pltpu
from jax.sharding import PartitionSpec as P

BF16 = jnp.bfloat16
F32 = jnp.float32
STEP = 32
GROUP = 8
CHUNKS = 2
PARAMS = pltpu.CompilerParams(vmem_limit_bytes=56 * 1024 * 1024)


def cost(flops, *arrays):
    return pl.CostEstimate(
        flops=flops,
        bytes_accessed=sum(a.size * a.dtype.itemsize for a in arrays),
        transcendentals=0,
    )


def chunk_spans(width, parts, chunk):
    part = width // parts
    piece = part // CHUNKS
    return [
        slice(s * part + chunk * piece, s * part + (chunk + 1) * piece)
        for s in range(parts)
    ]


def store_lines(turned, out, parts):
    piece = out.shape[2]
    for l in range(turned.shape[1]):
        for s in range(parts):
            got = turned[:, l, s * piece : (s + 1) * piece]
            out[l * parts + s] = got.astype(BF16)


def lines_body(parts, chunk, block, out, turned):
    piece = out.shape[2]
    for s, span in enumerate(chunk_spans(block.shape[2], parts, chunk)):
        turned[:, :, s * piece : (s + 1) * piece] = block[:, :, span].astype(F32)
    store_lines(turned, out, parts)


def as_lines(block, parts, chunk):
    rows, levels, width = block.shape
    shape = (levels * parts, rows, width // parts // CHUNKS)
    return pl.pallas_call(
        functools.partial(lines_body, parts, chunk),
        grid=(rows // STEP,),
        in_specs=[pl.BlockSpec((STEP, levels, width), lambda i: (i, 0, 0))],
        out_specs=pl.BlockSpec((shape[0], STEP, shape[2]), lambda i: (0, i, 0)),
        out_shape=jax.ShapeDtypeStruct(shape, BF16),
        scratch_shapes=[pltpu.VMEM((STEP, levels, width // CHUNKS), F32)],
        compiler_params=PARAMS,
        cost_estimate=cost(0, block, block),
        name="as_lines",
    )(block)


def gradient_body(parts, lines, control, *rest):
    out, turned = rest[-2:]
    levels, width = control.shape[1:]
    part = width // parts
    for l in range(levels):
        for s in range(parts):
            turned[:, l, s * part : (s + 1) * part] = lines[l * parts + s].astype(F32)
    out[...] = control[...].astype(F32) + turned[...]


def add_lines(control, lines, parts, chunk, target):
    rows, levels, width = control.shape
    whole = (STEP, levels, width)
    cut = rows // CHUNKS
    offset = chunk * cut // STEP
    operands = [lines, control] + ([] if target is None else [target])
    return pl.pallas_call(
        functools.partial(gradient_body, parts),
        grid=(cut // STEP,),
        in_specs=[
            pl.BlockSpec((lines.shape[0], STEP, lines.shape[2]), lambda i: (0, i, 0)),
            pl.BlockSpec(whole, lambda i: (i + offset, 0, 0)),
        ]
        + [pl.BlockSpec(memory_space=pl.ANY)] * (len(operands) - 2),
        out_specs=pl.BlockSpec(whole, lambda i: (i + offset, 0, 0)),
        out_shape=jax.ShapeDtypeStruct(control.shape, F32),
        input_output_aliases={} if target is None else {2: 0},
        scratch_shapes=[pltpu.VMEM(whole, F32)],
        compiler_params=PARAMS,
        cost_estimate=cost(control.size // 2, control, control),
        name="add_lines",
    )(*operands)


def forward_body(*refs):
    starts = refs[:CHUNKS]
    rows_in, sides, innovation, weight, wind_x, wind_y = refs[CHUNKS : CHUNKS + 6]
    end, flat, state, carry = refs[CHUNKS + 6 :]
    step = pl.program_id(0)
    rows, levels, width = flat.shape
    cut = rows // CHUNKS

    @pl.when(step == 0)
    def _():
        state[pl.ds(0, 1)] = rows_in[pl.ds(0, 1)]
        state[pl.ds(rows + 1, 1)] = rows_in[pl.ds(1, 1)]
        for h in range(CHUNKS):
            state[pl.ds(1 + h * cut, cut)] = starts[h][...].astype(F32)
        carry[...] = jnp.zeros(carry.shape, F32)

    first = step * STEP
    place = lax.broadcasted_iota(jnp.int32, (GROUP, levels, width), 2)
    left_edge, right_edge = place == 0, place == width - 1
    for j in range(0, STEP, GROUP):
        rows_j, at = pl.ds(j, GROUP), first + j
        here = state[pl.ds(at + 1, GROUP)]
        cx, cy = wind_x[rows_j], wind_y[rows_j]
        left = jnp.where(left_edge, sides[rows_j, :, 0:1], pltpu.roll(here, 1, 2))
        right = jnp.where(
            right_edge, sides[rows_j, :, 1:2], pltpu.roll(here, width - 1, 2)
        )
        dx = state[pl.ds(at + 2, GROUP)] - state[pl.ds(at, GROUP)]
        after = here - cx * dx * 0.5 - cy * (right - left) * 0.5
        end[rows_j] = after
        misfit = weight[rows_j] * (after - innovation[rows_j])
        p, q = cy * misfit, cx * misfit
        left = jnp.where(left_edge, 0.0, pltpu.roll(p, 1, 2))
        right = jnp.where(right_edge, 0.0, pltpu.roll(p, width - 1, 2))
        flat_j = misfit + 0.5 * (right - left)
        flat[jnp.maximum(at - 1, 0)] = carry[2] + 0.5 * (q[0] - carry[0])
        flat[at] = flat_j[0] + 0.5 * (q[1] - carry[1])
        flat[pl.ds(at + 1, GROUP - 2)] = flat_j[1:-1] + 0.5 * (q[2:] - q[:-2])
        carry[0], carry[1], carry[2] = q[GROUP - 2], q[GROUP - 1], flat_j[GROUP - 1]

    @pl.when(step == rows // STEP - 1)
    def _():
        flat[rows - 1] = carry[2] - 0.5 * carry[0]


def forward(starts, rows_in, sides, innovation, weight, wind_x, wind_y):
    rows, levels, width = innovation.shape
    blocked = pl.BlockSpec((STEP, levels, width), lambda i: (i, 0, 0))
    side = pl.BlockSpec((STEP, levels, 2), lambda i: (i, 0, 0))
    pair = pl.BlockSpec((2, levels, width), lambda i: (0, 0, 0))
    start = pl.BlockSpec(starts[0].shape, lambda i: (0, 0, 0))
    whole = pl.BlockSpec((rows, levels, width), lambda i: (0, 0, 0))
    return pl.pallas_call(
        forward_body,
        grid=(rows // STEP,),
        in_specs=[start] * CHUNKS + [pair, side, blocked, blocked, blocked, blocked],
        out_specs=[blocked, whole],
        out_shape=[
            jax.ShapeDtypeStruct((rows, levels, width), F32),
            jax.ShapeDtypeStruct((rows, levels, width), F32),
        ],
        scratch_shapes=[
            pltpu.VMEM((rows + 2, levels, width), F32),
            pltpu.VMEM((3, levels, width), F32),
        ],
        compiler_params=PARAMS,
        cost_estimate=cost(30 * innovation.size, *[innovation] * 7),
        name="forward",
    )(*starts, rows_in, sides, innovation, weight, wind_x, wind_y)


def rim_body(parts, chunk, last, flat, rows_in, sides, out, turned):
    step = pl.program_id(0)
    levels, width = flat.shape[1:]
    piece = out.shape[2]
    place = lax.broadcasted_iota(jnp.int32, (STEP, levels, piece), 2)
    spans = chunk_spans(width, parts, chunk)
    for s, span in enumerate(spans):
        value = flat[:, :, span]
        if span.start == 0:
            value = value - jnp.where(place == 0, 0.5 * sides[:, :, 0:1], 0.0)
        if span.stop == width:
            value = value + jnp.where(place == piece - 1, 0.5 * sides[:, :, 1:2], 0.0)
        turned[:, :, s * piece : (s + 1) * piece] = value

    @pl.when(step == 0)
    def _():
        for s, span in enumerate(spans):
            at = slice(s * piece, (s + 1) * piece)
            turned[0, :, at] += -0.5 * rows_in[0, :, span]

    @pl.when(step == last)
    def _():
        for s, span in enumerate(spans):
            at = slice(s * piece, (s + 1) * piece)
            turned[STEP - 1, :, at] += 0.5 * rows_in[1, :, span]

    store_lines(turned, out, parts)


def rim_lines(flat, rows_in, sides, parts, chunk):
    rows, levels, width = flat.shape
    shape = (levels * parts, rows, width // parts // CHUNKS)
    return pl.pallas_call(
        functools.partial(rim_body, parts, chunk, rows // STEP - 1),
        grid=(rows // STEP,),
        in_specs=[
            pl.BlockSpec((STEP, levels, width), lambda i: (i, 0, 0)),
            pl.BlockSpec((2, levels, width), lambda i: (0, 0, 0)),
            pl.BlockSpec((STEP, levels, 2), lambda i: (i, 0, 0)),
        ],
        out_specs=pl.BlockSpec((shape[0], STEP, shape[2]), lambda i: (0, i, 0)),
        out_shape=jax.ShapeDtypeStruct(shape, BF16),
        scratch_shapes=[pltpu.VMEM((STEP, levels, width // CHUNKS), F32)],
        compiler_params=PARAMS,
        cost_estimate=cost(4 * flat.size, flat, flat),
        name="rim_lines",
    )(flat, rows_in, sides)


def swap_all(lines):
    return lax.all_to_all(lines, "gx", 0, 0, tiled=True)


def plane_pieces(lines, parts, after=None):
    n_x, n_y = lax.axis_size("gx"), lax.axis_size("gy")
    groups = [list(range(i, i + parts)) for i in range(0, n_x, parts)]
    if n_y == 2 and parts == 2:
        pairs = [(a, b) for g in groups for a, b in (g, g[::-1])]
        sent = lines if after is None else lax.optimization_barrier((lines, after))[0]
        far = lax.ppermute(sent, "gy", [(0, 1), (1, 0)])
        near = lax.ppermute(lines, "gx", pairs)
        cross = lax.ppermute(far, "gx", pairs)
        return [lines, near, far, cross]
    plane = lax.all_gather(lines, "gy", axis=0, tiled=False)
    plane = lax.all_gather(plane, "gx", axis=0, tiled=False, axis_index_groups=groups)
    return [plane[s, g] for s in range(parts) for g in range(n_y)]


def piece_order(parts):
    n_y = lax.axis_size("gy")
    sub, me = lax.rem(lax.axis_index("gx"), parts), lax.axis_index("gy")
    if n_y == 2 and parts == 2:
        return [(sub, me), (1 - sub, me), (sub, 1 - me), (1 - sub, 1 - me)]
    return [(s, g) for s in range(parts) for g in range(n_y)]


def filter_rows(filter_y, parts):
    width = filter_y.shape[0]
    part = width // parts
    sub = lax.rem(lax.axis_index("gx"), parts)
    return [
        lax.dynamic_slice(filter_y, (sub * part, g * width + s * part), (part, part))
        for s, g in piece_order(parts)
    ]


def send_columns(filter_y, parts):
    width, n_y = filter_y.shape[0], lax.axis_size("gy")
    part = width // parts
    sub, me = lax.rem(lax.axis_index("gx"), parts), lax.axis_index("gy")
    if n_y == 2 and parts == 2:
        sent = lax.dynamic_slice(
            filter_y, (0, (1 - me) * width + sub * part), (width, part)
        )
        return lax.ppermute(sent, "gy", [(0, 1), (1, 0)])
    split = filter_y.reshape(width, n_y, parts, part)
    split = lax.dynamic_index_in_dim(split, sub, axis=2, keepdims=False)
    return lax.all_to_all(split, "gy", 1, 0, tiled=True)


def filter_columns(filter_y, got, parts):
    width, n_y = filter_y.shape[0], lax.axis_size("gy")
    part = width // parts
    sub, me = lax.rem(lax.axis_index("gx"), parts), lax.axis_index("gy")
    order = piece_order(parts)
    if n_y == 2 and parts == 2:
        mine = lax.dynamic_slice(filter_y, (0, me * width + sub * part), (width, part))
        return [
            lax.dynamic_slice_in_dim(source, s * part, part, axis=0)
            for source, (s, _) in zip((mine, mine, got, got), order)
        ]
    split = got.reshape(n_y, parts, part, part)
    return [split[g, s] for s, g in order]


def row_halo(first, last):
    n_x = lax.axis_size("gx")
    up = [(i, i + 1) for i in range(n_x - 1)]
    down = [(i + 1, i) for i in range(n_x - 1)]
    return jnp.stack([lax.ppermute(last, "gx", up), lax.ppermute(first, "gx", down)])


def side_halo(first, last):
    n_y, me = lax.axis_size("gy"), lax.axis_index("gy")
    if n_y == 2:
        got = lax.ppermute(jnp.where(me == 0, last, first), "gy", [(0, 1), (1, 0)])
        none = jnp.zeros_like(got)
        return jnp.where(me == 0, none, got), jnp.where(me == 0, got, none)
    up = [(i, i + 1) for i in range(n_y - 1)]
    down = [(i + 1, i) for i in range(n_y - 1)]
    return lax.ppermute(last, "gy", up), lax.ppermute(first, "gy", down)


def edge_flux(starts, rows_in, before, after, fields):
    def flux(up, here, down, left, right, fields, wind):
        innovation, weight, cx, cy = fields
        end = here - cx * (down - up) * 0.5 - cy * (right - left) * 0.5
        return fields[wind] * (weight * (end - innovation))

    top = starts[0][:2].astype(F32)
    bottom = starts[-1][-2:].astype(F32)
    here = jnp.stack([top[0], bottom[1]])
    ends = jnp.stack([before[0], before[-1]]), jnp.stack([after[0], after[-1]])
    row_flux = flux(
        jnp.stack([rows_in[0], bottom[0]]),
        here,
        jnp.stack([top[1], rows_in[1]]),
        jnp.concatenate([ends[0][:, :, None], here[:, :, :-1]], axis=2),
        jnp.concatenate([here[:, :, 1:], ends[1][:, :, None]], axis=2),
        [jnp.stack([f[0], f[-1]]) for f in fields],
        2,
    )
    side = [
        jnp.concatenate([s[:, :, at] for s in starts]).astype(F32)
        for at in (0, 1, -2, -1)
    ]
    here = jnp.stack([side[0], side[3]])
    halo = jnp.stack([rows_in[:, :, 0], rows_in[:, :, -1]])
    side_flux = flux(
        jnp.concatenate([halo[:, :1], here[:, :-1]], axis=1),
        here,
        jnp.concatenate([here[:, 1:], halo[:, 1:]], axis=1),
        jnp.stack([before, side[2]]),
        jnp.stack([side[1], after]),
        [jnp.stack([f[:, :, 0], f[:, :, -1]]) for f in fields],
        3,
    )
    return row_flux, side_flux


def per_device(control, innovation, obs_weight, courant_x, courant_y, filter_x, filter_y):
    rows, levels, width = control.shape
    n_x = lax.axis_size("gx")
    parts = n_x // levels
    part = width // parts
    cut, piece = rows // CHUNKS, part // CHUNKS
    spans = [slice(w * piece, (w + 1) * piece) for w in range(CHUNKS)]

    rows_y = filter_rows(filter_y, parts)
    matrix_x = [lax.all_gather(filter_x[:cut], "gx", axis=0, tiled=True)]
    lines = [swap_all(as_lines(control, parts, w)) for w in range(CHUNKS)]
    lines = [l.reshape(n_x * rows, piece) for l in lines]
    lines[-1], filter_x = lax.optimization_barrier((lines[-1], filter_x))
    for h in range(1, CHUNKS):
        share = filter_x[h * cut : (h + 1) * cut]
        matrix_x.append(lax.all_gather(share, "gx", axis=0, tiled=True))
    starts = []
    for h in range(CHUNKS):
        start = 0.0
        for w, span in enumerate(spans):
            smoothed = jnp.dot(matrix_x[h], lines[w], preferred_element_type=F32)
            smoothed = smoothed.astype(BF16).reshape(n_x, cut, piece)
            if h > 0:
                smoothed, columns_y = lax.optimization_barrier((smoothed, columns_y))
            for plane, matrix in zip(plane_pieces(smoothed, parts), rows_y):
                start = start + jnp.einsum(
                    "brc,kc->brk", plane, matrix[:, span], preferred_element_type=F32
                )
        start = start.astype(BF16)
        if h == 0:
            start, filter_y = lax.optimization_barrier((start, filter_y))
            columns_y = send_columns(filter_y, parts)
        came = swap_all(start).reshape(levels, parts, cut, part)
        came = came.transpose(2, 0, 1, 3).reshape(cut, levels, width)
        starts.append(came)

    rows_in = row_halo(starts[0][0], starts[-1][-1]).astype(F32)
    before, after = side_halo(
        jnp.concatenate([s[:, :, 0] for s in starts]),
        jnp.concatenate([s[:, :, -1] for s in starts]),
    )
    before, after = before.astype(F32), after.astype(F32)
    fields = (innovation, obs_weight, courant_x, courant_y)
    row_flux, side_flux = edge_flux(starts, rows_in, before, after, fields)
    end_state, flat = forward(
        starts, rows_in, jnp.stack([before, after], axis=2), *fields
    )
    rows_in = row_halo(row_flux[0], row_flux[1])
    sides = jnp.stack(side_halo(side_flux[0], side_flux[1]), axis=2)
    columns_y = filter_columns(filter_y, columns_y, parts)

    pulled = []
    for w in range(CHUNKS):
        adjoint = swap_all(rim_lines(flat, rows_in, sides, parts, w))
        adjoint = adjoint.reshape(n_x, CHUNKS, cut, piece)
        total = 0.0
        for h in range(CHUNKS):
            total = total + jnp.einsum(
                "ij,ic->jc",
                matrix_x[h],
                adjoint[:, h].reshape(n_x * cut, piece),
                preferred_element_type=F32,
            )
        pulled.append(total.astype(BF16).reshape(n_x, CHUNKS, cut, piece))
    gradient = far = None
    for h in range(CHUNKS):
        carried = 0.0
        for w, span in enumerate(spans):
            held = far if h > 0 and w == CHUNKS - 1 else None
            planes = plane_pieces(pulled[w][:, h], parts, held)
            far = planes[-2] if w == CHUNKS - 1 else far
            for plane, matrix in zip(planes, columns_y):
                carried = carried + jnp.einsum(
                    "brk,kc->brc", plane, matrix[span], preferred_element_type=F32
                )
        carried = swap_all(carried.astype(BF16))
        gradient = add_lines(control, carried, parts, h, gradient)
    return (end_state, gradient)


def solution(mesh):
    placed = (
        P("gx", None, "gy"),
        P("gx", None, "gy"),
        P("gx", None, "gy"),
        P("gx", None, "gy"),
        P("gx", None, "gy"),
        P("gx", None),
        P("gy", None),
    )
    return jax.shard_map(
        per_device,
        mesh=mesh,
        in_specs=placed,
        out_specs=(P("gx", None, "gy"), P("gx", None, "gy")),
        check_vma=False,
    )
```

```python
import functools

import jax
import jax.numpy as jnp
from jax import lax
from jax.experimental import pallas as pl
from jax.experimental.pallas import tpu as pltpu
from jax.sharding import PartitionSpec as P

BF16 = jnp.bfloat16
F32 = jnp.float32
STEP = 32
GROUP = 8
CHUNKS = 2
PARAMS = pltpu.CompilerParams(vmem_limit_bytes=56 * 1024 * 1024)


def cost(flops, *arrays):
    return pl.CostEstimate(
        flops=flops,
        bytes_accessed=sum(a.size * a.dtype.itemsize for a in arrays),
        transcendentals=0,
    )


def chunk_spans(width, parts, chunk):
    part = width // parts
    piece = part // CHUNKS
    return [
        slice(s * part + chunk * piece, s * part + (chunk + 1) * piece)
        for s in range(parts)
    ]


def store_lines(turned, out, parts):
    piece = out.shape[2]
    for l in range(turned.shape[1]):
        for s in range(parts):
            got = turned[:, l, s * piece : (s + 1) * piece]
            out[l * parts + s] = got.astype(BF16)


def lines_body(parts, chunk, block, out, turned):
    piece = out.shape[2]
    for s, span in enumerate(chunk_spans(block.shape[2], parts, chunk)):
        turned[:, :, s * piece : (s + 1) * piece] = block[:, :, span].astype(F32)
    store_lines(turned, out, parts)


def as_lines(block, parts, chunk):
    rows, levels, width = block.shape
    shape = (levels * parts, rows, width // parts // CHUNKS)
    return pl.pallas_call(
        functools.partial(lines_body, parts, chunk),
        grid=(rows // STEP,),
        in_specs=[pl.BlockSpec((STEP, levels, width), lambda i: (i, 0, 0))],
        out_specs=pl.BlockSpec((shape[0], STEP, shape[2]), lambda i: (0, i, 0)),
        out_shape=jax.ShapeDtypeStruct(shape, BF16),
        scratch_shapes=[pltpu.VMEM((STEP, levels, width // CHUNKS), F32)],
        compiler_params=PARAMS,
        cost_estimate=cost(0, block, block),
        name="as_lines",
    )(block)


def gradient_body(parts, lines, control, *rest):
    out, turned = rest[-2:]
    levels, width = control.shape[1:]
    part = width // parts
    for l in range(levels):
        for s in range(parts):
            turned[:, l, s * part : (s + 1) * part] = lines[l * parts + s].astype(F32)
    out[...] = control[...].astype(F32) + turned[...]


def add_lines(control, lines, parts, chunk, target):
    rows, levels, width = control.shape
    whole = (STEP, levels, width)
    cut = rows // CHUNKS
    offset = chunk * cut // STEP
    operands = [lines, control] + ([] if target is None else [target])
    return pl.pallas_call(
        functools.partial(gradient_body, parts),
        grid=(cut // STEP,),
        in_specs=[
            pl.BlockSpec((lines.shape[0], STEP, lines.shape[2]), lambda i: (0, i, 0)),
            pl.BlockSpec(whole, lambda i: (i + offset, 0, 0)),
        ]
        + [pl.BlockSpec(memory_space=pl.ANY)] * (len(operands) - 2),
        out_specs=pl.BlockSpec(whole, lambda i: (i + offset, 0, 0)),
        out_shape=jax.ShapeDtypeStruct(control.shape, F32),
        input_output_aliases={} if target is None else {2: 0},
        scratch_shapes=[pltpu.VMEM(whole, F32)],
        compiler_params=PARAMS,
        cost_estimate=cost(control.size // 2, control, control),
        name="add_lines",
    )(*operands)


def forward_body(*refs):
    starts = refs[:CHUNKS]
    rows_in, sides, innovation, weight, wind_x, wind_y = refs[CHUNKS : CHUNKS + 6]
    end, flat, row_flux, side_flux, state, carry = refs[CHUNKS + 6 :]
    step = pl.program_id(0)
    rows, levels, width = flat.shape
    cut = rows // CHUNKS

    @pl.when(step == 0)
    def _():
        state[pl.ds(0, 1)] = rows_in[pl.ds(0, 1)]
        state[pl.ds(rows + 1, 1)] = rows_in[pl.ds(1, 1)]
        for h in range(CHUNKS):
            state[pl.ds(1 + h * cut, cut)] = starts[h][...].astype(F32)
        carry[...] = jnp.zeros(carry.shape, F32)

    first = step * STEP
    place = lax.broadcasted_iota(jnp.int32, (GROUP, levels, width), 2)
    left_edge, right_edge = place == 0, place == width - 1
    for j in range(0, STEP, GROUP):
        rows_j, at = pl.ds(j, GROUP), first + j
        here = state[pl.ds(at + 1, GROUP)]
        cx, cy = wind_x[rows_j], wind_y[rows_j]
        left = jnp.where(left_edge, sides[rows_j, :, 0:1], pltpu.roll(here, 1, 2))
        right = jnp.where(
            right_edge, sides[rows_j, :, 1:2], pltpu.roll(here, width - 1, 2)
        )
        dx = state[pl.ds(at + 2, GROUP)] - state[pl.ds(at, GROUP)]
        after = here - cx * dx * 0.5 - cy * (right - left) * 0.5
        end[rows_j] = after
        misfit = weight[rows_j] * (after - innovation[rows_j])
        p, q = cy * misfit, cx * misfit
        side_flux[rows_j, :, 0:1] = p[:, :, 0:1]
        side_flux[rows_j, :, 1:2] = p[:, :, width - 1 : width]
        left = jnp.where(left_edge, 0.0, pltpu.roll(p, 1, 2))
        right = jnp.where(right_edge, 0.0, pltpu.roll(p, width - 1, 2))
        flat_j = misfit + 0.5 * (right - left)
        flat[jnp.maximum(at - 1, 0)] = carry[2] + 0.5 * (q[0] - carry[0])
        flat[at] = flat_j[0] + 0.5 * (q[1] - carry[1])
        flat[pl.ds(at + 1, GROUP - 2)] = flat_j[1:-1] + 0.5 * (q[2:] - q[:-2])
        if j == 0:
            carry[3] = q[0]
        carry[0], carry[1], carry[2] = q[GROUP - 2], q[GROUP - 1], flat_j[GROUP - 1]

    @pl.when(step == 0)
    def _():
        row_flux[0] = carry[3]

    @pl.when(step == rows // STEP - 1)
    def _():
        flat[rows - 1] = carry[2] - 0.5 * carry[0]
        row_flux[1] = carry[1]


def forward(starts, rows_in, sides, innovation, weight, wind_x, wind_y):
    rows, levels, width = innovation.shape
    blocked = pl.BlockSpec((STEP, levels, width), lambda i: (i, 0, 0))
    side = pl.BlockSpec((STEP, levels, 2), lambda i: (i, 0, 0))
    pair = pl.BlockSpec((2, levels, width), lambda i: (0, 0, 0))
    start = pl.BlockSpec(starts[0].shape, lambda i: (0, 0, 0))
    whole = pl.BlockSpec((rows, levels, width), lambda i: (0, 0, 0))
    return pl.pallas_call(
        forward_body,
        grid=(rows // STEP,),
        in_specs=[start] * CHUNKS + [pair, side, blocked, blocked, blocked, blocked],
        out_specs=[blocked, whole, pair, side],
        out_shape=[
            jax.ShapeDtypeStruct((rows, levels, width), F32),
            jax.ShapeDtypeStruct((rows, levels, width), F32),
            jax.ShapeDtypeStruct((2, levels, width), F32),
            jax.ShapeDtypeStruct((rows, levels, 2), F32),
        ],
        scratch_shapes=[
            pltpu.VMEM((rows + 2, levels, width), F32),
            pltpu.VMEM((4, levels, width), F32),
        ],
        compiler_params=PARAMS,
        cost_estimate=cost(30 * innovation.size, *[innovation] * 7),
        name="forward",
    )(*starts, rows_in, sides, innovation, weight, wind_x, wind_y)


def rim_body(parts, chunk, last, flat, rows_in, sides, out, turned):
    step = pl.program_id(0)
    levels, width = flat.shape[1:]
    piece = out.shape[2]
    place = lax.broadcasted_iota(jnp.int32, (STEP, levels, piece), 2)
    spans = chunk_spans(width, parts, chunk)
    for s, span in enumerate(spans):
        value = flat[:, :, span]
        if span.start == 0:
            value = value - jnp.where(place == 0, 0.5 * sides[:, :, 0:1], 0.0)
        if span.stop == width:
            value = value + jnp.where(place == piece - 1, 0.5 * sides[:, :, 1:2], 0.0)
        turned[:, :, s * piece : (s + 1) * piece] = value

    @pl.when(step == 0)
    def _():
        for s, span in enumerate(spans):
            at = slice(s * piece, (s + 1) * piece)
            turned[0, :, at] += -0.5 * rows_in[0, :, span]

    @pl.when(step == last)
    def _():
        for s, span in enumerate(spans):
            at = slice(s * piece, (s + 1) * piece)
            turned[STEP - 1, :, at] += 0.5 * rows_in[1, :, span]

    store_lines(turned, out, parts)


def rim_lines(flat, rows_in, sides, parts, chunk):
    rows, levels, width = flat.shape
    shape = (levels * parts, rows, width // parts // CHUNKS)
    return pl.pallas_call(
        functools.partial(rim_body, parts, chunk, rows // STEP - 1),
        grid=(rows // STEP,),
        in_specs=[
            pl.BlockSpec((STEP, levels, width), lambda i: (i, 0, 0)),
            pl.BlockSpec((2, levels, width), lambda i: (0, 0, 0)),
            pl.BlockSpec((STEP, levels, 2), lambda i: (i, 0, 0)),
        ],
        out_specs=pl.BlockSpec((shape[0], STEP, shape[2]), lambda i: (0, i, 0)),
        out_shape=jax.ShapeDtypeStruct(shape, BF16),
        scratch_shapes=[pltpu.VMEM((STEP, levels, width // CHUNKS), F32)],
        compiler_params=PARAMS,
        cost_estimate=cost(4 * flat.size, flat, flat),
        name="rim_lines",
    )(flat, rows_in, sides)


def swap_all(lines):
    return lax.all_to_all(lines, "gx", 0, 0, tiled=True)


def plane_pieces(lines, parts, after=None):
    n_x, n_y = lax.axis_size("gx"), lax.axis_size("gy")
    groups = [list(range(i, i + parts)) for i in range(0, n_x, parts)]
    if n_y == 2 and parts == 2:
        pairs = [(a, b) for g in groups for a, b in (g, g[::-1])]
        sent = lines if after is None else lax.optimization_barrier((lines, after))[0]
        far = lax.ppermute(sent, "gy", [(0, 1), (1, 0)])
        near = lax.ppermute(lines, "gx", pairs)
        cross = lax.ppermute(far, "gx", pairs)
        return [lines, near, far, cross]
    plane = lax.all_gather(lines, "gy", axis=0, tiled=False)
    plane = lax.all_gather(plane, "gx", axis=0, tiled=False, axis_index_groups=groups)
    return [plane[s, g] for s in range(parts) for g in range(n_y)]


def piece_order(parts):
    n_y = lax.axis_size("gy")
    sub, me = lax.rem(lax.axis_index("gx"), parts), lax.axis_index("gy")
    if n_y == 2 and parts == 2:
        return [(sub, me), (1 - sub, me), (sub, 1 - me), (1 - sub, 1 - me)]
    return [(s, g) for s in range(parts) for g in range(n_y)]


def filter_rows(filter_y, parts):
    width = filter_y.shape[0]
    part = width // parts
    sub = lax.rem(lax.axis_index("gx"), parts)
    return [
        lax.dynamic_slice(filter_y, (sub * part, g * width + s * part), (part, part))
        for s, g in piece_order(parts)
    ]


def send_columns(filter_y, parts):
    width, n_y = filter_y.shape[0], lax.axis_size("gy")
    part = width // parts
    sub, me = lax.rem(lax.axis_index("gx"), parts), lax.axis_index("gy")
    if n_y == 2 and parts == 2:
        sent = lax.dynamic_slice(
            filter_y, (0, (1 - me) * width + sub * part), (width, part)
        )
        return lax.ppermute(sent, "gy", [(0, 1), (1, 0)])
    split = filter_y.reshape(width, n_y, parts, part)
    split = lax.dynamic_index_in_dim(split, sub, axis=2, keepdims=False)
    return lax.all_to_all(split, "gy", 1, 0, tiled=True)


def filter_columns(filter_y, got, parts):
    width, n_y = filter_y.shape[0], lax.axis_size("gy")
    part = width // parts
    sub, me = lax.rem(lax.axis_index("gx"), parts), lax.axis_index("gy")
    order = piece_order(parts)
    if n_y == 2 and parts == 2:
        mine = lax.dynamic_slice(filter_y, (0, me * width + sub * part), (width, part))
        return [
            lax.dynamic_slice_in_dim(source, s * part, part, axis=0)
            for source, (s, _) in zip((mine, mine, got, got), order)
        ]
    split = got.reshape(n_y, parts, part, part)
    return [split[g, s] for s, g in order]


def row_halo(first, last):
    n_x = lax.axis_size("gx")
    up = [(i, i + 1) for i in range(n_x - 1)]
    down = [(i + 1, i) for i in range(n_x - 1)]
    return jnp.stack([lax.ppermute(last, "gx", up), lax.ppermute(first, "gx", down)])


def side_halo(first, last):
    n_y, me = lax.axis_size("gy"), lax.axis_index("gy")
    if n_y == 2:
        got = lax.ppermute(jnp.where(me == 0, last, first), "gy", [(0, 1), (1, 0)])
        none = jnp.zeros_like(got)
        return jnp.where(me == 0, none, got), jnp.where(me == 0, got, none)
    up = [(i, i + 1) for i in range(n_y - 1)]
    down = [(i + 1, i) for i in range(n_y - 1)]
    return lax.ppermute(last, "gy", up), lax.ppermute(first, "gy", down)


def per_device(control, innovation, obs_weight, courant_x, courant_y, filter_x, filter_y):
    rows, levels, width = control.shape
    n_x = lax.axis_size("gx")
    parts = n_x // levels
    part = width // parts
    cut, piece = rows // CHUNKS, part // CHUNKS
    spans = [slice(w * piece, (w + 1) * piece) for w in range(CHUNKS)]

    rows_y = filter_rows(filter_y, parts)
    matrix_x = [lax.all_gather(filter_x[:cut], "gx", axis=0, tiled=True)]
    lines = [swap_all(as_lines(control, parts, w)) for w in range(CHUNKS)]
    lines = [l.reshape(n_x * rows, piece) for l in lines]
    lines[-1], filter_x = lax.optimization_barrier((lines[-1], filter_x))
    for h in range(1, CHUNKS):
        share = filter_x[h * cut : (h + 1) * cut]
        matrix_x.append(lax.all_gather(share, "gx", axis=0, tiled=True))
    starts = []
    for h in range(CHUNKS):
        start = 0.0
        for w, span in enumerate(spans):
            smoothed = jnp.dot(matrix_x[h], lines[w], preferred_element_type=F32)
            smoothed = smoothed.astype(BF16).reshape(n_x, cut, piece)
            for plane, matrix in zip(plane_pieces(smoothed, parts), rows_y):
                start = start + jnp.einsum(
                    "brc,kc->brk", plane, matrix[:, span], preferred_element_type=F32
                )
        start = start.astype(BF16)
        if h == CHUNKS - 1:
            start, filter_y = lax.optimization_barrier((start, filter_y))
            columns_y = send_columns(filter_y, parts)
        came = swap_all(start).reshape(levels, parts, cut, part)
        came = came.transpose(2, 0, 1, 3).reshape(cut, levels, width)
        starts.append(came)

    rows_in = row_halo(starts[0][0], starts[-1][-1]).astype(F32)
    before, after = side_halo(
        jnp.concatenate([s[:, :, 0] for s in starts]),
        jnp.concatenate([s[:, :, -1] for s in starts]),
    )
    sides = jnp.stack([before, after], axis=2).astype(F32)
    end_state, flat, row_flux, side_flux = forward(
        starts, rows_in, sides, innovation, obs_weight, courant_x, courant_y
    )
    rows_in = row_halo(row_flux[0], row_flux[1])
    before, after = side_halo(side_flux[:, :, 0], side_flux[:, :, 1])
    sides = jnp.stack([before, after], axis=2)
    flat, columns_y = lax.optimization_barrier((flat, columns_y))
    columns_y = filter_columns(filter_y, columns_y, parts)

    pulled = []
    for w in range(CHUNKS):
        adjoint = swap_all(rim_lines(flat, rows_in, sides, parts, w))
        adjoint = adjoint.reshape(n_x, CHUNKS, cut, piece)
        total = 0.0
        for h in range(CHUNKS):
            total = total + jnp.einsum(
                "ij,ic->jc",
                matrix_x[h],
                adjoint[:, h].reshape(n_x * cut, piece),
                preferred_element_type=F32,
            )
        pulled.append(total.astype(BF16).reshape(n_x, CHUNKS, cut, piece))
    gradient = far = None
    for h in range(CHUNKS):
        carried = 0.0
        for w, span in enumerate(spans):
            held = far if h > 0 and w == CHUNKS - 1 else None
            planes = plane_pieces(pulled[w][:, h], parts, held)
            far = planes[-2] if w == CHUNKS - 1 else far
            for plane, matrix in zip(planes, columns_y):
                carried = carried + jnp.einsum(
                    "brk,kc->brc", plane, matrix[span], preferred_element_type=F32
                )
        carried = swap_all(carried.astype(BF16))
        gradient = add_lines(control, carried, parts, h, gradient)
    return (end_state, gradient)


def solution(mesh):
    placed = (
        P("gx", None, "gy"),
        P("gx", None, "gy"),
        P("gx", None, "gy"),
        P("gx", None, "gy"),
        P("gx", None, "gy"),
        P("gx", None),
        P("gy", None),
    )
    return jax.shard_map(
        per_device,
        mesh=mesh,
        in_specs=placed,
        out_specs=(P("gx", None, "gy"), P("gx", None, "gy")),
        check_vma=False,
    )
```

```python
import functools

import jax
import jax.numpy as jnp
from jax import lax
from jax.experimental import pallas as pl
from jax.experimental.pallas import tpu as pltpu
from jax.sharding import PartitionSpec as P

BF16 = jnp.bfloat16
F32 = jnp.float32
STEP = 32
GROUP = 8
CHUNKS = 2
PARAMS = pltpu.CompilerParams(vmem_limit_bytes=56 * 1024 * 1024)


def cost(flops, *arrays):
    return pl.CostEstimate(
        flops=flops,
        bytes_accessed=sum(a.size * a.dtype.itemsize for a in arrays),
        transcendentals=0,
    )


def chunk_spans(width, parts, chunk):
    part = width // parts
    piece = part // CHUNKS
    return [
        slice(s * part + chunk * piece, s * part + (chunk + 1) * piece)
        for s in range(parts)
    ]


def store_lines(turned, out, parts):
    piece = out.shape[2]
    for l in range(turned.shape[1]):
        for s in range(parts):
            got = turned[:, l, s * piece : (s + 1) * piece]
            out[l * parts + s] = got.astype(BF16)


def lines_body(parts, chunk, block, out, turned):
    piece = out.shape[2]
    for s, span in enumerate(chunk_spans(block.shape[2], parts, chunk)):
        turned[:, :, s * piece : (s + 1) * piece] = block[:, :, span].astype(F32)
    store_lines(turned, out, parts)


def as_lines(block, parts, chunk):
    rows, levels, width = block.shape
    shape = (levels * parts, rows, width // parts // CHUNKS)
    return pl.pallas_call(
        functools.partial(lines_body, parts, chunk),
        grid=(rows // STEP,),
        in_specs=[pl.BlockSpec((STEP, levels, width), lambda i: (i, 0, 0))],
        out_specs=pl.BlockSpec((shape[0], STEP, shape[2]), lambda i: (0, i, 0)),
        out_shape=jax.ShapeDtypeStruct(shape, BF16),
        scratch_shapes=[pltpu.VMEM((STEP, levels, width // CHUNKS), F32)],
        compiler_params=PARAMS,
        cost_estimate=cost(0, block, block),
        name="as_lines",
    )(block)


def gradient_body(parts, lines, control, *rest):
    out, turned = rest[-2:]
    levels, width = control.shape[1:]
    part = width // parts
    for l in range(levels):
        for s in range(parts):
            turned[:, l, s * part : (s + 1) * part] = lines[l * parts + s].astype(F32)
    out[...] = control[...].astype(F32) + turned[...]


def add_lines(control, lines, parts, chunk, target):
    rows, levels, width = control.shape
    whole = (STEP, levels, width)
    cut = rows // CHUNKS
    offset = chunk * cut // STEP
    operands = [lines, control] + ([] if target is None else [target])
    return pl.pallas_call(
        functools.partial(gradient_body, parts),
        grid=(cut // STEP,),
        in_specs=[
            pl.BlockSpec((lines.shape[0], STEP, lines.shape[2]), lambda i: (0, i, 0)),
            pl.BlockSpec(whole, lambda i: (i + offset, 0, 0)),
        ]
        + [pl.BlockSpec(memory_space=pl.ANY)] * (len(operands) - 2),
        out_specs=pl.BlockSpec(whole, lambda i: (i + offset, 0, 0)),
        out_shape=jax.ShapeDtypeStruct(control.shape, F32),
        input_output_aliases={} if target is None else {2: 0},
        scratch_shapes=[pltpu.VMEM(whole, F32)],
        compiler_params=PARAMS,
        cost_estimate=cost(control.size // 2, control, control),
        name="add_lines",
    )(*operands)


def forward_body(*refs):
    starts = refs[:CHUNKS]
    rows_in, sides, innovation, weight, wind_x, wind_y = refs[CHUNKS : CHUNKS + 6]
    end, flat, row_flux, side_flux, state, carry = refs[CHUNKS + 6 :]
    step = pl.program_id(0)
    rows, levels, width = flat.shape
    cut = rows // CHUNKS

    @pl.when(step == 0)
    def _():
        state[pl.ds(0, 1)] = rows_in[pl.ds(0, 1)]
        state[pl.ds(rows + 1, 1)] = rows_in[pl.ds(1, 1)]
        for h in range(CHUNKS):
            state[pl.ds(1 + h * cut, cut)] = starts[h][...].astype(F32)
        carry[...] = jnp.zeros(carry.shape, F32)

    first = step * STEP
    place = lax.broadcasted_iota(jnp.int32, (GROUP, levels, width), 2)
    left_edge, right_edge = place == 0, place == width - 1
    @pl.loop(0, STEP // GROUP)
    def _(group):
        j = group * GROUP
        rows_j, at = pl.ds(j, GROUP), first + j
        here = state[pl.ds(at + 1, GROUP)]
        cx, cy = wind_x[rows_j], wind_y[rows_j]
        left = jnp.where(left_edge, sides[rows_j, :, 0:1], pltpu.roll(here, 1, 2))
        right = jnp.where(
            right_edge, sides[rows_j, :, 1:2], pltpu.roll(here, width - 1, 2)
        )
        dx = state[pl.ds(at + 2, GROUP)] - state[pl.ds(at, GROUP)]
        after = here - cx * dx * 0.5 - cy * (right - left) * 0.5
        end[rows_j] = after
        misfit = weight[rows_j] * (after - innovation[rows_j])
        p, q = cy * misfit, cx * misfit
        side_flux[rows_j, :, 0:1] = p[:, :, 0:1]
        side_flux[rows_j, :, 1:2] = p[:, :, width - 1 : width]
        left = jnp.where(left_edge, 0.0, pltpu.roll(p, 1, 2))
        right = jnp.where(right_edge, 0.0, pltpu.roll(p, width - 1, 2))
        flat_j = misfit + 0.5 * (right - left)
        flat[jnp.maximum(at - 1, 0)] = carry[2] + 0.5 * (q[0] - carry[0])
        flat[at] = flat_j[0] + 0.5 * (q[1] - carry[1])
        flat[pl.ds(at + 1, GROUP - 2)] = flat_j[1:-1] + 0.5 * (q[2:] - q[:-2])

        @pl.when(at == 0)
        def _():
            row_flux[0] = q[0]

        carry[0], carry[1], carry[2] = q[GROUP - 2], q[GROUP - 1], flat_j[GROUP - 1]

    @pl.when(step == rows // STEP - 1)
    def _():
        flat[rows - 1] = carry[2] - 0.5 * carry[0]
        row_flux[1] = carry[1]


def forward(starts, rows_in, sides, innovation, weight, wind_x, wind_y):
    rows, levels, width = innovation.shape
    blocked = pl.BlockSpec((STEP, levels, width), lambda i: (i, 0, 0))
    side = pl.BlockSpec((STEP, levels, 2), lambda i: (i, 0, 0))
    pair = pl.BlockSpec((2, levels, width), lambda i: (0, 0, 0))
    start = pl.BlockSpec(starts[0].shape, lambda i: (0, 0, 0))
    whole = pl.BlockSpec((rows, levels, width), lambda i: (0, 0, 0))
    return pl.pallas_call(
        forward_body,
        grid=(rows // STEP,),
        in_specs=[start] * CHUNKS + [pair, side, blocked, blocked, blocked, blocked],
        out_specs=[blocked, whole, pair, side],
        out_shape=[
            jax.ShapeDtypeStruct((rows, levels, width), F32),
            jax.ShapeDtypeStruct((rows, levels, width), F32),
            jax.ShapeDtypeStruct((2, levels, width), F32),
            jax.ShapeDtypeStruct((rows, levels, 2), F32),
        ],
        scratch_shapes=[
            pltpu.VMEM((rows + 2, levels, width), F32),
            pltpu.VMEM((3, levels, width), F32),
        ],
        compiler_params=PARAMS,
        cost_estimate=cost(30 * innovation.size, *[innovation] * 7),
        name="forward",
    )(*starts, rows_in, sides, innovation, weight, wind_x, wind_y)


def rim_body(parts, chunk, last, flat, rows_in, sides, out, turned):
    step = pl.program_id(0)
    levels, width = flat.shape[1:]
    piece = out.shape[2]
    place = lax.broadcasted_iota(jnp.int32, (STEP, levels, piece), 2)
    spans = chunk_spans(width, parts, chunk)
    for s, span in enumerate(spans):
        value = flat[:, :, span]
        if span.start == 0:
            value = value - jnp.where(place == 0, 0.5 * sides[:, :, 0:1], 0.0)
        if span.stop == width:
            value = value + jnp.where(place == piece - 1, 0.5 * sides[:, :, 1:2], 0.0)
        turned[:, :, s * piece : (s + 1) * piece] = value

    @pl.when(step == 0)
    def _():
        for s, span in enumerate(spans):
            at = slice(s * piece, (s + 1) * piece)
            turned[0, :, at] += -0.5 * rows_in[0, :, span]

    @pl.when(step == last)
    def _():
        for s, span in enumerate(spans):
            at = slice(s * piece, (s + 1) * piece)
            turned[STEP - 1, :, at] += 0.5 * rows_in[1, :, span]

    store_lines(turned, out, parts)


def rim_lines(flat, rows_in, sides, parts, chunk):
    rows, levels, width = flat.shape
    shape = (levels * parts, rows, width // parts // CHUNKS)
    return pl.pallas_call(
        functools.partial(rim_body, parts, chunk, rows // STEP - 1),
        grid=(rows // STEP,),
        in_specs=[
            pl.BlockSpec((STEP, levels, width), lambda i: (i, 0, 0)),
            pl.BlockSpec((2, levels, width), lambda i: (0, 0, 0)),
            pl.BlockSpec((STEP, levels, 2), lambda i: (i, 0, 0)),
        ],
        out_specs=pl.BlockSpec((shape[0], STEP, shape[2]), lambda i: (0, i, 0)),
        out_shape=jax.ShapeDtypeStruct(shape, BF16),
        scratch_shapes=[pltpu.VMEM((STEP, levels, width // CHUNKS), F32)],
        compiler_params=PARAMS,
        cost_estimate=cost(4 * flat.size, flat, flat),
        name="rim_lines",
    )(flat, rows_in, sides)


def swap_all(lines):
    return lax.all_to_all(lines, "gx", 0, 0, tiled=True)


def plane_pieces(lines, parts, after=None):
    n_x, n_y = lax.axis_size("gx"), lax.axis_size("gy")
    groups = [list(range(i, i + parts)) for i in range(0, n_x, parts)]
    if n_y == 2 and parts == 2:
        pairs = [(a, b) for g in groups for a, b in (g, g[::-1])]
        sent = lines if after is None else lax.optimization_barrier((lines, after))[0]
        far = lax.ppermute(sent, "gy", [(0, 1), (1, 0)])
        near = lax.ppermute(lines, "gx", pairs)
        cross = lax.ppermute(far, "gx", pairs)
        return [lines, near, far, cross]
    plane = lax.all_gather(lines, "gy", axis=0, tiled=False)
    plane = lax.all_gather(plane, "gx", axis=0, tiled=False, axis_index_groups=groups)
    return [plane[s, g] for s in range(parts) for g in range(n_y)]


def piece_order(parts):
    n_y = lax.axis_size("gy")
    sub, me = lax.rem(lax.axis_index("gx"), parts), lax.axis_index("gy")
    if n_y == 2 and parts == 2:
        return [(sub, me), (1 - sub, me), (sub, 1 - me), (1 - sub, 1 - me)]
    return [(s, g) for s in range(parts) for g in range(n_y)]


def filter_rows(filter_y, parts):
    width = filter_y.shape[0]
    part = width // parts
    sub = lax.rem(lax.axis_index("gx"), parts)
    return [
        lax.dynamic_slice(filter_y, (sub * part, g * width + s * part), (part, part))
        for s, g in piece_order(parts)
    ]


def send_columns(filter_y, parts):
    width, n_y = filter_y.shape[0], lax.axis_size("gy")
    part = width // parts
    sub, me = lax.rem(lax.axis_index("gx"), parts), lax.axis_index("gy")
    if n_y == 2 and parts == 2:
        sent = lax.dynamic_slice(
            filter_y, (0, (1 - me) * width + sub * part), (width, part)
        )
        return lax.ppermute(sent, "gy", [(0, 1), (1, 0)])
    split = filter_y.reshape(width, n_y, parts, part)
    split = lax.dynamic_index_in_dim(split, sub, axis=2, keepdims=False)
    return lax.all_to_all(split, "gy", 1, 0, tiled=True)


def filter_columns(filter_y, got, parts):
    width, n_y = filter_y.shape[0], lax.axis_size("gy")
    part = width // parts
    sub, me = lax.rem(lax.axis_index("gx"), parts), lax.axis_index("gy")
    order = piece_order(parts)
    if n_y == 2 and parts == 2:
        mine = lax.dynamic_slice(filter_y, (0, me * width + sub * part), (width, part))
        return [
            lax.dynamic_slice_in_dim(source, s * part, part, axis=0)
            for source, (s, _) in zip((mine, mine, got, got), order)
        ]
    split = got.reshape(n_y, parts, part, part)
    return [split[g, s] for s, g in order]


def sums_body(rule, *refs):
    pieces = (len(refs) - 2) // 2
    planes, matrices = refs[1 : 1 + pieces], refs[1 + pieces : 1 + 2 * pieces]
    rest = refs[1 + 2 * pieces :]
    total = rest[0][...] if len(rest) > 1 else 0.0
    for plane, matrix in zip(planes, matrices):
        total = total + lax.dot_general(
            plane[...], matrix[...], (rule, ((), ())), preferred_element_type=F32
        )
    rest[-1][...] = total.astype(rest[-1].dtype)


def y_sums(planes, sources, places, block, total, dtype):
    planes = [p.reshape(-1, p.shape[-1]) for p in planes]
    rows, depth = planes[0].shape
    tall = block[0] == depth
    width = block[1] if tall else block[0]
    tile = min(rows, 256)
    out = pl.BlockSpec((tile, width), lambda i, at: (i, 0))
    in_specs = [pl.BlockSpec((tile, depth), lambda i, at: (i, 0))] * len(planes)
    for q in range(len(sources)):
        in_specs.append(
            pl.BlockSpec(block, lambda i, at, q=q: (at[2 * q], at[2 * q + 1]))
        )
    operands = [*planes, *sources]
    if total is not None:
        in_specs.append(out)
        operands.append(total)
    return pl.pallas_call(
        functools.partial(sums_body, ((1,), (0 if tall else 1,))),
        grid_spec=pltpu.PrefetchScalarGridSpec(
            num_scalar_prefetch=1,
            grid=(rows // tile,),
            in_specs=in_specs,
            out_specs=out,
        ),
        out_shape=jax.ShapeDtypeStruct((rows, width), dtype),
        compiler_params=PARAMS,
        cost_estimate=cost(2 * rows * width * depth * len(planes), *planes),
        name="y_sums",
    )(jnp.stack([jnp.int32(p) for p in places]), *operands)


def y_filter(planes, filter_y, got, parts, backward):
    width, n_y = filter_y.shape[0], lax.axis_size("gy")
    part = width // parts
    piece = part // CHUNKS
    sub, me = lax.rem(lax.axis_index("gx"), parts), lax.axis_index("gy")
    order = piece_order(parts)
    blocks, rows, _ = planes[0][0].shape
    total = None
    if n_y == 2 and parts == 2 and piece % 128 == 0:
        for w in range(CHUNKS):
            places = []
            for q, (s, g) in enumerate(order):
                if not backward:
                    places += [sub, (g * parts + s) * CHUNKS + w]
                else:
                    places += [s * CHUNKS + w, me * parts + sub if q < 2 else 0]
            sources = [filter_y] * 2 + [got if backward else filter_y] * 2
            block = (piece, part) if backward else (part, piece)
            dtype = BF16 if w == CHUNKS - 1 else F32
            total = y_sums(planes[w], sources, places, block, total, dtype)
        return total.reshape(blocks, rows, part)
    matrices = (
        filter_columns(filter_y, got, parts) if backward else filter_rows(filter_y, parts)
    )
    total = 0.0
    for w in range(CHUNKS):
        span = slice(w * piece, (w + 1) * piece)
        for plane, matrix in zip(planes[w], matrices):
            if backward:
                total = total + jnp.einsum(
                    "brk,kc->brc", plane, matrix[span], preferred_element_type=F32
                )
            else:
                total = total + jnp.einsum(
                    "brc,kc->brk", plane, matrix[:, span], preferred_element_type=F32
                )
    return total.astype(BF16)


def row_halo(first, last):
    n_x = lax.axis_size("gx")
    up = [(i, i + 1) for i in range(n_x - 1)]
    down = [(i + 1, i) for i in range(n_x - 1)]
    return jnp.stack([lax.ppermute(last, "gx", up), lax.ppermute(first, "gx", down)])


def side_halo(first, last):
    n_y, me = lax.axis_size("gy"), lax.axis_index("gy")
    if n_y == 2:
        got = lax.ppermute(jnp.where(me == 0, last, first), "gy", [(0, 1), (1, 0)])
        none = jnp.zeros_like(got)
        return jnp.where(me == 0, none, got), jnp.where(me == 0, got, none)
    up = [(i, i + 1) for i in range(n_y - 1)]
    down = [(i + 1, i) for i in range(n_y - 1)]
    return lax.ppermute(last, "gy", up), lax.ppermute(first, "gy", down)


def per_device(control, innovation, obs_weight, courant_x, courant_y, filter_x, filter_y):
    rows, levels, width = control.shape
    n_x = lax.axis_size("gx")
    parts = n_x // levels
    part = width // parts
    cut, piece = rows // CHUNKS, part // CHUNKS

    matrix_x = [lax.all_gather(filter_x[:cut], "gx", axis=0, tiled=True)]
    lines = [swap_all(as_lines(control, parts, w)) for w in range(CHUNKS)]
    lines = [l.reshape(n_x * rows, piece) for l in lines]
    lines[-1], filter_x = lax.optimization_barrier((lines[-1], filter_x))
    for h in range(1, CHUNKS):
        share = filter_x[h * cut : (h + 1) * cut]
        matrix_x.append(lax.all_gather(share, "gx", axis=0, tiled=True))
    starts = []
    for h in range(CHUNKS):
        planes = []
        for w in range(CHUNKS):
            smoothed = jnp.dot(matrix_x[h], lines[w], preferred_element_type=F32)
            smoothed = smoothed.astype(BF16).reshape(n_x, cut, piece)
            planes.append(plane_pieces(smoothed, parts))
        start = y_filter(planes, filter_y, None, parts, False)
        if h == CHUNKS - 1:
            start, filter_y = lax.optimization_barrier((start, filter_y))
            sent_y = send_columns(filter_y, parts)
        came = swap_all(start).reshape(levels, parts, cut, part)
        came = came.transpose(2, 0, 1, 3).reshape(cut, levels, width)
        starts.append(came)

    rows_in = row_halo(starts[0][0], starts[-1][-1]).astype(F32)
    before, after = side_halo(
        jnp.concatenate([s[:, :, 0] for s in starts]),
        jnp.concatenate([s[:, :, -1] for s in starts]),
    )
    sides = jnp.stack([before, after], axis=2).astype(F32)
    end_state, flat, row_flux, side_flux = forward(
        starts, rows_in, sides, innovation, obs_weight, courant_x, courant_y
    )
    rows_in = row_halo(row_flux[0], row_flux[1])
    before, after = side_halo(side_flux[:, :, 0], side_flux[:, :, 1])
    sides = jnp.stack([before, after], axis=2)
    flat, sent_y = lax.optimization_barrier((flat, sent_y))

    pulled = []
    for w in range(CHUNKS):
        adjoint = swap_all(rim_lines(flat, rows_in, sides, parts, w))
        adjoint = adjoint.reshape(n_x, CHUNKS, cut, piece)
        total = 0.0
        for h in range(CHUNKS):
            total = total + jnp.einsum(
                "ij,ic->jc",
                matrix_x[h],
                adjoint[:, h].reshape(n_x * cut, piece),
                preferred_element_type=F32,
            )
        pulled.append(total.astype(BF16).reshape(n_x, CHUNKS, cut, piece))
    gradient = far = None
    for h in range(CHUNKS):
        planes = []
        for w in range(CHUNKS):
            held = far if h > 0 and w == CHUNKS - 1 else None
            planes.append(plane_pieces(pulled[w][:, h], parts, held))
            far = planes[w][-2] if w == CHUNKS - 1 else far
        carried = swap_all(y_filter(planes, filter_y, sent_y, parts, True))
        gradient = add_lines(control, carried, parts, h, gradient)
    return (end_state, gradient)


def solution(mesh):
    placed = (
        P("gx", None, "gy"),
        P("gx", None, "gy"),
        P("gx", None, "gy"),
        P("gx", None, "gy"),
        P("gx", None, "gy"),
        P("gx", None),
        P("gy", None),
    )
    return jax.shard_map(
        per_device,
        mesh=mesh,
        in_specs=placed,
        out_specs=(P("gx", None, "gy"), P("gx", None, "gy")),
        check_vma=False,
    )
```

```python
import functools

import jax
import jax.numpy as jnp
from jax import lax
from jax.experimental import pallas as pl
from jax.experimental.pallas import tpu as pltpu
from jax.sharding import PartitionSpec as P

BF16 = jnp.bfloat16
F32 = jnp.float32
STEP = 32
TILE = 16
GROUP = 8
CHUNKS = 2
PARAMS = pltpu.CompilerParams(vmem_limit_bytes=56 * 1024 * 1024)


def cost(flops, *arrays):
    return pl.CostEstimate(
        flops=flops,
        bytes_accessed=sum(a.size * a.dtype.itemsize for a in arrays),
        transcendentals=0,
    )


def chunk_spans(width, parts, chunk):
    part = width // parts
    piece = part // CHUNKS
    return [
        slice(s * part + chunk * piece, s * part + (chunk + 1) * piece)
        for s in range(parts)
    ]


def store_lines(turned, out, parts):
    piece = out.shape[2]

    @pl.loop(0, turned.shape[0] // TILE)
    def _(tile):
        at = pl.ds(tile * TILE, TILE)
        for l in range(turned.shape[1]):
            for s in range(parts):
                got = turned[at, l, s * piece : (s + 1) * piece]
                out[l * parts + s, at] = got.astype(BF16)


def lines_body(parts, chunk, block, out, turned):
    piece = out.shape[2]
    for s, span in enumerate(chunk_spans(block.shape[2], parts, chunk)):
        turned[:, :, s * piece : (s + 1) * piece] = block[:, :, span].astype(F32)
    store_lines(turned, out, parts)


def as_lines(block, parts, chunk):
    rows, levels, width = block.shape
    shape = (levels * parts, rows, width // parts // CHUNKS)
    return pl.pallas_call(
        functools.partial(lines_body, parts, chunk),
        grid=(rows // STEP,),
        in_specs=[pl.BlockSpec((STEP, levels, width), lambda i: (i, 0, 0))],
        out_specs=pl.BlockSpec((shape[0], STEP, shape[2]), lambda i: (0, i, 0)),
        out_shape=jax.ShapeDtypeStruct(shape, BF16),
        scratch_shapes=[pltpu.VMEM((STEP, levels, width // CHUNKS), F32)],
        compiler_params=PARAMS,
        cost_estimate=cost(0, block, block),
        name="as_lines",
    )(block)


def gradient_body(parts, lines, control, *rest):
    out, turned = rest[-2:]
    levels, width = control.shape[1:]
    part = width // parts
    for l in range(levels):
        for s in range(parts):
            turned[:, l, s * part : (s + 1) * part] = lines[l * parts + s].astype(F32)
    out[...] = control[...].astype(F32) + turned[...]


def add_lines(control, lines, parts, first, target):
    rows, levels, width = control.shape
    whole = (TILE, levels, width)
    cut = lines.shape[1]
    offset = first // TILE
    operands = [lines, control] + ([] if target is None else [target])
    return pl.pallas_call(
        functools.partial(gradient_body, parts),
        grid=(cut // TILE,),
        in_specs=[
            pl.BlockSpec((lines.shape[0], TILE, lines.shape[2]), lambda i: (0, i, 0)),
            pl.BlockSpec(whole, lambda i: (i + offset, 0, 0)),
        ]
        + [pl.BlockSpec(memory_space=pl.ANY)] * (len(operands) - 2),
        out_specs=pl.BlockSpec(whole, lambda i: (i + offset, 0, 0)),
        out_shape=jax.ShapeDtypeStruct(control.shape, F32),
        input_output_aliases={} if target is None else {2: 0},
        scratch_shapes=[pltpu.VMEM(whole, F32)],
        compiler_params=PARAMS,
        cost_estimate=cost(control.size // 2, control, control),
        name="add_lines",
    )(*operands)


def forward_body(*refs):
    starts = refs[:CHUNKS]
    rows_in, sides, innovation, weight, wind_x, wind_y = refs[CHUNKS : CHUNKS + 6]
    end, flat, row_flux, side_flux, state, carry = refs[CHUNKS + 6 :]
    step = pl.program_id(0)
    rows, levels, width = flat.shape
    cut = rows // CHUNKS

    @pl.when(step == 0)
    def _():
        state[pl.ds(0, 1)] = rows_in[pl.ds(0, 1)]
        state[pl.ds(rows + 1, 1)] = rows_in[pl.ds(1, 1)]
        for h in range(CHUNKS):
            state[pl.ds(1 + h * cut, cut)] = starts[h][...].astype(F32)
        carry[...] = jnp.zeros(carry.shape, F32)

    first = step * STEP
    place = lax.broadcasted_iota(jnp.int32, (GROUP, levels, width), 2)
    left_edge, right_edge = place == 0, place == width - 1
    @pl.loop(0, STEP // GROUP)
    def _(group):
        j = group * GROUP
        rows_j, at = pl.ds(j, GROUP), first + j
        here = state[pl.ds(at + 1, GROUP)]
        cx, cy = wind_x[rows_j], wind_y[rows_j]
        left = jnp.where(left_edge, sides[rows_j, :, 0:1], pltpu.roll(here, 1, 2))
        right = jnp.where(
            right_edge, sides[rows_j, :, 1:2], pltpu.roll(here, width - 1, 2)
        )
        dx = state[pl.ds(at + 2, GROUP)] - state[pl.ds(at, GROUP)]
        after = here - cx * dx * 0.5 - cy * (right - left) * 0.5
        end[rows_j] = after
        misfit = weight[rows_j] * (after - innovation[rows_j])
        p, q = cy * misfit, cx * misfit
        side_flux[rows_j, :, 0:1] = p[:, :, 0:1]
        side_flux[rows_j, :, 1:2] = p[:, :, width - 1 : width]
        left = jnp.where(left_edge, 0.0, pltpu.roll(p, 1, 2))
        right = jnp.where(right_edge, 0.0, pltpu.roll(p, width - 1, 2))
        flat_j = misfit + 0.5 * (right - left)
        flat[jnp.maximum(at - 1, 0)] = carry[2] + 0.5 * (q[0] - carry[0])
        flat[at] = flat_j[0] + 0.5 * (q[1] - carry[1])
        flat[pl.ds(at + 1, GROUP - 2)] = flat_j[1:-1] + 0.5 * (q[2:] - q[:-2])

        @pl.when(at == 0)
        def _():
            row_flux[0] = q[0]

        carry[0], carry[1], carry[2] = q[GROUP - 2], q[GROUP - 1], flat_j[GROUP - 1]

    @pl.when(step == rows // STEP - 1)
    def _():
        flat[rows - 1] = carry[2] - 0.5 * carry[0]
        row_flux[1] = carry[1]


def forward(starts, rows_in, sides, innovation, weight, wind_x, wind_y):
    rows, levels, width = innovation.shape
    blocked = pl.BlockSpec((STEP, levels, width), lambda i: (i, 0, 0))
    side = pl.BlockSpec((STEP, levels, 2), lambda i: (i, 0, 0))
    pair = pl.BlockSpec((2, levels, width), lambda i: (0, 0, 0))
    start = pl.BlockSpec(starts[0].shape, lambda i: (0, 0, 0))
    whole = pl.BlockSpec((rows, levels, width), lambda i: (0, 0, 0))
    return pl.pallas_call(
        forward_body,
        grid=(rows // STEP,),
        in_specs=[start] * CHUNKS + [pair, side, blocked, blocked, blocked, blocked],
        out_specs=[blocked, whole, pair, side],
        out_shape=[
            jax.ShapeDtypeStruct((rows, levels, width), F32),
            jax.ShapeDtypeStruct((rows, levels, width), F32),
            jax.ShapeDtypeStruct((2, levels, width), F32),
            jax.ShapeDtypeStruct((rows, levels, 2), F32),
        ],
        scratch_shapes=[
            pltpu.VMEM((rows + 2, levels, width), F32),
            pltpu.VMEM((3, levels, width), F32),
        ],
        compiler_params=PARAMS,
        cost_estimate=cost(30 * innovation.size, *[innovation] * 7),
        name="forward",
    )(*starts, rows_in, sides, innovation, weight, wind_x, wind_y)


def rim_body(parts, chunk, last, flat, rows_in, sides, out, turned):
    step = pl.program_id(0)
    levels, width = flat.shape[1:]
    piece = out.shape[2]
    place = lax.broadcasted_iota(jnp.int32, (STEP, levels, piece), 2)
    spans = chunk_spans(width, parts, chunk)
    for s, span in enumerate(spans):
        value = flat[:, :, span]
        if span.start == 0:
            value = value - jnp.where(place == 0, 0.5 * sides[:, :, 0:1], 0.0)
        if span.stop == width:
            value = value + jnp.where(place == piece - 1, 0.5 * sides[:, :, 1:2], 0.0)
        turned[:, :, s * piece : (s + 1) * piece] = value

    @pl.when(step == 0)
    def _():
        for s, span in enumerate(spans):
            at = slice(s * piece, (s + 1) * piece)
            turned[0, :, at] += -0.5 * rows_in[0, :, span]

    @pl.when(step == last)
    def _():
        for s, span in enumerate(spans):
            at = slice(s * piece, (s + 1) * piece)
            turned[STEP - 1, :, at] += 0.5 * rows_in[1, :, span]

    store_lines(turned, out, parts)


def rim_lines(flat, rows_in, sides, parts, chunk):
    rows, levels, width = flat.shape
    shape = (levels * parts, rows, width // parts // CHUNKS)
    return pl.pallas_call(
        functools.partial(rim_body, parts, chunk, rows // STEP - 1),
        grid=(rows // STEP,),
        in_specs=[
            pl.BlockSpec((STEP, levels, width), lambda i: (i, 0, 0)),
            pl.BlockSpec((2, levels, width), lambda i: (0, 0, 0)),
            pl.BlockSpec((STEP, levels, 2), lambda i: (i, 0, 0)),
        ],
        out_specs=pl.BlockSpec((shape[0], STEP, shape[2]), lambda i: (0, i, 0)),
        out_shape=jax.ShapeDtypeStruct(shape, BF16),
        scratch_shapes=[pltpu.VMEM((STEP, levels, width // CHUNKS), F32)],
        compiler_params=PARAMS,
        cost_estimate=cost(4 * flat.size, flat, flat),
        name="rim_lines",
    )(flat, rows_in, sides)


def swap_all(lines):
    return lax.all_to_all(lines, "gx", 0, 0, tiled=True)


def plane_pieces(lines, parts, after=None, near_first=False):
    n_x, n_y = lax.axis_size("gx"), lax.axis_size("gy")
    groups = [list(range(i, i + parts)) for i in range(0, n_x, parts)]
    if n_y == 2 and parts == 2:
        pairs = [(a, b) for g in groups for a, b in (g, g[::-1])]
        sent = lines if after is None else lax.optimization_barrier((lines, after))[0]
        far = lax.ppermute(sent, "gy", [(0, 1), (1, 0)])
        near = lax.ppermute(lines, "gx", pairs)
        if near_first:
            far, near = lax.optimization_barrier((far, near))
        cross = lax.ppermute(far, "gx", pairs)
        return [lines, near, far, cross]
    plane = lax.all_gather(lines, "gy", axis=0, tiled=False)
    plane = lax.all_gather(plane, "gx", axis=0, tiled=False, axis_index_groups=groups)
    return [plane[s, g] for s in range(parts) for g in range(n_y)]


def piece_order(parts):
    n_y = lax.axis_size("gy")
    sub, me = lax.rem(lax.axis_index("gx"), parts), lax.axis_index("gy")
    if n_y == 2 and parts == 2:
        return [(sub, me), (1 - sub, me), (sub, 1 - me), (1 - sub, 1 - me)]
    return [(s, g) for s in range(parts) for g in range(n_y)]


def filter_rows(filter_y, parts):
    width = filter_y.shape[0]
    part = width // parts
    sub = lax.rem(lax.axis_index("gx"), parts)
    return [
        lax.dynamic_slice(filter_y, (sub * part, g * width + s * part), (part, part))
        for s, g in piece_order(parts)
    ]


def send_columns(filter_y, parts):
    width, n_y = filter_y.shape[0], lax.axis_size("gy")
    part = width // parts
    sub, me = lax.rem(lax.axis_index("gx"), parts), lax.axis_index("gy")
    if n_y == 2 and parts == 2:
        sent = lax.dynamic_slice(
            filter_y, (0, (1 - me) * width + sub * part), (width, part)
        )
        return lax.ppermute(sent, "gy", [(0, 1), (1, 0)])
    split = filter_y.reshape(width, n_y, parts, part)
    split = lax.dynamic_index_in_dim(split, sub, axis=2, keepdims=False)
    return lax.all_to_all(split, "gy", 1, 0, tiled=True)


def filter_columns(filter_y, got, parts):
    width, n_y = filter_y.shape[0], lax.axis_size("gy")
    part = width // parts
    sub, me = lax.rem(lax.axis_index("gx"), parts), lax.axis_index("gy")
    order = piece_order(parts)
    if n_y == 2 and parts == 2:
        mine = lax.dynamic_slice(filter_y, (0, me * width + sub * part), (width, part))
        return [
            lax.dynamic_slice_in_dim(source, s * part, part, axis=0)
            for source, (s, _) in zip((mine, mine, got, got), order)
        ]
    split = got.reshape(n_y, parts, part, part)
    return [split[g, s] for s, g in order]


def row_halo(first, last):
    n_x = lax.axis_size("gx")
    up = [(i, i + 1) for i in range(n_x - 1)]
    down = [(i + 1, i) for i in range(n_x - 1)]
    return jnp.stack([lax.ppermute(last, "gx", up), lax.ppermute(first, "gx", down)])


def side_halo(first, last):
    n_y, me = lax.axis_size("gy"), lax.axis_index("gy")
    if n_y == 2:
        got = lax.ppermute(jnp.where(me == 0, last, first), "gy", [(0, 1), (1, 0)])
        none = jnp.zeros_like(got)
        return jnp.where(me == 0, none, got), jnp.where(me == 0, got, none)
    up = [(i, i + 1) for i in range(n_y - 1)]
    down = [(i + 1, i) for i in range(n_y - 1)]
    return lax.ppermute(last, "gy", up), lax.ppermute(first, "gy", down)


def per_device(control, innovation, obs_weight, courant_x, courant_y, filter_x, filter_y):
    rows, levels, width = control.shape
    n_x = lax.axis_size("gx")
    parts = n_x // levels
    part = width // parts
    cut, piece = rows // CHUNKS, part // CHUNKS
    spans = [slice(w * piece, (w + 1) * piece) for w in range(CHUNKS)]

    rows_y = filter_rows(filter_y, parts)
    matrix_x = [lax.all_gather(filter_x[:cut], "gx", axis=0, tiled=True)]
    lines = [swap_all(as_lines(control, parts, w)) for w in range(CHUNKS)]
    lines = [l.reshape(n_x * rows, piece) for l in lines]
    lines[-1], filter_x = lax.optimization_barrier((lines[-1], filter_x))
    for h in range(1, CHUNKS):
        share = filter_x[h * cut : (h + 1) * cut]
        matrix_x.append(lax.all_gather(share, "gx", axis=0, tiled=True))
    starts = []
    for h in range(CHUNKS):
        start = 0.0
        for w, span in enumerate(spans):
            smoothed = jnp.dot(matrix_x[h], lines[w], preferred_element_type=F32)
            smoothed = smoothed.astype(BF16).reshape(n_x, cut, piece)
            for plane, matrix in zip(plane_pieces(smoothed, parts), rows_y):
                start = start + jnp.einsum(
                    "brc,kc->brk", plane, matrix[:, span], preferred_element_type=F32
                )
        start = start.astype(BF16)
        if h == CHUNKS - 1:
            start, filter_y = lax.optimization_barrier((start, filter_y))
            columns_y = send_columns(filter_y, parts)
        came = swap_all(start).reshape(levels, parts, cut, part)
        came = came.transpose(2, 0, 1, 3).reshape(cut, levels, width)
        starts.append(came)

    rows_in = row_halo(starts[0][0], starts[-1][-1]).astype(F32)
    before, after = side_halo(
        jnp.concatenate([s[:, :, 0] for s in starts]),
        jnp.concatenate([s[:, :, -1] for s in starts]),
    )
    sides = jnp.stack([before, after], axis=2).astype(F32)
    end_state, flat, row_flux, side_flux = forward(
        starts, rows_in, sides, innovation, obs_weight, courant_x, courant_y
    )
    rows_in = row_halo(row_flux[0], row_flux[1])
    before, after = side_halo(side_flux[:, :, 0], side_flux[:, :, 1])
    sides = jnp.stack([before, after], axis=2)
    flat, columns_y = lax.optimization_barrier((flat, columns_y))
    columns_y = filter_columns(filter_y, columns_y, parts)

    pulled = []
    for w in range(CHUNKS):
        adjoint = swap_all(rim_lines(flat, rows_in, sides, parts, w))
        adjoint = adjoint.reshape(n_x, CHUNKS, cut, piece)
        total = 0.0
        for h in range(CHUNKS):
            total = total + jnp.einsum(
                "ij,ic->jc",
                matrix_x[h],
                adjoint[:, h].reshape(n_x * cut, piece),
                preferred_element_type=F32,
            )
        pulled.append(total.astype(BF16).reshape(n_x, rows, piece))
    gradient = far = None
    for h, (at, end) in enumerate(((0, rows // 4), (rows // 4, rows))):
        carried = 0.0
        for w, span in enumerate(spans):
            last = w == CHUNKS - 1
            held = far if h > 0 and last else None
            planes = plane_pieces(pulled[w][:, at:end], parts, held, h == 0 and last)
            far = planes[-2] if last else far
            for plane, matrix in zip(planes, columns_y):
                carried = carried + jnp.einsum(
                    "brk,kc->brc", plane, matrix[span], preferred_element_type=F32
                )
        carried = swap_all(carried.astype(BF16))
        gradient = add_lines(control, carried, parts, at, gradient)
    return (end_state, gradient)


def solution(mesh):
    placed = (
        P("gx", None, "gy"),
        P("gx", None, "gy"),
        P("gx", None, "gy"),
        P("gx", None, "gy"),
        P("gx", None, "gy"),
        P("gx", None),
        P("gy", None),
    )
    return jax.shard_map(
        per_device,
        mesh=mesh,
        in_specs=placed,
        out_specs=(P("gx", None, "gy"), P("gx", None, "gy")),
        check_vma=False,
    )
```

```python
import functools

import jax
import jax.numpy as jnp
from jax import lax
from jax.experimental import pallas as pl
from jax.experimental.pallas import tpu as pltpu
from jax.sharding import PartitionSpec as P

BF16 = jnp.bfloat16
F32 = jnp.float32
STEP = 32
TILE = 16
GROUP = 8
CHUNKS = 2
PARAMS = pltpu.CompilerParams(vmem_limit_bytes=56 * 1024 * 1024)


def cost(flops, *arrays):
    return pl.CostEstimate(
        flops=flops,
        bytes_accessed=sum(a.size * a.dtype.itemsize for a in arrays),
        transcendentals=0,
    )


def chunk_spans(width, parts, chunk):
    part = width // parts
    piece = part // CHUNKS
    return [
        slice(s * part + chunk * piece, s * part + (chunk + 1) * piece)
        for s in range(parts)
    ]


def store_lines(turned, out, parts):
    piece = out.shape[2]

    @pl.loop(0, turned.shape[0] // TILE)
    def _(tile):
        at = pl.ds(tile * TILE, TILE)
        for l in range(turned.shape[1]):
            for s in range(parts):
                got = turned[at, l, s * piece : (s + 1) * piece]
                out[l * parts + s, at] = got.astype(BF16)


def lines_body(parts, chunk, block, out, turned):
    piece = out.shape[2]
    for s, span in enumerate(chunk_spans(block.shape[2], parts, chunk)):
        turned[:, :, s * piece : (s + 1) * piece] = block[:, :, span].astype(F32)
    store_lines(turned, out, parts)


def as_lines(block, parts, chunk):
    rows, levels, width = block.shape
    shape = (levels * parts, rows, width // parts // CHUNKS)
    return pl.pallas_call(
        functools.partial(lines_body, parts, chunk),
        grid=(rows // STEP,),
        in_specs=[pl.BlockSpec((STEP, levels, width), lambda i: (i, 0, 0))],
        out_specs=pl.BlockSpec((shape[0], STEP, shape[2]), lambda i: (0, i, 0)),
        out_shape=jax.ShapeDtypeStruct(shape, BF16),
        scratch_shapes=[pltpu.VMEM((STEP, levels, width // CHUNKS), F32)],
        compiler_params=PARAMS,
        cost_estimate=cost(0, block, block),
        name="as_lines",
    )(block)


def gradient_body(parts, lines, control, *rest):
    out, turned = rest[-2:]
    levels, width = control.shape[1:]
    part = width // parts

    @pl.loop(0, STEP // TILE)
    def _(tile):
        at = pl.ds(tile * TILE, TILE)
        for l in range(levels):
            for s in range(parts):
                got = lines[l * parts + s, at].astype(F32)
                turned[at, l, s * part : (s + 1) * part] = got

    out[...] = control[...].astype(F32) + turned[...]


def add_lines(control, lines, parts, first, target):
    rows, levels, width = control.shape
    whole = (STEP, levels, width)
    cut = lines.shape[1]
    offset = first // STEP
    operands = [lines, control] + ([] if target is None else [target])
    return pl.pallas_call(
        functools.partial(gradient_body, parts),
        grid=(cut // STEP,),
        in_specs=[
            pl.BlockSpec((lines.shape[0], STEP, lines.shape[2]), lambda i: (0, i, 0)),
            pl.BlockSpec(whole, lambda i: (i + offset, 0, 0)),
        ]
        + [pl.BlockSpec(memory_space=pl.ANY)] * (len(operands) - 2),
        out_specs=pl.BlockSpec(whole, lambda i: (i + offset, 0, 0)),
        out_shape=jax.ShapeDtypeStruct(control.shape, F32),
        input_output_aliases={} if target is None else {2: 0},
        scratch_shapes=[pltpu.VMEM(whole, F32)],
        compiler_params=PARAMS,
        cost_estimate=cost(control.size // 2, control, control),
        name="add_lines",
    )(*operands)


def forward_body(*refs):
    starts = refs[:CHUNKS]
    rows_in, sides, innovation, weight, wind_x, wind_y = refs[CHUNKS : CHUNKS + 6]
    end, flat, row_flux, side_flux, state, carry = refs[CHUNKS + 6 :]
    step = pl.program_id(0)
    rows, levels, width = flat.shape
    cut = rows // CHUNKS

    @pl.when(step == 0)
    def _():
        state[pl.ds(0, 1)] = rows_in[pl.ds(0, 1)]
        state[pl.ds(rows + 1, 1)] = rows_in[pl.ds(1, 1)]
        for h in range(CHUNKS):
            state[pl.ds(1 + h * cut, cut)] = starts[h][...].astype(F32)
        carry[...] = jnp.zeros(carry.shape, F32)

    first = step * STEP
    place = lax.broadcasted_iota(jnp.int32, (GROUP, levels, width), 2)
    left_edge, right_edge = place == 0, place == width - 1
    @pl.loop(0, STEP // GROUP)
    def _(group):
        j = group * GROUP
        rows_j, at = pl.ds(j, GROUP), first + j
        here = state[pl.ds(at + 1, GROUP)]
        cx, cy = wind_x[rows_j], wind_y[rows_j]
        left = jnp.where(left_edge, sides[rows_j, :, 0:1], pltpu.roll(here, 1, 2))
        right = jnp.where(
            right_edge, sides[rows_j, :, 1:2], pltpu.roll(here, width - 1, 2)
        )
        dx = state[pl.ds(at + 2, GROUP)] - state[pl.ds(at, GROUP)]
        after = here - cx * dx * 0.5 - cy * (right - left) * 0.5
        end[rows_j] = after
        misfit = weight[rows_j] * (after - innovation[rows_j])
        p, q = cy * misfit, cx * misfit
        side_flux[rows_j, :, 0:1] = p[:, :, 0:1]
        side_flux[rows_j, :, 1:2] = p[:, :, width - 1 : width]
        left = jnp.where(left_edge, 0.0, pltpu.roll(p, 1, 2))
        right = jnp.where(right_edge, 0.0, pltpu.roll(p, width - 1, 2))
        flat_j = misfit + 0.5 * (right - left)
        flat[jnp.maximum(at - 1, 0)] = carry[2] + 0.5 * (q[0] - carry[0])
        flat[at] = flat_j[0] + 0.5 * (q[1] - carry[1])
        flat[pl.ds(at + 1, GROUP - 2)] = flat_j[1:-1] + 0.5 * (q[2:] - q[:-2])

        @pl.when(at == 0)
        def _():
            row_flux[0] = q[0]

        carry[0], carry[1], carry[2] = q[GROUP - 2], q[GROUP - 1], flat_j[GROUP - 1]

    @pl.when(step == rows // STEP - 1)
    def _():
        flat[rows - 1] = carry[2] - 0.5 * carry[0]
        row_flux[1] = carry[1]


def forward(starts, rows_in, sides, innovation, weight, wind_x, wind_y):
    rows, levels, width = innovation.shape
    blocked = pl.BlockSpec((STEP, levels, width), lambda i: (i, 0, 0))
    side = pl.BlockSpec((STEP, levels, 2), lambda i: (i, 0, 0))
    pair = pl.BlockSpec((2, levels, width), lambda i: (0, 0, 0))
    start = pl.BlockSpec(starts[0].shape, lambda i: (0, 0, 0))
    whole = pl.BlockSpec((rows, levels, width), lambda i: (0, 0, 0))
    return pl.pallas_call(
        forward_body,
        grid=(rows // STEP,),
        in_specs=[start] * CHUNKS + [pair, side, blocked, blocked, blocked, blocked],
        out_specs=[blocked, whole, pair, side],
        out_shape=[
            jax.ShapeDtypeStruct((rows, levels, width), F32),
            jax.ShapeDtypeStruct((rows, levels, width), F32),
            jax.ShapeDtypeStruct((2, levels, width), F32),
            jax.ShapeDtypeStruct((rows, levels, 2), F32),
        ],
        scratch_shapes=[
            pltpu.VMEM((rows + 2, levels, width), F32),
            pltpu.VMEM((3, levels, width), F32),
        ],
        compiler_params=PARAMS,
        cost_estimate=cost(30 * innovation.size, *[innovation] * 7),
        name="forward",
    )(*starts, rows_in, sides, innovation, weight, wind_x, wind_y)


def rim_body(parts, chunk, last, flat, rows_in, sides, out, turned):
    step = pl.program_id(0)
    levels, width = flat.shape[1:]
    piece = out.shape[2]
    place = lax.broadcasted_iota(jnp.int32, (STEP, levels, piece), 2)
    spans = chunk_spans(width, parts, chunk)
    for s, span in enumerate(spans):
        value = flat[:, :, span]
        if span.start == 0:
            value = value - jnp.where(place == 0, 0.5 * sides[:, :, 0:1], 0.0)
        if span.stop == width:
            value = value + jnp.where(place == piece - 1, 0.5 * sides[:, :, 1:2], 0.0)
        turned[:, :, s * piece : (s + 1) * piece] = value

    @pl.when(step == 0)
    def _():
        for s, span in enumerate(spans):
            at = slice(s * piece, (s + 1) * piece)
            turned[0, :, at] += -0.5 * rows_in[0, :, span]

    @pl.when(step == last)
    def _():
        for s, span in enumerate(spans):
            at = slice(s * piece, (s + 1) * piece)
            turned[STEP - 1, :, at] += 0.5 * rows_in[1, :, span]

    store_lines(turned, out, parts)


def rim_lines(flat, rows_in, sides, parts, chunk):
    rows, levels, width = flat.shape
    shape = (levels * parts, rows, width // parts // CHUNKS)
    return pl.pallas_call(
        functools.partial(rim_body, parts, chunk, rows // STEP - 1),
        grid=(rows // STEP,),
        in_specs=[
            pl.BlockSpec((STEP, levels, width), lambda i: (i, 0, 0)),
            pl.BlockSpec((2, levels, width), lambda i: (0, 0, 0)),
            pl.BlockSpec((STEP, levels, 2), lambda i: (i, 0, 0)),
        ],
        out_specs=pl.BlockSpec((shape[0], STEP, shape[2]), lambda i: (0, i, 0)),
        out_shape=jax.ShapeDtypeStruct(shape, BF16),
        scratch_shapes=[pltpu.VMEM((STEP, levels, width // CHUNKS), F32)],
        compiler_params=PARAMS,
        cost_estimate=cost(4 * flat.size, flat, flat),
        name="rim_lines",
    )(flat, rows_in, sides)


def swap_all(lines):
    return lax.all_to_all(lines, "gx", 0, 0, tiled=True)


def plane_pieces(lines, parts, after=None, near_first=False):
    n_x, n_y = lax.axis_size("gx"), lax.axis_size("gy")
    groups = [list(range(i, i + parts)) for i in range(0, n_x, parts)]
    if n_y == 2 and parts == 2:
        pairs = [(a, b) for g in groups for a, b in (g, g[::-1])]
        sent = lines if after is None else lax.optimization_barrier((lines, after))[0]
        far = lax.ppermute(sent, "gy", [(0, 1), (1, 0)])
        near = lax.ppermute(lines, "gx", pairs)
        if near_first:
            far, near = lax.optimization_barrier((far, near))
        cross = lax.ppermute(far, "gx", pairs)
        return [lines, near, far, cross]
    plane = lax.all_gather(lines, "gy", axis=0, tiled=False)
    plane = lax.all_gather(plane, "gx", axis=0, tiled=False, axis_index_groups=groups)
    return [plane[s, g] for s in range(parts) for g in range(n_y)]


def piece_order(parts):
    n_y = lax.axis_size("gy")
    sub, me = lax.rem(lax.axis_index("gx"), parts), lax.axis_index("gy")
    if n_y == 2 and parts == 2:
        return [(sub, me), (1 - sub, me), (sub, 1 - me), (1 - sub, 1 - me)]
    return [(s, g) for s in range(parts) for g in range(n_y)]


def filter_rows(filter_y, parts):
    width = filter_y.shape[0]
    part = width // parts
    sub = lax.rem(lax.axis_index("gx"), parts)
    return [
        lax.dynamic_slice(filter_y, (sub * part, g * width + s * part), (part, part))
        for s, g in piece_order(parts)
    ]


def send_columns(filter_y, parts):
    width, n_y = filter_y.shape[0], lax.axis_size("gy")
    part = width // parts
    sub, me = lax.rem(lax.axis_index("gx"), parts), lax.axis_index("gy")
    if n_y == 2 and parts == 2:
        sent = lax.dynamic_slice(
            filter_y, (0, (1 - me) * width + sub * part), (width, part)
        )
        return lax.ppermute(sent, "gy", [(0, 1), (1, 0)])
    split = filter_y.reshape(width, n_y, parts, part)
    split = lax.dynamic_index_in_dim(split, sub, axis=2, keepdims=False)
    return lax.all_to_all(split, "gy", 1, 0, tiled=True)


def filter_columns(filter_y, got, parts):
    width, n_y = filter_y.shape[0], lax.axis_size("gy")
    part = width // parts
    sub, me = lax.rem(lax.axis_index("gx"), parts), lax.axis_index("gy")
    order = piece_order(parts)
    if n_y == 2 and parts == 2:
        mine = lax.dynamic_slice(filter_y, (0, me * width + sub * part), (width, part))
        return [
            lax.dynamic_slice_in_dim(source, s * part, part, axis=0)
            for source, (s, _) in zip((mine, mine, got, got), order)
        ]
    split = got.reshape(n_y, parts, part, part)
    return [split[g, s] for s, g in order]


def row_halo(first, last):
    n_x = lax.axis_size("gx")
    up = [(i, i + 1) for i in range(n_x - 1)]
    down = [(i + 1, i) for i in range(n_x - 1)]
    return jnp.stack([lax.ppermute(last, "gx", up), lax.ppermute(first, "gx", down)])


def side_halo(first, last):
    n_y, me = lax.axis_size("gy"), lax.axis_index("gy")
    if n_y == 2:
        got = lax.ppermute(jnp.where(me == 0, last, first), "gy", [(0, 1), (1, 0)])
        none = jnp.zeros_like(got)
        return jnp.where(me == 0, none, got), jnp.where(me == 0, got, none)
    up = [(i, i + 1) for i in range(n_y - 1)]
    down = [(i + 1, i) for i in range(n_y - 1)]
    return lax.ppermute(last, "gy", up), lax.ppermute(first, "gy", down)


def per_device(control, innovation, obs_weight, courant_x, courant_y, filter_x, filter_y):
    rows, levels, width = control.shape
    n_x = lax.axis_size("gx")
    parts = n_x // levels
    part = width // parts
    cut, piece = rows // CHUNKS, part // CHUNKS
    spans = [slice(w * piece, (w + 1) * piece) for w in range(CHUNKS)]

    rows_y = filter_rows(filter_y, parts)
    matrix_x = [lax.all_gather(filter_x[:cut], "gx", axis=0, tiled=True)]
    lines = [swap_all(as_lines(control, parts, w)) for w in range(CHUNKS)]
    lines = [l.reshape(n_x * rows, piece) for l in lines]
    lines[-1], filter_x = lax.optimization_barrier((lines[-1], filter_x))
    for h in range(1, CHUNKS):
        share = filter_x[h * cut : (h + 1) * cut]
        matrix_x.append(lax.all_gather(share, "gx", axis=0, tiled=True))
    starts = []
    for h in range(CHUNKS):
        start = 0.0
        for w, span in enumerate(spans):
            smoothed = jnp.dot(matrix_x[h], lines[w], preferred_element_type=F32)
            smoothed = smoothed.astype(BF16).reshape(n_x, cut, piece)
            for plane, matrix in zip(plane_pieces(smoothed, parts), rows_y):
                start = start + jnp.einsum(
                    "brc,kc->brk", plane, matrix[:, span], preferred_element_type=F32
                )
        start = start.astype(BF16)
        if h == CHUNKS - 1:
            start, filter_y = lax.optimization_barrier((start, filter_y))
            columns_y = send_columns(filter_y, parts)
        came = swap_all(start).reshape(levels, parts, cut, part)
        came = came.transpose(2, 0, 1, 3).reshape(cut, levels, width)
        starts.append(came)

    rows_in = row_halo(starts[0][0], starts[-1][-1]).astype(F32)
    before, after = side_halo(
        jnp.concatenate([s[:, :, 0] for s in starts]),
        jnp.concatenate([s[:, :, -1] for s in starts]),
    )
    sides = jnp.stack([before, after], axis=2).astype(F32)
    end_state, flat, row_flux, side_flux = forward(
        starts, rows_in, sides, innovation, obs_weight, courant_x, courant_y
    )
    rows_in = row_halo(row_flux[0], row_flux[1])
    before, after = side_halo(side_flux[:, :, 0], side_flux[:, :, 1])
    sides = jnp.stack([before, after], axis=2)
    flat, columns_y = lax.optimization_barrier((flat, columns_y))
    columns_y = filter_columns(filter_y, columns_y, parts)

    pulled = []
    for w in range(CHUNKS):
        adjoint = swap_all(rim_lines(flat, rows_in, sides, parts, w))
        adjoint = adjoint.reshape(n_x, CHUNKS, cut, piece)
        total = 0.0
        for h in range(CHUNKS):
            total = total + jnp.einsum(
                "ij,ic->jc",
                matrix_x[h],
                adjoint[:, h].reshape(n_x * cut, piece),
                preferred_element_type=F32,
            )
        pulled.append(total.astype(BF16).reshape(n_x, rows, piece))
    gradient = far = None
    for h in range(CHUNKS):
        at, end = h * cut, (h + 1) * cut
        carried = 0.0
        for w, span in enumerate(spans):
            last = w == CHUNKS - 1
            held = far if h > 0 and last else None
            planes = plane_pieces(pulled[w][:, at:end], parts, held, h == 0 and last)
            far = planes[-2] if last else far
            for plane, matrix in zip(planes, columns_y):
                carried = carried + jnp.einsum(
                    "brk,kc->brc", plane, matrix[span], preferred_element_type=F32
                )
        carried = swap_all(carried.astype(BF16))
        gradient = add_lines(control, carried, parts, at, gradient)
    return (end_state, gradient)


def solution(mesh):
    placed = (
        P("gx", None, "gy"),
        P("gx", None, "gy"),
        P("gx", None, "gy"),
        P("gx", None, "gy"),
        P("gx", None, "gy"),
        P("gx", None),
        P("gy", None),
    )
    return jax.shard_map(
        per_device,
        mesh=mesh,
        in_specs=placed,
        out_specs=(P("gx", None, "gy"), P("gx", None, "gy")),
        check_vma=False,
    )
```

```python
import functools

import jax
import jax.numpy as jnp
from jax import lax
from jax.experimental import pallas as pl
from jax.experimental.pallas import tpu as pltpu
from jax.sharding import PartitionSpec as P

BF16 = jnp.bfloat16
F32 = jnp.float32
STEP = 32
TILE = 16
GROUP = 8
CHUNKS = 2
PARAMS = pltpu.CompilerParams(vmem_limit_bytes=56 * 1024 * 1024)


def cost(flops, *arrays):
    return pl.CostEstimate(
        flops=flops,
        bytes_accessed=sum(a.size * a.dtype.itemsize for a in arrays),
        transcendentals=0,
    )


def chunk_spans(width, parts, chunk):
    part = width // parts
    piece = part // CHUNKS
    return [
        slice(s * part + chunk * piece, s * part + (chunk + 1) * piece)
        for s in range(parts)
    ]


def store_lines(block, out, parts, chunk, finish):
    levels, width = block.shape[1:]

    @pl.loop(0, block.shape[0] // TILE)
    def _(tile):
        at = pl.ds(tile * TILE, TILE)
        for s, span in enumerate(chunk_spans(width, parts, chunk)):
            turned = jnp.swapaxes(finish(at, span), 0, 1)
            for l in range(levels):
                out[l * parts + s, at] = turned[l].astype(BF16)


def lines_body(parts, chunk, block, out):
    store_lines(
        block, out, parts, chunk, lambda at, span: block[at, :, span].astype(F32)
    )


def as_lines(block, parts, chunk):
    rows, levels, width = block.shape
    shape = (levels * parts, rows, width // parts // CHUNKS)
    return pl.pallas_call(
        functools.partial(lines_body, parts, chunk),
        grid=(rows // STEP,),
        in_specs=[pl.BlockSpec((STEP, levels, width), lambda i: (i, 0, 0))],
        out_specs=pl.BlockSpec((shape[0], STEP, shape[2]), lambda i: (0, i, 0)),
        out_shape=jax.ShapeDtypeStruct(shape, BF16),
        compiler_params=PARAMS,
        cost_estimate=cost(0, block, block),
        name="as_lines",
    )(block)


def gradient_body(parts, lines, control, *rest):
    out = rest[-1]
    levels, width = control.shape[1:]
    part = width // parts

    @pl.loop(0, STEP // TILE)
    def _(tile):
        at = pl.ds(tile * TILE, TILE)
        for s in range(parts):
            span = slice(s * part, (s + 1) * part)
            got = [lines[l * parts + s, at].astype(F32) for l in range(levels)]
            got = jnp.swapaxes(jnp.stack(got), 0, 1)
            out[at, :, span] = control[at, :, span].astype(F32) + got


def add_lines(control, lines, parts, first, target):
    rows, levels, width = control.shape
    whole = (STEP, levels, width)
    cut = lines.shape[1]
    offset = first // STEP
    operands = [lines, control] + ([] if target is None else [target])
    return pl.pallas_call(
        functools.partial(gradient_body, parts),
        grid=(cut // STEP,),
        in_specs=[
            pl.BlockSpec((lines.shape[0], STEP, lines.shape[2]), lambda i: (0, i, 0)),
            pl.BlockSpec(whole, lambda i: (i + offset, 0, 0)),
        ]
        + [pl.BlockSpec(memory_space=pl.ANY)] * (len(operands) - 2),
        out_specs=pl.BlockSpec(whole, lambda i: (i + offset, 0, 0)),
        out_shape=jax.ShapeDtypeStruct(control.shape, F32),
        input_output_aliases={} if target is None else {2: 0},
        compiler_params=PARAMS,
        cost_estimate=cost(control.size // 2, control, control),
        name="add_lines",
    )(*operands)


def forward_body(*refs):
    starts = refs[:CHUNKS]
    rows_in, sides, innovation, weight, wind_x, wind_y = refs[CHUNKS : CHUNKS + 6]
    end, flat, row_flux, side_flux, state, carry = refs[CHUNKS + 6 :]
    step = pl.program_id(0)
    rows, levels, width = flat.shape
    cut = rows // CHUNKS

    @pl.when(step == 0)
    def _():
        state[pl.ds(0, 1)] = rows_in[pl.ds(0, 1)]
        state[pl.ds(rows + 1, 1)] = rows_in[pl.ds(1, 1)]
        for h in range(CHUNKS):
            state[pl.ds(1 + h * cut, cut)] = starts[h][...].astype(F32)
        carry[...] = jnp.zeros(carry.shape, F32)

    first = step * STEP
    place = lax.broadcasted_iota(jnp.int32, (GROUP, levels, width), 2)
    left_edge, right_edge = place == 0, place == width - 1
    @pl.loop(0, STEP // GROUP)
    def _(group):
        j = group * GROUP
        rows_j, at = pl.ds(j, GROUP), first + j
        here = state[pl.ds(at + 1, GROUP)]
        cx, cy = wind_x[rows_j], wind_y[rows_j]
        left = jnp.where(left_edge, sides[rows_j, :, 0:1], pltpu.roll(here, 1, 2))
        right = jnp.where(
            right_edge, sides[rows_j, :, 1:2], pltpu.roll(here, width - 1, 2)
        )
        dx = state[pl.ds(at + 2, GROUP)] - state[pl.ds(at, GROUP)]
        after = here - cx * dx * 0.5 - cy * (right - left) * 0.5
        end[rows_j] = after
        misfit = weight[rows_j] * (after - innovation[rows_j])
        p, q = cy * misfit, cx * misfit
        side_flux[rows_j, :, 0:1] = p[:, :, 0:1]
        side_flux[rows_j, :, 1:2] = p[:, :, width - 1 : width]
        left = jnp.where(left_edge, 0.0, pltpu.roll(p, 1, 2))
        right = jnp.where(right_edge, 0.0, pltpu.roll(p, width - 1, 2))
        flat_j = misfit + 0.5 * (right - left)
        flat[jnp.maximum(at - 1, 0)] = carry[2] + 0.5 * (q[0] - carry[0])
        flat[at] = flat_j[0] + 0.5 * (q[1] - carry[1])
        flat[pl.ds(at + 1, GROUP - 2)] = flat_j[1:-1] + 0.5 * (q[2:] - q[:-2])

        @pl.when(at == 0)
        def _():
            row_flux[0] = q[0]

        carry[0], carry[1], carry[2] = q[GROUP - 2], q[GROUP - 1], flat_j[GROUP - 1]

    @pl.when(step == rows // STEP - 1)
    def _():
        flat[rows - 1] = carry[2] - 0.5 * carry[0]
        row_flux[1] = carry[1]


def forward(starts, rows_in, sides, innovation, weight, wind_x, wind_y):
    rows, levels, width = innovation.shape
    blocked = pl.BlockSpec((STEP, levels, width), lambda i: (i, 0, 0))
    side = pl.BlockSpec((STEP, levels, 2), lambda i: (i, 0, 0))
    pair = pl.BlockSpec((2, levels, width), lambda i: (0, 0, 0))
    start = pl.BlockSpec(starts[0].shape, lambda i: (0, 0, 0))
    whole = pl.BlockSpec((rows, levels, width), lambda i: (0, 0, 0))
    return pl.pallas_call(
        forward_body,
        grid=(rows // STEP,),
        in_specs=[start] * CHUNKS + [pair, side, blocked, blocked, blocked, blocked],
        out_specs=[blocked, whole, pair, side],
        out_shape=[
            jax.ShapeDtypeStruct((rows, levels, width), F32),
            jax.ShapeDtypeStruct((rows, levels, width), F32),
            jax.ShapeDtypeStruct((2, levels, width), F32),
            jax.ShapeDtypeStruct((rows, levels, 2), F32),
        ],
        scratch_shapes=[
            pltpu.VMEM((rows + 2, levels, width), F32),
            pltpu.VMEM((3, levels, width), F32),
        ],
        compiler_params=PARAMS,
        cost_estimate=cost(30 * innovation.size, *[innovation] * 7),
        name="forward",
    )(*starts, rows_in, sides, innovation, weight, wind_x, wind_y)


def rim_body(parts, chunk, rows, flat, rows_in, sides, out):
    step = pl.program_id(0)
    width = flat.shape[2]

    def finish(at, span):
        value = flat[at, :, span]
        row = step * STEP + at.start + lax.broadcasted_iota(jnp.int32, value.shape, 0)
        value = value - jnp.where(row == 0, 0.5 * rows_in[0:1, :, span], 0.0)
        value = value + jnp.where(row == rows - 1, 0.5 * rows_in[1:2, :, span], 0.0)
        place = lax.broadcasted_iota(jnp.int32, value.shape, 2)
        if span.start == 0:
            value = value - jnp.where(place == 0, 0.5 * sides[at, :, 0:1], 0.0)
        if span.stop == width:
            edge = place == span.stop - span.start - 1
            value = value + jnp.where(edge, 0.5 * sides[at, :, 1:2], 0.0)
        return value

    store_lines(flat, out, parts, chunk, finish)


def rim_lines(flat, rows_in, sides, parts, chunk):
    rows, levels, width = flat.shape
    shape = (levels * parts, rows, width // parts // CHUNKS)
    return pl.pallas_call(
        functools.partial(rim_body, parts, chunk, rows),
        grid=(rows // STEP,),
        in_specs=[
            pl.BlockSpec((STEP, levels, width), lambda i: (i, 0, 0)),
            pl.BlockSpec((2, levels, width), lambda i: (0, 0, 0)),
            pl.BlockSpec((STEP, levels, 2), lambda i: (i, 0, 0)),
        ],
        out_specs=pl.BlockSpec((shape[0], STEP, shape[2]), lambda i: (0, i, 0)),
        out_shape=jax.ShapeDtypeStruct(shape, BF16),
        compiler_params=PARAMS,
        cost_estimate=cost(4 * flat.size, flat, flat),
        name="rim_lines",
    )(flat, rows_in, sides)


def swap_all(lines):
    return lax.all_to_all(lines, "gx", 0, 0, tiled=True)


def plane_pieces(lines, parts, after=None, near_first=False):
    n_x, n_y = lax.axis_size("gx"), lax.axis_size("gy")
    groups = [list(range(i, i + parts)) for i in range(0, n_x, parts)]
    if n_y == 2 and parts == 2:
        pairs = [(a, b) for g in groups for a, b in (g, g[::-1])]
        sent = lines if after is None else lax.optimization_barrier((lines, after))[0]
        far = lax.ppermute(sent, "gy", [(0, 1), (1, 0)])
        near = lax.ppermute(lines, "gx", pairs)
        if near_first:
            far, near = lax.optimization_barrier((far, near))
        cross = lax.ppermute(far, "gx", pairs)
        return [lines, near, far, cross]
    plane = lax.all_gather(lines, "gy", axis=0, tiled=False)
    plane = lax.all_gather(plane, "gx", axis=0, tiled=False, axis_index_groups=groups)
    return [plane[s, g] for s in range(parts) for g in range(n_y)]


def piece_order(parts):
    n_y = lax.axis_size("gy")
    sub, me = lax.rem(lax.axis_index("gx"), parts), lax.axis_index("gy")
    if n_y == 2 and parts == 2:
        return [(sub, me), (1 - sub, me), (sub, 1 - me), (1 - sub, 1 - me)]
    return [(s, g) for s in range(parts) for g in range(n_y)]


def filter_rows(filter_y, parts):
    width = filter_y.shape[0]
    part = width // parts
    sub = lax.rem(lax.axis_index("gx"), parts)
    return [
        lax.dynamic_slice(filter_y, (sub * part, g * width + s * part), (part, part))
        for s, g in piece_order(parts)
    ]


def send_columns(filter_y, parts):
    width, n_y = filter_y.shape[0], lax.axis_size("gy")
    part = width // parts
    sub, me = lax.rem(lax.axis_index("gx"), parts), lax.axis_index("gy")
    if n_y == 2 and parts == 2:
        sent = lax.dynamic_slice(
            filter_y, (0, (1 - me) * width + sub * part), (width, part)
        )
        return lax.ppermute(sent, "gy", [(0, 1), (1, 0)])
    split = filter_y.reshape(width, n_y, parts, part)
    split = lax.dynamic_index_in_dim(split, sub, axis=2, keepdims=False)
    return lax.all_to_all(split, "gy", 1, 0, tiled=True)


def filter_columns(filter_y, got, parts):
    width, n_y = filter_y.shape[0], lax.axis_size("gy")
    part = width // parts
    sub, me = lax.rem(lax.axis_index("gx"), parts), lax.axis_index("gy")
    order = piece_order(parts)
    if n_y == 2 and parts == 2:
        mine = lax.dynamic_slice(filter_y, (0, me * width + sub * part), (width, part))
        return [
            lax.dynamic_slice_in_dim(source, s * part, part, axis=0)
            for source, (s, _) in zip((mine, mine, got, got), order)
        ]
    split = got.reshape(n_y, parts, part, part)
    return [split[g, s] for s, g in order]


def row_halo(first, last):
    n_x = lax.axis_size("gx")
    up = [(i, i + 1) for i in range(n_x - 1)]
    down = [(i + 1, i) for i in range(n_x - 1)]
    return jnp.stack([lax.ppermute(last, "gx", up), lax.ppermute(first, "gx", down)])


def side_halo(first, last):
    n_y, me = lax.axis_size("gy"), lax.axis_index("gy")
    if n_y == 2:
        got = lax.ppermute(jnp.where(me == 0, last, first), "gy", [(0, 1), (1, 0)])
        none = jnp.zeros_like(got)
        return jnp.where(me == 0, none, got), jnp.where(me == 0, got, none)
    up = [(i, i + 1) for i in range(n_y - 1)]
    down = [(i + 1, i) for i in range(n_y - 1)]
    return lax.ppermute(last, "gy", up), lax.ppermute(first, "gy", down)


def per_device(control, innovation, obs_weight, courant_x, courant_y, filter_x, filter_y):
    rows, levels, width = control.shape
    n_x = lax.axis_size("gx")
    parts = n_x // levels
    part = width // parts
    cut, piece = rows // CHUNKS, part // CHUNKS
    spans = [slice(w * piece, (w + 1) * piece) for w in range(CHUNKS)]

    rows_y = filter_rows(filter_y, parts)
    matrix_x = [lax.all_gather(filter_x[:cut], "gx", axis=0, tiled=True)]
    lines = [swap_all(as_lines(control, parts, w)) for w in range(CHUNKS)]
    lines = [l.reshape(n_x * rows, piece) for l in lines]
    lines[-1], filter_x = lax.optimization_barrier((lines[-1], filter_x))
    for h in range(1, CHUNKS):
        share = filter_x[h * cut : (h + 1) * cut]
        matrix_x.append(lax.all_gather(share, "gx", axis=0, tiled=True))
    starts = []
    for h in range(CHUNKS):
        start = 0.0
        for w, span in enumerate(spans):
            smoothed = jnp.dot(matrix_x[h], lines[w], preferred_element_type=F32)
            smoothed = smoothed.astype(BF16).reshape(n_x, cut, piece)
            for plane, matrix in zip(plane_pieces(smoothed, parts), rows_y):
                start = start + jnp.einsum(
                    "brc,kc->brk", plane, matrix[:, span], preferred_element_type=F32
                )
        start = start.astype(BF16)
        if h == CHUNKS - 1:
            start, filter_y = lax.optimization_barrier((start, filter_y))
            columns_y = send_columns(filter_y, parts)
        came = swap_all(start).reshape(levels, parts, cut, part)
        came = came.transpose(2, 0, 1, 3).reshape(cut, levels, width)
        starts.append(came)

    rows_in = row_halo(starts[0][0], starts[-1][-1]).astype(F32)
    before, after = side_halo(
        jnp.concatenate([s[:, :, 0] for s in starts]),
        jnp.concatenate([s[:, :, -1] for s in starts]),
    )
    sides = jnp.stack([before, after], axis=2).astype(F32)
    end_state, flat, row_flux, side_flux = forward(
        starts, rows_in, sides, innovation, obs_weight, courant_x, courant_y
    )
    rows_in = row_halo(row_flux[0], row_flux[1])
    before, after = side_halo(side_flux[:, :, 0], side_flux[:, :, 1])
    sides = jnp.stack([before, after], axis=2)
    flat, columns_y = lax.optimization_barrier((flat, columns_y))
    columns_y = filter_columns(filter_y, columns_y, parts)

    pulled = []
    for w in range(CHUNKS):
        adjoint = swap_all(rim_lines(flat, rows_in, sides, parts, w))
        adjoint = adjoint.reshape(n_x, CHUNKS, cut, piece)
        total = 0.0
        for h in range(CHUNKS):
            total = total + jnp.einsum(
                "ij,ic->jc",
                matrix_x[h],
                adjoint[:, h].reshape(n_x * cut, piece),
                preferred_element_type=F32,
            )
        pulled.append(total.astype(BF16).reshape(n_x, rows, piece))
    gradient = far = None
    for h in range(CHUNKS):
        at, end = h * cut, (h + 1) * cut
        carried = 0.0
        for w, span in enumerate(spans):
            last = w == CHUNKS - 1
            held = far if h > 0 and last else None
            planes = plane_pieces(pulled[w][:, at:end], parts, held, h == 0 and last)
            far = planes[-2] if last else far
            for plane, matrix in zip(planes, columns_y):
                carried = carried + jnp.einsum(
                    "brk,kc->brc", plane, matrix[span], preferred_element_type=F32
                )
        carried = swap_all(carried.astype(BF16))
        gradient = add_lines(control, carried, parts, at, gradient)
    return (end_state, gradient)


def solution(mesh):
    placed = (
        P("gx", None, "gy"),
        P("gx", None, "gy"),
        P("gx", None, "gy"),
        P("gx", None, "gy"),
        P("gx", None, "gy"),
        P("gx", None),
        P("gy", None),
    )
    return jax.shard_map(
        per_device,
        mesh=mesh,
        in_specs=placed,
        out_specs=(P("gx", None, "gy"), P("gx", None, "gy")),
        check_vma=False,
    )
```

```python
import functools

import jax
import jax.numpy as jnp
from jax import lax
from jax.experimental import pallas as pl
from jax.experimental.pallas import tpu as pltpu
from jax.sharding import PartitionSpec as P

BF16 = jnp.bfloat16
F32 = jnp.float32
STEP = 32
TILE = 16
GROUP = 8
CHUNKS = 2
PARAMS = pltpu.CompilerParams(vmem_limit_bytes=56 * 1024 * 1024)


def cost(flops, *arrays):
    return pl.CostEstimate(
        flops=flops,
        bytes_accessed=sum(a.size * a.dtype.itemsize for a in arrays),
        transcendentals=0,
    )


def chunk_spans(width, parts, chunk):
    part = width // parts
    piece = part // CHUNKS
    return [
        slice(s * part + chunk * piece, s * part + (chunk + 1) * piece)
        for s in range(parts)
    ]


def store_lines(block, out, parts, chunk, finish):
    levels, width = block.shape[1:]

    @pl.loop(0, block.shape[0] // TILE)
    def _(tile):
        at = pl.ds(tile * TILE, TILE)
        for s, span in enumerate(chunk_spans(width, parts, chunk)):
            turned = jnp.swapaxes(finish(at, span), 0, 1)
            for l in range(levels):
                out[l * parts + s, at] = turned[l].astype(BF16)


def lines_body(parts, chunk, block, out):
    store_lines(
        block, out, parts, chunk, lambda at, span: block[at, :, span].astype(F32)
    )


def as_lines(block, parts, chunk):
    rows, levels, width = block.shape
    shape = (levels * parts, rows, width // parts // CHUNKS)
    return pl.pallas_call(
        functools.partial(lines_body, parts, chunk),
        grid=(rows // STEP,),
        in_specs=[pl.BlockSpec((STEP, levels, width), lambda i: (i, 0, 0))],
        out_specs=pl.BlockSpec((shape[0], STEP, shape[2]), lambda i: (0, i, 0)),
        out_shape=jax.ShapeDtypeStruct(shape, BF16),
        compiler_params=PARAMS,
        cost_estimate=cost(0, block, block),
        name="as_lines",
    )(block)


def gradient_body(parts, lines, control, *rest):
    out = rest[-1]
    levels, width = control.shape[1:]
    part = width // parts

    @pl.loop(0, STEP // TILE)
    def _(tile):
        at = pl.ds(tile * TILE, TILE)
        for s in range(parts):
            span = slice(s * part, (s + 1) * part)
            got = [lines[l * parts + s, at].astype(F32) for l in range(levels)]
            got = jnp.swapaxes(jnp.stack(got), 0, 1)
            out[at, :, span] = control[at, :, span].astype(F32) + got


def add_lines(control, lines, parts, first, target):
    rows, levels, width = control.shape
    whole = (STEP, levels, width)
    cut = lines.shape[1]
    offset = first // STEP
    operands = [lines, control] + ([] if target is None else [target])
    return pl.pallas_call(
        functools.partial(gradient_body, parts),
        grid=(cut // STEP,),
        in_specs=[
            pl.BlockSpec((lines.shape[0], STEP, lines.shape[2]), lambda i: (0, i, 0)),
            pl.BlockSpec(whole, lambda i: (i + offset, 0, 0)),
        ]
        + [pl.BlockSpec(memory_space=pl.ANY)] * (len(operands) - 2),
        out_specs=pl.BlockSpec(whole, lambda i: (i + offset, 0, 0)),
        out_shape=jax.ShapeDtypeStruct(control.shape, F32),
        input_output_aliases={} if target is None else {2: 0},
        compiler_params=PARAMS,
        cost_estimate=cost(control.size // 2, control, control),
        name="add_lines",
    )(*operands)


def forward_body(*refs):
    starts = refs[:CHUNKS]
    rows_in, sides, innovation, weight, wind_x, wind_y = refs[CHUNKS : CHUNKS + 6]
    end, flat, row_flux, side_flux, state, carry = refs[CHUNKS + 6 :]
    step = pl.program_id(0)
    rows, levels, width = flat.shape
    cut = rows // CHUNKS

    @pl.when(step == 0)
    def _():
        state[pl.ds(0, 1)] = rows_in[pl.ds(0, 1)]
        state[pl.ds(rows + 1, 1)] = rows_in[pl.ds(1, 1)]
        for h in range(CHUNKS):
            state[pl.ds(1 + h * cut, cut)] = starts[h][...].astype(F32)
        carry[...] = jnp.zeros(carry.shape, F32)

    first = step * STEP
    place = lax.broadcasted_iota(jnp.int32, (GROUP, levels, width), 2)
    left_edge, right_edge = place == 0, place == width - 1
    @pl.loop(0, STEP // GROUP)
    def _(group):
        j = group * GROUP
        rows_j, at = pl.ds(j, GROUP), first + j
        here = state[pl.ds(at + 1, GROUP)]
        cx, cy = wind_x[rows_j], wind_y[rows_j]
        left = jnp.where(left_edge, sides[rows_j, :, 0:1], pltpu.roll(here, 1, 2))
        right = jnp.where(
            right_edge, sides[rows_j, :, 1:2], pltpu.roll(here, width - 1, 2)
        )
        dx = state[pl.ds(at + 2, GROUP)] - state[pl.ds(at, GROUP)]
        after = here - cx * dx * 0.5 - cy * (right - left) * 0.5
        end[rows_j] = after
        misfit = weight[rows_j] * (after - innovation[rows_j])
        p, q = cy * misfit, cx * misfit
        side_flux[rows_j, :, 0:1] = p[:, :, 0:1]
        side_flux[rows_j, :, 1:2] = p[:, :, width - 1 : width]
        left = jnp.where(left_edge, 0.0, pltpu.roll(p, 1, 2))
        right = jnp.where(right_edge, 0.0, pltpu.roll(p, width - 1, 2))
        flat_j = misfit + 0.5 * (right - left)
        flat[jnp.maximum(at - 1, 0)] = carry[2] + 0.5 * (q[0] - carry[0])
        flat[at] = flat_j[0] + 0.5 * (q[1] - carry[1])
        flat[pl.ds(at + 1, GROUP - 2)] = flat_j[1:-1] + 0.5 * (q[2:] - q[:-2])

        @pl.when(at == 0)
        def _():
            row_flux[0] = q[0]

        carry[0], carry[1], carry[2] = q[GROUP - 2], q[GROUP - 1], flat_j[GROUP - 1]

    @pl.when(step == rows // STEP - 1)
    def _():
        flat[rows - 1] = carry[2] - 0.5 * carry[0]
        row_flux[1] = carry[1]


def forward(starts, rows_in, sides, innovation, weight, wind_x, wind_y):
    rows, levels, width = innovation.shape
    blocked = pl.BlockSpec((STEP, levels, width), lambda i: (i, 0, 0))
    side = pl.BlockSpec((STEP, levels, 2), lambda i: (i, 0, 0))
    pair = pl.BlockSpec((2, levels, width), lambda i: (0, 0, 0))
    start = pl.BlockSpec(starts[0].shape, lambda i: (0, 0, 0))
    whole = pl.BlockSpec((rows, levels, width), lambda i: (0, 0, 0))
    return pl.pallas_call(
        forward_body,
        grid=(rows // STEP,),
        in_specs=[start] * CHUNKS + [pair, side, blocked, blocked, blocked, blocked],
        out_specs=[blocked, whole, pair, side],
        out_shape=[
            jax.ShapeDtypeStruct((rows, levels, width), F32),
            jax.ShapeDtypeStruct((rows, levels, width), F32),
            jax.ShapeDtypeStruct((2, levels, width), F32),
            jax.ShapeDtypeStruct((rows, levels, 2), F32),
        ],
        scratch_shapes=[
            pltpu.VMEM((rows + 2, levels, width), F32),
            pltpu.VMEM((3, levels, width), F32),
        ],
        compiler_params=PARAMS,
        cost_estimate=cost(30 * innovation.size, *[innovation] * 7),
        name="forward",
    )(*starts, rows_in, sides, innovation, weight, wind_x, wind_y)


def rim_body(parts, chunk, rows, flat, rows_in, sides, out):
    step = pl.program_id(0)
    width = flat.shape[2]

    def finish(at, span):
        value = flat[at, :, span]
        row = step * STEP + at.start + lax.broadcasted_iota(jnp.int32, value.shape, 0)
        value = value - jnp.where(row == 0, 0.5 * rows_in[0:1, :, span], 0.0)
        value = value + jnp.where(row == rows - 1, 0.5 * rows_in[1:2, :, span], 0.0)
        place = lax.broadcasted_iota(jnp.int32, value.shape, 2)
        if span.start == 0:
            value = value - jnp.where(place == 0, 0.5 * sides[at, :, 0:1], 0.0)
        if span.stop == width:
            edge = place == span.stop - span.start - 1
            value = value + jnp.where(edge, 0.5 * sides[at, :, 1:2], 0.0)
        return value

    store_lines(flat, out, parts, chunk, finish)


def rim_lines(flat, rows_in, sides, parts, chunk):
    rows, levels, width = flat.shape
    shape = (levels * parts, rows, width // parts // CHUNKS)
    return pl.pallas_call(
        functools.partial(rim_body, parts, chunk, rows),
        grid=(rows // STEP,),
        in_specs=[
            pl.BlockSpec((STEP, levels, width), lambda i: (i, 0, 0)),
            pl.BlockSpec((2, levels, width), lambda i: (0, 0, 0)),
            pl.BlockSpec((STEP, levels, 2), lambda i: (i, 0, 0)),
        ],
        out_specs=pl.BlockSpec((shape[0], STEP, shape[2]), lambda i: (0, i, 0)),
        out_shape=jax.ShapeDtypeStruct(shape, BF16),
        compiler_params=PARAMS,
        cost_estimate=cost(4 * flat.size, flat, flat),
        name="rim_lines",
    )(flat, rows_in, sides)


def swap_all(lines):
    return lax.all_to_all(lines, "gx", 0, 0, tiled=True)


def plane_pieces(lines, parts, after=None, near_first=False):
    n_x, n_y = lax.axis_size("gx"), lax.axis_size("gy")
    groups = [list(range(i, i + parts)) for i in range(0, n_x, parts)]
    if n_y == 2 and parts == 2:
        pairs = [(a, b) for g in groups for a, b in (g, g[::-1])]
        sent = lines if after is None else lax.optimization_barrier((lines, after))[0]
        far = lax.ppermute(sent, "gy", [(0, 1), (1, 0)])
        near = lax.ppermute(lines, "gx", pairs)
        if near_first:
            far, near = lax.optimization_barrier((far, near))
        cross = lax.ppermute(far, "gx", pairs)
        return [lines, near, far, cross]
    plane = lax.all_gather(lines, "gy", axis=0, tiled=False)
    plane = lax.all_gather(plane, "gx", axis=0, tiled=False, axis_index_groups=groups)
    return [plane[s, g] for s in range(parts) for g in range(n_y)]


def piece_order(parts):
    n_y = lax.axis_size("gy")
    sub, me = lax.rem(lax.axis_index("gx"), parts), lax.axis_index("gy")
    if n_y == 2 and parts == 2:
        return [(sub, me), (1 - sub, me), (sub, 1 - me), (1 - sub, 1 - me)]
    return [(s, g) for s in range(parts) for g in range(n_y)]


def filter_rows(filter_y, parts):
    width = filter_y.shape[0]
    part = width // parts
    sub = lax.rem(lax.axis_index("gx"), parts)
    return [
        lax.dynamic_slice(filter_y, (sub * part, g * width + s * part), (part, part))
        for s, g in piece_order(parts)
    ]


def send_columns(filter_y, parts):
    width, n_y = filter_y.shape[0], lax.axis_size("gy")
    part = width // parts
    sub, me = lax.rem(lax.axis_index("gx"), parts), lax.axis_index("gy")
    if n_y == 2 and parts == 2:
        sent = lax.dynamic_slice(
            filter_y, (0, (1 - me) * width + sub * part), (width, part)
        )
        return lax.ppermute(sent, "gy", [(0, 1), (1, 0)])
    split = filter_y.reshape(width, n_y, parts, part)
    split = lax.dynamic_index_in_dim(split, sub, axis=2, keepdims=False)
    return lax.all_to_all(split, "gy", 1, 0, tiled=True)


def filter_columns(filter_y, got, parts):
    width, n_y = filter_y.shape[0], lax.axis_size("gy")
    part = width // parts
    sub, me = lax.rem(lax.axis_index("gx"), parts), lax.axis_index("gy")
    order = piece_order(parts)
    if n_y == 2 and parts == 2:
        mine = lax.dynamic_slice(filter_y, (0, me * width + sub * part), (width, part))
        return [
            lax.dynamic_slice_in_dim(source, s * part, part, axis=0)
            for source, (s, _) in zip((mine, mine, got, got), order)
        ]
    split = got.reshape(n_y, parts, part, part)
    return [split[g, s] for s, g in order]


def row_halo(first, last):
    n_x = lax.axis_size("gx")
    up = [(i, i + 1) for i in range(n_x - 1)]
    down = [(i + 1, i) for i in range(n_x - 1)]
    return jnp.stack([lax.ppermute(last, "gx", up), lax.ppermute(first, "gx", down)])


def side_halo(first, last):
    n_y, me = lax.axis_size("gy"), lax.axis_index("gy")
    if n_y == 2:
        got = lax.ppermute(jnp.where(me == 0, last, first), "gy", [(0, 1), (1, 0)])
        none = jnp.zeros_like(got)
        return jnp.where(me == 0, none, got), jnp.where(me == 0, got, none)
    up = [(i, i + 1) for i in range(n_y - 1)]
    down = [(i + 1, i) for i in range(n_y - 1)]
    return lax.ppermute(last, "gy", up), lax.ppermute(first, "gy", down)


def per_device(control, innovation, obs_weight, courant_x, courant_y, filter_x, filter_y):
    rows, levels, width = control.shape
    n_x = lax.axis_size("gx")
    parts = n_x // levels
    part = width // parts
    cut, piece = rows // CHUNKS, part // CHUNKS
    spans = [slice(w * piece, (w + 1) * piece) for w in range(CHUNKS)]

    rows_y = filter_rows(filter_y, parts)
    matrix_x = [lax.all_gather(filter_x[:cut], "gx", axis=0, tiled=True)]
    lines = [swap_all(as_lines(control, parts, w)) for w in range(CHUNKS)]
    lines = [l.reshape(n_x * rows, piece) for l in lines]
    lines[-1], filter_x = lax.optimization_barrier((lines[-1], filter_x))
    for h in range(1, CHUNKS):
        share = filter_x[h * cut : (h + 1) * cut]
        matrix_x.append(lax.all_gather(share, "gx", axis=0, tiled=True))
    starts = []
    for h in range(CHUNKS):
        start = 0.0
        for w, span in enumerate(spans):
            smoothed = jnp.dot(matrix_x[h], lines[w], preferred_element_type=F32)
            smoothed = smoothed.astype(BF16).reshape(n_x, cut, piece)
            for plane, matrix in zip(plane_pieces(smoothed, parts), rows_y):
                start = start + jnp.einsum(
                    "brc,kc->brk", plane, matrix[:, span], preferred_element_type=F32
                )
        start = start.astype(BF16)
        if h == CHUNKS - 1:
            start, filter_y = lax.optimization_barrier((start, filter_y))
            columns_y = send_columns(filter_y, parts)
        came = swap_all(start).reshape(levels, parts, cut, part)
        came = came.transpose(2, 0, 1, 3).reshape(cut, levels, width)
        starts.append(came)

    rows_in = row_halo(starts[0][0], starts[-1][-1]).astype(F32)
    before, after = side_halo(
        jnp.concatenate([s[:, :, 0] for s in starts]),
        jnp.concatenate([s[:, :, -1] for s in starts]),
    )
    sides = jnp.stack([before, after], axis=2).astype(F32)
    end_state, flat, row_flux, side_flux = forward(
        starts, rows_in, sides, innovation, obs_weight, courant_x, courant_y
    )
    rows_in = row_halo(row_flux[0], row_flux[1])
    before, after = side_halo(side_flux[:, :, 0], side_flux[:, :, 1])
    sides = jnp.stack([before, after], axis=2)
    flat, columns_y = lax.optimization_barrier((flat, columns_y))
    columns_y = filter_columns(filter_y, columns_y, parts)

    pulled = []
    for w in range(CHUNKS):
        adjoint = swap_all(rim_lines(flat, rows_in, sides, parts, w))
        adjoint = adjoint.reshape(n_x, CHUNKS, cut, piece)
        total = 0.0
        for h in range(CHUNKS):
            total = total + jnp.einsum(
                "ij,ic->jc",
                matrix_x[h],
                adjoint[:, h].reshape(n_x * cut, piece),
                preferred_element_type=F32,
            )
        pulled.append(total.astype(BF16).reshape(n_x, rows, piece))
    gradient = cross = None
    for h in range(CHUNKS):
        at, end = h * cut, (h + 1) * cut
        carried = 0.0
        for w, span in enumerate(spans):
            last = w == CHUNKS - 1
            held = cross if h > 0 and last else None
            planes = plane_pieces(pulled[w][:, at:end], parts, held, h == 0 and last)
            cross = planes[-1] if last else cross
            for plane, matrix in zip(planes, columns_y):
                carried = carried + jnp.einsum(
                    "brk,kc->brc", plane, matrix[span], preferred_element_type=F32
                )
        carried = swap_all(carried.astype(BF16))
        gradient = add_lines(control, carried, parts, at, gradient)
    return (end_state, gradient)


def solution(mesh):
    placed = (
        P("gx", None, "gy"),
        P("gx", None, "gy"),
        P("gx", None, "gy"),
        P("gx", None, "gy"),
        P("gx", None, "gy"),
        P("gx", None),
        P("gy", None),
    )
    return jax.shard_map(
        per_device,
        mesh=mesh,
        in_specs=placed,
        out_specs=(P("gx", None, "gy"), P("gx", None, "gy")),
        check_vma=False,
    )
```

```python
import functools

import jax
import jax.numpy as jnp
from jax import lax
from jax.experimental import pallas as pl
from jax.experimental.pallas import tpu as pltpu
from jax.sharding import PartitionSpec as P

BF16 = jnp.bfloat16
F32 = jnp.float32
STEP = 32
TILE = 16
GROUP = 8
CHUNKS = 2
PARAMS = pltpu.CompilerParams(vmem_limit_bytes=56 * 1024 * 1024)


def cost(flops, *arrays):
    return pl.CostEstimate(
        flops=flops,
        bytes_accessed=sum(a.size * a.dtype.itemsize for a in arrays),
        transcendentals=0,
    )


def chunk_spans(width, parts, chunk):
    part = width // parts
    piece = part // CHUNKS
    return [
        slice(s * part + chunk * piece, s * part + (chunk + 1) * piece)
        for s in range(parts)
    ]


def store_lines(block, out, parts, chunk, finish):
    levels, width = block.shape[1:]

    @pl.loop(0, block.shape[0] // TILE)
    def _(tile):
        at = pl.ds(tile * TILE, TILE)
        for s, span in enumerate(chunk_spans(width, parts, chunk)):
            turned = jnp.swapaxes(finish(at, span), 0, 1)
            for l in range(levels):
                out[l * parts + s, at] = turned[l].astype(BF16)


def lines_body(parts, chunk, block, out):
    store_lines(
        block, out, parts, chunk, lambda at, span: block[at, :, span].astype(F32)
    )


def as_lines(block, parts, chunk):
    rows, levels, width = block.shape
    shape = (levels * parts, rows, width // parts // CHUNKS)
    return pl.pallas_call(
        functools.partial(lines_body, parts, chunk),
        grid=(rows // STEP,),
        in_specs=[pl.BlockSpec((STEP, levels, width), lambda i: (i, 0, 0))],
        out_specs=pl.BlockSpec((shape[0], STEP, shape[2]), lambda i: (0, i, 0)),
        out_shape=jax.ShapeDtypeStruct(shape, BF16),
        compiler_params=PARAMS,
        cost_estimate=cost(0, block, block),
        name="as_lines",
    )(block)


def gradient_body(parts, lines, control, *rest):
    out = rest[-1]
    levels, width = control.shape[1:]
    part = width // parts

    @pl.loop(0, STEP // TILE)
    def _(tile):
        at = pl.ds(tile * TILE, TILE)
        for s in range(parts):
            span = slice(s * part, (s + 1) * part)
            got = [lines[l * parts + s, at].astype(F32) for l in range(levels)]
            got = jnp.swapaxes(jnp.stack(got), 0, 1)
            out[at, :, span] = control[at, :, span].astype(F32) + got


def add_lines(control, lines, parts, first, target):
    rows, levels, width = control.shape
    whole = (STEP, levels, width)
    cut = lines.shape[1]
    offset = first // STEP
    operands = [lines, control] + ([] if target is None else [target])
    return pl.pallas_call(
        functools.partial(gradient_body, parts),
        grid=(cut // STEP,),
        in_specs=[
            pl.BlockSpec((lines.shape[0], STEP, lines.shape[2]), lambda i: (0, i, 0)),
            pl.BlockSpec(whole, lambda i: (i + offset, 0, 0)),
        ]
        + [pl.BlockSpec(memory_space=pl.ANY)] * (len(operands) - 2),
        out_specs=pl.BlockSpec(whole, lambda i: (i + offset, 0, 0)),
        out_shape=jax.ShapeDtypeStruct(control.shape, F32),
        input_output_aliases={} if target is None else {2: 0},
        compiler_params=PARAMS,
        cost_estimate=cost(control.size // 2, control, control),
        name="add_lines",
    )(*operands)


def forward_body(*refs):
    starts = refs[:CHUNKS]
    rows_in, sides, innovation, weight, wind_x, wind_y = refs[CHUNKS : CHUNKS + 6]
    end, flat, row_flux, side_flux, state, carry = refs[CHUNKS + 6 :]
    step = pl.program_id(0)
    rows, levels, width = flat.shape
    cut = rows // CHUNKS

    @pl.when(step == 0)
    def _():
        state[pl.ds(0, 1)] = rows_in[pl.ds(0, 1)]
        state[pl.ds(rows + 1, 1)] = rows_in[pl.ds(1, 1)]
        for h in range(CHUNKS):
            state[pl.ds(1 + h * cut, cut)] = starts[h][...].astype(F32)
        carry[...] = jnp.zeros(carry.shape, F32)

    first = step * STEP
    place = lax.broadcasted_iota(jnp.int32, (GROUP, levels, width), 2)
    left_edge, right_edge = place == 0, place == width - 1
    @pl.loop(0, STEP // GROUP)
    def _(group):
        j = group * GROUP
        rows_j, at = pl.ds(j, GROUP), first + j
        here = state[pl.ds(at + 1, GROUP)]
        cx, cy = wind_x[rows_j], wind_y[rows_j]
        left = jnp.where(left_edge, sides[rows_j, :, 0:1], pltpu.roll(here, 1, 2))
        right = jnp.where(
            right_edge, sides[rows_j, :, 1:2], pltpu.roll(here, width - 1, 2)
        )
        dx = state[pl.ds(at + 2, GROUP)] - state[pl.ds(at, GROUP)]
        after = here - cx * dx * 0.5 - cy * (right - left) * 0.5
        end[rows_j] = after
        misfit = weight[rows_j] * (after - innovation[rows_j])
        p, q = cy * misfit, cx * misfit
        side_flux[rows_j, :, 0:1] = p[:, :, 0:1]
        side_flux[rows_j, :, 1:2] = p[:, :, width - 1 : width]
        left = jnp.where(left_edge, 0.0, pltpu.roll(p, 1, 2))
        right = jnp.where(right_edge, 0.0, pltpu.roll(p, width - 1, 2))
        flat_j = misfit + 0.5 * (right - left)
        flat[jnp.maximum(at - 1, 0)] = carry[2] + 0.5 * (q[0] - carry[0])
        flat[at] = flat_j[0] + 0.5 * (q[1] - carry[1])
        flat[pl.ds(at + 1, GROUP - 2)] = flat_j[1:-1] + 0.5 * (q[2:] - q[:-2])

        @pl.when(at == 0)
        def _():
            row_flux[0] = q[0]

        carry[0], carry[1], carry[2] = q[GROUP - 2], q[GROUP - 1], flat_j[GROUP - 1]

    @pl.when(step == rows // STEP - 1)
    def _():
        flat[rows - 1] = carry[2] - 0.5 * carry[0]
        row_flux[1] = carry[1]


def forward(starts, rows_in, sides, innovation, weight, wind_x, wind_y):
    rows, levels, width = innovation.shape
    blocked = pl.BlockSpec((STEP, levels, width), lambda i: (i, 0, 0))
    side = pl.BlockSpec((STEP, levels, 2), lambda i: (i, 0, 0))
    pair = pl.BlockSpec((2, levels, width), lambda i: (0, 0, 0))
    start = pl.BlockSpec(starts[0].shape, lambda i: (0, 0, 0))
    whole = pl.BlockSpec((rows, levels, width), lambda i: (0, 0, 0))
    return pl.pallas_call(
        forward_body,
        grid=(rows // STEP,),
        in_specs=[start] * CHUNKS + [pair, side, blocked, blocked, blocked, blocked],
        out_specs=[blocked, whole, pair, side],
        out_shape=[
            jax.ShapeDtypeStruct((rows, levels, width), F32),
            jax.ShapeDtypeStruct((rows, levels, width), F32),
            jax.ShapeDtypeStruct((2, levels, width), F32),
            jax.ShapeDtypeStruct((rows, levels, 2), F32),
        ],
        scratch_shapes=[
            pltpu.VMEM((rows + 2, levels, width), F32),
            pltpu.VMEM((3, levels, width), F32),
        ],
        compiler_params=PARAMS,
        cost_estimate=cost(30 * innovation.size, *[innovation] * 7),
        name="forward",
    )(*starts, rows_in, sides, innovation, weight, wind_x, wind_y)


def rim_body(parts, chunk, rows, flat, rows_in, sides, out):
    step = pl.program_id(0)
    width = flat.shape[2]

    def finish(at, span):
        value = flat[at, :, span]
        row = step * STEP + at.start + lax.broadcasted_iota(jnp.int32, value.shape, 0)
        value = value - jnp.where(row == 0, 0.5 * rows_in[0:1, :, span], 0.0)
        value = value + jnp.where(row == rows - 1, 0.5 * rows_in[1:2, :, span], 0.0)
        place = lax.broadcasted_iota(jnp.int32, value.shape, 2)
        if span.start == 0:
            value = value - jnp.where(place == 0, 0.5 * sides[at, :, 0:1], 0.0)
        if span.stop == width:
            edge = place == span.stop - span.start - 1
            value = value + jnp.where(edge, 0.5 * sides[at, :, 1:2], 0.0)
        return value

    store_lines(flat, out, parts, chunk, finish)


def rim_lines(flat, rows_in, sides, parts, chunk):
    rows, levels, width = flat.shape
    shape = (levels * parts, rows, width // parts // CHUNKS)
    return pl.pallas_call(
        functools.partial(rim_body, parts, chunk, rows),
        grid=(rows // STEP,),
        in_specs=[
            pl.BlockSpec((STEP, levels, width), lambda i: (i, 0, 0)),
            pl.BlockSpec((2, levels, width), lambda i: (0, 0, 0)),
            pl.BlockSpec((STEP, levels, 2), lambda i: (i, 0, 0)),
        ],
        out_specs=pl.BlockSpec((shape[0], STEP, shape[2]), lambda i: (0, i, 0)),
        out_shape=jax.ShapeDtypeStruct(shape, BF16),
        compiler_params=PARAMS,
        cost_estimate=cost(4 * flat.size, flat, flat),
        name="rim_lines",
    )(flat, rows_in, sides)


def swap_all(lines):
    return lax.all_to_all(lines, "gx", 0, 0, tiled=True)


def plane_pieces(lines, parts, after=None):
    n_x, n_y = lax.axis_size("gx"), lax.axis_size("gy")
    groups = [list(range(i, i + parts)) for i in range(0, n_x, parts)]
    if n_y == 2 and parts == 2:
        pairs = [(a, b) for g in groups for a, b in (g, g[::-1])]
        sent = lines if after is None else lax.optimization_barrier((lines, after))[0]
        far = lax.ppermute(sent, "gy", [(0, 1), (1, 0)])
        near = lax.ppermute(lines, "gx", pairs)
        cross = lax.ppermute(far, "gx", pairs)
        return [lines, near, far, cross]
    plane = lax.all_gather(lines, "gy", axis=0, tiled=False)
    plane = lax.all_gather(plane, "gx", axis=0, tiled=False, axis_index_groups=groups)
    return [plane[s, g] for s in range(parts) for g in range(n_y)]


def piece_order(parts):
    n_y = lax.axis_size("gy")
    sub, me = lax.rem(lax.axis_index("gx"), parts), lax.axis_index("gy")
    if n_y == 2 and parts == 2:
        return [(sub, me), (1 - sub, me), (sub, 1 - me), (1 - sub, 1 - me)]
    return [(s, g) for s in range(parts) for g in range(n_y)]


def filter_rows(filter_y, parts):
    width = filter_y.shape[0]
    part = width // parts
    sub = lax.rem(lax.axis_index("gx"), parts)
    return [
        lax.dynamic_slice(filter_y, (sub * part, g * width + s * part), (part, part))
        for s, g in piece_order(parts)
    ]


def send_columns(filter_y, parts):
    width, n_y = filter_y.shape[0], lax.axis_size("gy")
    part = width // parts
    sub, me = lax.rem(lax.axis_index("gx"), parts), lax.axis_index("gy")
    if n_y == 2 and parts == 2:
        sent = lax.dynamic_slice(
            filter_y, (0, (1 - me) * width + sub * part), (width, part)
        )
        return lax.ppermute(sent, "gy", [(0, 1), (1, 0)])
    split = filter_y.reshape(width, n_y, parts, part)
    split = lax.dynamic_index_in_dim(split, sub, axis=2, keepdims=False)
    return lax.all_to_all(split, "gy", 1, 0, tiled=True)


def filter_columns(filter_y, got, parts):
    width, n_y = filter_y.shape[0], lax.axis_size("gy")
    part = width // parts
    sub, me = lax.rem(lax.axis_index("gx"), parts), lax.axis_index("gy")
    order = piece_order(parts)
    if n_y == 2 and parts == 2:
        mine = lax.dynamic_slice(filter_y, (0, me * width + sub * part), (width, part))
        return [
            lax.dynamic_slice_in_dim(source, s * part, part, axis=0)
            for source, (s, _) in zip((mine, mine, got, got), order)
        ]
    split = got.reshape(n_y, parts, part, part)
    return [split[g, s] for s, g in order]


def row_halo(first, last):
    n_x = lax.axis_size("gx")
    up = [(i, i + 1) for i in range(n_x - 1)]
    down = [(i + 1, i) for i in range(n_x - 1)]
    return jnp.stack([lax.ppermute(last, "gx", up), lax.ppermute(first, "gx", down)])


def side_halo(first, last):
    n_y, me = lax.axis_size("gy"), lax.axis_index("gy")
    if n_y == 2:
        got = lax.ppermute(jnp.where(me == 0, last, first), "gy", [(0, 1), (1, 0)])
        none = jnp.zeros_like(got)
        return jnp.where(me == 0, none, got), jnp.where(me == 0, got, none)
    up = [(i, i + 1) for i in range(n_y - 1)]
    down = [(i + 1, i) for i in range(n_y - 1)]
    return lax.ppermute(last, "gy", up), lax.ppermute(first, "gy", down)


def per_device(control, innovation, obs_weight, courant_x, courant_y, filter_x, filter_y):
    rows, levels, width = control.shape
    n_x = lax.axis_size("gx")
    parts = n_x // levels
    part = width // parts
    cut, piece = rows // CHUNKS, part // CHUNKS
    spans = [slice(w * piece, (w + 1) * piece) for w in range(CHUNKS)]

    rows_y = filter_rows(filter_y, parts)
    matrix_x = [lax.all_gather(filter_x[:cut], "gx", axis=0, tiled=True)]
    lines = [swap_all(as_lines(control, parts, w)) for w in range(CHUNKS)]
    lines = [l.reshape(n_x * rows, piece) for l in lines]
    lines[-1], filter_x = lax.optimization_barrier((lines[-1], filter_x))
    for h in range(1, CHUNKS):
        share = filter_x[h * cut : (h + 1) * cut]
        matrix_x.append(lax.all_gather(share, "gx", axis=0, tiled=True))
    starts = []
    for h in range(CHUNKS):
        start = 0.0
        for w, span in enumerate(spans):
            smoothed = jnp.dot(matrix_x[h], lines[w], preferred_element_type=F32)
            smoothed = smoothed.astype(BF16).reshape(n_x, cut, piece)
            for plane, matrix in zip(plane_pieces(smoothed, parts), rows_y):
                start = start + jnp.einsum(
                    "brc,kc->brk", plane, matrix[:, span], preferred_element_type=F32
                )
        start = start.astype(BF16)
        if h == CHUNKS - 1:
            start, filter_y = lax.optimization_barrier((start, filter_y))
            columns_y = send_columns(filter_y, parts)
        came = swap_all(start).reshape(levels, parts, cut, part)
        came = came.transpose(2, 0, 1, 3).reshape(cut, levels, width)
        starts.append(came)

    rows_in = row_halo(starts[0][0], starts[-1][-1]).astype(F32)
    before, after = side_halo(
        jnp.concatenate([s[:, :, 0] for s in starts]),
        jnp.concatenate([s[:, :, -1] for s in starts]),
    )
    sides = jnp.stack([before, after], axis=2).astype(F32)
    end_state, flat, row_flux, side_flux = forward(
        starts, rows_in, sides, innovation, obs_weight, courant_x, courant_y
    )
    rows_in = row_halo(row_flux[0], row_flux[1])
    before, after = side_halo(side_flux[:, :, 0], side_flux[:, :, 1])
    sides = jnp.stack([before, after], axis=2)
    flat, columns_y = lax.optimization_barrier((flat, columns_y))
    columns_y = filter_columns(filter_y, columns_y, parts)

    pulled = []
    for w in range(CHUNKS):
        adjoint = swap_all(rim_lines(flat, rows_in, sides, parts, w))
        adjoint = adjoint.reshape(n_x, CHUNKS, cut, piece)
        total = 0.0
        for h in range(CHUNKS):
            total = total + jnp.einsum(
                "ij,ic->jc",
                matrix_x[h],
                adjoint[:, h].reshape(n_x * cut, piece),
                preferred_element_type=F32,
            )
        pulled.append(total.astype(BF16).reshape(n_x, rows, piece))
    gradient = cross = None
    for h in range(CHUNKS):
        at, end = h * cut, (h + 1) * cut
        planes = [plane_pieces(p[:, at:end], parts) for p in pulled[:-1]]
        planes.append(plane_pieces(pulled[-1][:, at:end], parts, cross))
        cross = planes[-1][-1]
        if h == 0:
            early, near = lax.optimization_barrier((planes[0][-1], planes[-1][1]))
            planes[0][-1], planes[-1][1] = early, near
        carried = 0.0
        for pieces, span in zip(planes, spans):
            for plane, matrix in zip(pieces, columns_y):
                carried = carried + jnp.einsum(
                    "brk,kc->brc", plane, matrix[span], preferred_element_type=F32
                )
        carried = swap_all(carried.astype(BF16))
        gradient = add_lines(control, carried, parts, at, gradient)
    return (end_state, gradient)


def solution(mesh):
    placed = (
        P("gx", None, "gy"),
        P("gx", None, "gy"),
        P("gx", None, "gy"),
        P("gx", None, "gy"),
        P("gx", None, "gy"),
        P("gx", None),
        P("gy", None),
    )
    return jax.shard_map(
        per_device,
        mesh=mesh,
        in_specs=placed,
        out_specs=(P("gx", None, "gy"), P("gx", None, "gy")),
        check_vma=False,
    )
```
